32 devices in a mesh: feat: 16 (over z, x, core), tok: 2 (over y).
Axes of the slice: x: 2, y: 2, z: 4, core: 2. Of those that a mesh axis runs over, the one named last changes fastest.
Arguments:
- features: bfloat16 [256, 131072], P('tok', 'feat'), may hold values from -6 to 6
- signs: int32 [131072], P('feat'), may hold values from -1 to 1, as said below
- columns: int32 [1024], replicated, may hold values from 0 to 131071, as said below
- labels: int32 [256, 1], P('tok'), may hold values from 0 to 31; in each aligned block of 128 rows (0 to 127, 128 to 255, ...) at most 8 rows name the same one
Outputs:
- gram: float32 [32, 1024, 1024], P('tok', 'feat')
The draws below stay inside these ranges and needn't reach their ends.
Inputs may be any that keep to these rules, and one draw needn't show every extreme that they name: `signs`: every entry is -1 or 1. `columns`: the 1024 indices are distinct. `labels`: among the rows of one device no concept appears more than 8 times.
All inputs are finite; a program needn't handle non-finite values.
Results may differ from the reference program's by a relative error of at most 0.004.
Values may be sent and summed in bfloat16 or wider, within the bound.
No kernel may reach another device: no remote copies, remote signals or barrier semaphores. Data moves between devices by JAX's collectives and lax.ppermute only.
A program may use at most 64 MiB of HBM per device.

```python
import math
import jax
import jax.numpy as jnp
import numpy as np
from jax import lax

F = 131072
K = 1024
C = 32
TOK_DEV = 128
TOKENS = 256
MOST = 8


def draw_signs(key, part):
    return (2 * jax.random.randint(key, (F,), 0, 2) - 1).astype(jnp.int32)


def draw_columns(key, part):
    return jax.random.permutation(key, F)[:K].astype(jnp.int32)


def levels(own_key, extent, cuts, smallest, largest):
    def one(axis_at, parts):
        draws = jax.random.uniform(jax.random.fold_in(jax.random.fold_in(own_key, 6), axis_at), (parts,), jnp.float32, smallest / len(cuts), largest / len(cuts))
        return jnp.repeat(jnp.exp(draws), extent[axis_at] // parts).reshape((-1,) + (1,) * (len(extent) - axis_at - 1))

    factor_of = one(*cuts[0])
    for cut in cuts[1:]:
        factor_of = factor_of * one(*cut)
    return factor_of


def assign_block(stream_key, own, number, rows, amount, top, reach, skew):
    sequence = jax.random.permutation(stream_key, amount)
    heavy_load, usual = portions_of(amount, rows * top, reach, skew, True), portions_of(amount, rows * top, reach, skew, False)
    places = jnp.arange(amount)

    def named(sizes, offset_by):
        used = int((sizes > 0).sum())
        fixed = max(1, used // 4)
        shifted = fixed + (places - fixed + offset_by * (used - fixed)) % max(1, amount - fixed)
        return jnp.zeros((amount,), jnp.int32).at[sequence[jnp.where(places < fixed, places, shifted)]].set(jnp.asarray(sizes, jnp.int32))

    sizes = jnp.where(number % 4 == 0, named(heavy_load, number // 4), named(usual, number - number // 4 - 1))
    mixed = jax.random.permutation(jax.random.fold_in(own, 3), amount)
    source_of, sink = mixed[0:amount // 2 * 2:2], mixed[1:amount // 2 * 2:2]
    slack = jnp.minimum(sizes[source_of] - 1, reach - sizes[sink]) // 2
    slack = jnp.where((source_of == sequence[0]) | (sink == sequence[0]) | (sizes[sink] == 0), 0, jnp.maximum(slack, 0))
    shifted = jax.random.randint(jax.random.fold_in(own, 4), (amount // 2,), 0, 1 << 20) % (slack + 1)
    sizes = sizes.at[source_of].add(-shifted).at[sink].add(shifted)
    items = jnp.searchsorted(jnp.cumsum(sizes), jnp.arange(rows * top), side="right").astype(jnp.int32)
    table = items.reshape(top, rows).T
    table = table[jax.random.permutation(jax.random.fold_in(own, 1), rows)]
    offset_by = jax.random.randint(jax.random.fold_in(own, 2), (rows, 1), 0, top)
    return jnp.take_along_axis(table, (jnp.arange(top)[None, :] + offset_by) % top, axis=1)


def portions_of(number_of, total, reach, slope, full):
    portions = [(1 << 20) // math.isqrt(standing ** slope) + 1 for standing in range(1, number_of + 1)]
    largest = reach if full else min(reach, max(-(-total // number_of), total * portions[0] // sum(portions)))
    least = 1 if total - largest >= number_of - 1 else 0
    given, surplus = [largest] + [least] * (number_of - 1), total - largest - least * (number_of - 1)
    while surplus > 0:
        candidates = [i for i in range(1, number_of) if given[i] < largest] or [i for i in range(1, number_of) if given[i] < reach]
        mass, budget = sum([portions[i] for i in candidates]), surplus
        for i in candidates:
            addition = min(reach - given[i], max(1, budget * portions[i] // mass), surplus)
            given[i] = given[i] + addition
            surplus = surplus - addition
    return np.array(given)


def gaussian(rng, shape, spread, most, split=(), held_as=jnp.bfloat16):
    values = jax.random.normal(rng, shape, jnp.float32) * spread
    if len(split) > 0:
        values = levels(rng, shape, split, -0.22, 0.18) * values
    return jnp.clip(values, min=-most, max=most).astype(held_as)


def setup_inputs(seed: int = 0) -> dict:
    arg_keys = jax.random.split(jax.random.key(seed), 5)
    features = gaussian(arg_keys[0], (TOKENS, F), 1.0, 6.0, ((0, 2), (1, 16)))
    signs = draw_signs(jax.random.fold_in(arg_keys[4], 71), 0)
    columns = draw_columns(jax.random.fold_in(arg_keys[4], 71), 0)
    labels_keys = jax.random.split(jax.random.fold_in(arg_keys[3], 1), TOKENS // TOK_DEV)
    labels_turns = jax.random.permutation(jax.random.fold_in(arg_keys[3], 3), TOKENS // TOK_DEV)
    labels = jax.vmap(lambda own, number: assign_block(jax.random.fold_in(arg_keys[3], 2), own, number, TOK_DEV, C, 1, MOST, 0))(labels_keys, labels_turns).reshape((TOKENS, 1))
    return {"features": features, "signs": signs, "columns": columns, "labels": labels}


def bit_parity(number, bit_count):
    total = jnp.zeros_like(number)
    for position in range(bit_count):
        total = total ^ number >> position & 1
    return total

def sylvester(order, dtype):
    index = lax.iota(jnp.int32, order)
    parity = bit_parity(index[:, None] & index[None, :], order.bit_length())
    return (1 - 2 * parity).astype(dtype)

def reference(features, signs, columns, labels):
    total_rows = features.shape[0]
    width = features.shape[1]
    blocks = width // 128
    table = sylvester(128, jnp.bfloat16)
    low_part = columns % 128
    high_part = columns // 128
    outer = lax.iota(jnp.int32, blocks)
    parity = bit_parity(high_part[:, None] & outer[None, :], blocks.bit_length())
    high_sign = (1 - 2 * parity).astype(jnp.float32)
    scale = 1.0 / math.sqrt(width)
    signed = features * signs.astype(jnp.bfloat16)[None, :]
    step_rows = math.gcd(total_rows, 32)
    flat_labels = labels[:, 0]

    def one_block(rows):
        inner = jnp.dot(rows.reshape(step_rows * blocks, 128), table, preferred_element_type=jnp.float32)
        inner = inner.reshape(step_rows, blocks, 128)
        picked = jnp.take(inner, low_part, axis=2)
        mixed = jnp.einsum('bnk,kn->bk', picked, high_sign, precision=lax.Precision.HIGHEST)
        return (mixed * scale).astype(jnp.bfloat16)
    sketch = lax.map(one_block, signed.reshape(total_rows // step_rows, step_rows, width))
    sketch = sketch.reshape(total_rows, columns.shape[0]).astype(jnp.float32)
    factor = C / total_rows

    def one_concept(concept):
        chosen = (flat_labels == concept).astype(jnp.float32)
        return jnp.dot((sketch * chosen[:, None]).T, sketch, precision=lax.Precision.HIGHEST) * factor
    return lax.map(one_concept, lax.iota(jnp.int32, C))
```

```python
import functools
import math

import jax
import jax.numpy as jnp
from jax import lax
from jax.experimental import pallas as pl
from jax.experimental.pallas import tpu as pltpu
from jax.sharding import PartitionSpec as P

C = 32
LOW = 256
LANES = 128
VMEM_LIMIT = 48 * 1024 * 1024


def parity_sign(number, bit_count):
    shift = 1
    while shift < bit_count:
        shift *= 2
    while shift > 1:
        shift //= 2
        number = number ^ (number >> shift)
    return (1 - 2 * (number & 1)).astype(jnp.float32)


def partial_kernel(high_count, total_bits, x_ref, s_ref, col_ref, send_ref, keep_ref, low, high, acc):
    step = pl.program_id(0)
    kept = col_ref.shape[1]
    blocks = x_ref.shape[1] // LOW
    me = lax.axis_index("feat")

    @pl.when(step == 0)
    def _():
        col = col_ref[...]
        low_index = lax.broadcasted_iota(jnp.int32, (LOW, kept), 0)
        low[...] = parity_sign(low_index & col, 8).astype(jnp.bfloat16)
        high_index = lax.broadcasted_iota(jnp.int32, high.shape, 0) + me * high_count
        high[...] = parity_sign(high_index & (col >> 8), total_bits - 8)
        acc[...] = jnp.zeros_like(acc)

    signs = s_ref[...].astype(jnp.bfloat16)
    signed = x_ref[...] * signs
    for part in range(kept // LOW):
        cols = slice(part * LOW, (part + 1) * LOW)
        table = low[:, cols]
        total = acc[:, cols]
        for block in range(blocks):
            inner = jnp.dot(
                signed[:, block * LOW:(block + 1) * LOW], table, preferred_element_type=jnp.float32
            )
            total = total + inner * high[pl.ds(step * blocks + block, 1), cols]
        acc[:, cols] = total

    @pl.when(step == pl.num_programs(0) - 1)
    def _():
        half = keep_ref.shape[0]
        mine = lax.rem(me, 2)
        keep_ref[...] = acc[pl.ds(pl.multiple_of(mine * half, half), half), :]
        send_ref[...] = acc[pl.ds(pl.multiple_of((1 - mine) * half, half), half), :]


def partial_halves(features, signs, columns, feat_count):
    rows, width = features.shape
    kept = columns.shape[0]
    step_width = min(width, 2048)
    high_count = width // LOW
    total_bits = (width * feat_count).bit_length() - 1
    half = jax.ShapeDtypeStruct((rows // 2, kept), jnp.float32)
    return pl.pallas_call(
        functools.partial(partial_kernel, high_count, total_bits),
        grid=(width // step_width,),
        in_specs=[
            pl.BlockSpec((rows, step_width), lambda i: (0, i)),
            pl.BlockSpec((1, step_width), lambda i: (0, i)),
            pl.BlockSpec((1, kept), lambda i: (0, 0)),
        ],
        out_specs=[pl.BlockSpec((rows // 2, kept), lambda i: (0, 0))] * 2,
        out_shape=[half, half],
        scratch_shapes=[
            pltpu.VMEM((LOW, kept), jnp.bfloat16),
            pltpu.VMEM((high_count, kept), jnp.float32),
            pltpu.VMEM((rows, kept), jnp.float32),
        ],
        compiler_params=pltpu.CompilerParams(vmem_limit_bytes=VMEM_LIMIT),
        cost_estimate=pl.CostEstimate(
            flops=2 * rows * width * kept, bytes_accessed=2 * rows * width + 4 * rows * kept, transcendentals=0
        ),
        name="partial_transform",
    )(features, signs.reshape(1, width), columns.reshape(1, kept))


def gram_kernel(shard, group, factor, a_ref, b_ref, out_ref, own):
    step = pl.program_id(0)
    kept = out_ref.shape[1]
    wide = group * shard
    steps = pl.num_programs(0)

    @pl.when(step == 0)
    def _():
        first = lax.axis_index("feat") * shard
        source = lax.broadcasted_iota(jnp.int32, (kept, wide), 0)
        lane = lax.broadcasted_iota(jnp.int32, (kept, wide), 1)
        pick = jnp.where(source == first + (lane & (shard - 1)), 1.0, 0.0).astype(jnp.bfloat16)
        for at, ref in enumerate((a_ref, b_ref)):
            own[at] = jnp.dot(ref[:, :kept], pick, preferred_element_type=jnp.float32).astype(jnp.bfloat16)

    lane = lax.broadcasted_iota(jnp.int32, (a_ref.shape[0], wide), 1)
    concept = (lax.axis_index("tok") * steps + step) * group + lane // shard
    total = None
    for at, ref in enumerate((a_ref, b_ref)):
        label = ref[:, kept:kept + 1].astype(jnp.float32).astype(jnp.int32)
        chosen = jnp.where(label == concept, own[at].astype(jnp.float32), 0.0).astype(jnp.bfloat16)
        gram = lax.dot_general(
            chosen, ref[:, :kept], (((0,), (0,)), ((), ())), preferred_element_type=jnp.float32
        )
        total = gram if total is None else total + gram
    out_ref[...] = total * factor


def gram_blocks(ours, theirs, concepts, shard, kept, factor):
    tokens, lanes = ours.shape
    group = max(1, min(concepts, LOW // shard))
    return pl.pallas_call(
        functools.partial(gram_kernel, shard, group, factor),
        grid=(concepts // group,),
        in_specs=[pl.BlockSpec((tokens, lanes), lambda i: (0, 0))] * 2,
        out_specs=pl.BlockSpec((group * shard, kept), lambda i: (i, 0)),
        out_shape=jax.ShapeDtypeStruct((concepts * shard, kept), jnp.float32),
        scratch_shapes=[pltpu.VMEM((2, tokens, group * shard), jnp.bfloat16)],
        compiler_params=pltpu.CompilerParams(vmem_limit_bytes=VMEM_LIMIT),
        cost_estimate=pl.CostEstimate(
            flops=4 * tokens * concepts * shard * kept, bytes_accessed=4 * concepts * shard * kept, transcendentals=0
        ),
        name="gram",
    )(ours, theirs)


def body(features, signs, columns, labels):
    rows, width = features.shape
    feat_count = lax.axis_size("feat")
    feat_index = lax.axis_index("feat")
    tok_count = lax.axis_size("tok")
    kept = columns.shape[0]
    shard = kept // feat_count
    peers = feat_count // 2
    chunk = rows // feat_count
    core_pairs = [(i, i ^ 1) for i in range(feat_count)]
    feat_groups = [list(range(core, feat_count, 2)) for core in range(2)]
    all_groups = [list(range(core, tok_count * feat_count, 2)) for core in range(2)]

    send, keep = partial_halves(features, signs, columns, feat_count)
    half = keep + lax.ppermute(send, "feat", core_pairs)
    parts = lax.all_to_all(
        half.reshape(peers, chunk, kept), "feat", 0, 0, axis_index_groups=feat_groups, tiled=True
    )
    summed = jnp.sum(parts, axis=0)
    sketch = (summed * (1.0 / math.sqrt(width * feat_count))).astype(jnp.bfloat16)

    first = (feat_index & 1) * (rows // 2) + (feat_index >> 1) * chunk
    own_labels = lax.dynamic_slice_in_dim(labels, first, chunk, 0).astype(jnp.bfloat16)
    row = jnp.concatenate([sketch, jnp.broadcast_to(own_labels, (chunk, LANES))], axis=1)
    spread = jnp.broadcast_to(row[None], (tok_count * peers,) + row.shape)
    ours = lax.all_to_all(
        spread, ("tok", "feat"), 0, 0, axis_index_groups=all_groups, tiled=True
    ).reshape(tok_count * peers * chunk, kept + LANES)
    theirs = lax.ppermute(ours, "feat", core_pairs)
    concepts = C // tok_count
    gram = gram_blocks(ours, theirs, concepts, shard, kept, C / (rows * tok_count))
    return gram.reshape(concepts, shard, kept)


def solution(mesh):
    in_specs = (P("tok", "feat"), P("feat"), P(), P("tok", None))
    out_specs = P("tok", "feat", None)
    return jax.shard_map(body, mesh=mesh, in_specs=in_specs, out_specs=out_specs, check_vma=False)
```

```python
import functools
import math

import jax
import jax.numpy as jnp
from jax import lax
from jax.experimental import pallas as pl
from jax.experimental.pallas import tpu as pltpu
from jax.sharding import PartitionSpec as P

C = 32
LOW = 256
LANES = 128
VMEM_LIMIT = 48 * 1024 * 1024


def parity_sign(number, bit_count):
    shift = 1
    while shift < bit_count:
        shift *= 2
    while shift > 1:
        shift //= 2
        number = number ^ (number >> shift)
    return (1 - 2 * (number & 1)).astype(jnp.float32)


def partial_kernel(high_count, total_bits, parts, x_hbm, s_hbm, col_hbm, send_ref, keep_ref, x_buf, s_buf, col_buf, low, high, acc, sems):
    kept = col_hbm.shape[1]
    wide = x_hbm.shape[1] // parts
    me = lax.axis_index("feat")
    col_copy = pltpu.make_async_copy(col_hbm, col_buf, sems.at[parts])
    sign_copy = pltpu.make_async_copy(s_hbm, s_buf, sems.at[parts + 1])
    col_copy.start()
    sign_copy.start()
    copies = []
    for part in range(parts):
        cols = pl.ds(part * wide, wide)
        copies.append(pltpu.make_async_copy(x_hbm.at[:, cols], x_buf.at[:, cols], sems.at[part]))
        copies[-1].start()
    col_copy.wait()
    col = col_buf[...]
    index = lax.broadcasted_iota(jnp.int32, (16, kept), 0)
    inner = parity_sign(index & col, 4)
    outer = parity_sign(index & (col >> 4), 4)
    for row in range(LOW // 16):
        low[row * 16:(row + 1) * 16] = (inner * outer[row:row + 1]).astype(jnp.bfloat16)
    high_index = lax.broadcasted_iota(jnp.int32, high.shape, 0) + me * high_count
    high[...] = parity_sign(high_index & (col >> 8), total_bits - 8)
    sign_copy.wait()
    blocks = wide // LOW
    rows = x_hbm.shape[0]
    for part in range(parts):
        copies[part].wait()
        stack = []
        for block in range(part * blocks, (part + 1) * blocks):
            cols = slice(block * LOW, (block + 1) * LOW)
            stack.append(x_buf[:, cols] * s_buf[:, cols].astype(jnp.bfloat16))
        stack = jnp.concatenate(stack, axis=0)
        for group in range(kept // LOW):
            cols = slice(group * LOW, (group + 1) * LOW)
            products = jnp.dot(stack, low[:, cols], preferred_element_type=jnp.float32)
            total = None
            for at in range(blocks):
                row = part * blocks + at
                term = products[at * rows:(at + 1) * rows] * high[row:row + 1, cols]
                total = term if total is None else total + term
            if part > 0:
                total = total + acc[:, cols]
            acc[:, cols] = total
    half = keep_ref.shape[0]
    mine = lax.rem(me, 2)
    keep_ref[...] = acc[pl.ds(pl.multiple_of(mine * half, half), half), :]
    send_ref[...] = acc[pl.ds(pl.multiple_of((1 - mine) * half, half), half), :]


def partial_halves(features, signs, columns, feat_count):
    rows, width = features.shape
    kept = columns.shape[0]
    parts = max(1, width // 2048)
    high_count = width // LOW
    total_bits = (width * feat_count).bit_length() - 1
    half = jax.ShapeDtypeStruct((rows // 2, kept), jnp.float32)
    return pl.pallas_call(
        functools.partial(partial_kernel, high_count, total_bits, parts),
        in_specs=[pl.BlockSpec(memory_space=pltpu.HBM)] * 3,
        out_specs=[pl.BlockSpec(memory_space=pltpu.VMEM)] * 2,
        out_shape=[half, half],
        scratch_shapes=[
            pltpu.VMEM((rows, width), jnp.bfloat16),
            pltpu.VMEM((1, width), jnp.int32),
            pltpu.VMEM((1, kept), jnp.int32),
            pltpu.VMEM((LOW, kept), jnp.bfloat16),
            pltpu.VMEM((high_count, kept), jnp.float32),
            pltpu.VMEM((rows, kept), jnp.float32),
            pltpu.SemaphoreType.DMA((parts + 2,)),
        ],
        compiler_params=pltpu.CompilerParams(vmem_limit_bytes=VMEM_LIMIT),
        cost_estimate=pl.CostEstimate(
            flops=2 * rows * width * kept, bytes_accessed=2 * rows * width + 4 * rows * kept, transcendentals=0
        ),
        name="partial_transform",
    )(*(
        pltpu.with_memory_space_constraint(operand, pltpu.HBM)
        for operand in (features, signs.reshape(1, width), columns.reshape(1, kept))
    ))


def gram_kernel(shard, group, factor, a_ref, b_ref, out_ref, rows, own, label):
    step = pl.program_id(0)
    kept = out_ref.shape[1]
    wide = group * shard
    steps = pl.num_programs(0)
    half = a_ref.shape[0]

    @pl.when(step == 0)
    def _():
        first = lax.axis_index("feat") * shard
        source = lax.broadcasted_iota(jnp.int32, (kept, wide), 0)
        lane = lax.broadcasted_iota(jnp.int32, (kept, wide), 1)
        pick = jnp.where(source == first + (lane & (shard - 1)), 1.0, 0.0).astype(jnp.bfloat16)
        lane = lax.broadcasted_iota(jnp.int32, (half, wide), 1)
        for at, ref in enumerate((a_ref, b_ref)):
            span = slice(at * half, (at + 1) * half)
            rows[span] = ref[:, :kept]
            named = ref[:, kept:kept + 1].astype(jnp.float32).astype(jnp.int32)
            label[span] = named - lane // shard
        own[...] = jnp.dot(rows[...], pick, preferred_element_type=jnp.float32)

    first = (lax.axis_index("tok") * steps + step) * group
    chosen = jnp.where(label[...] == first, own[...], 0.0).astype(jnp.bfloat16)
    gram = lax.dot_general(chosen, rows[...], (((0,), (0,)), ((), ())), preferred_element_type=jnp.float32)
    out_ref[...] = gram * factor


def gram_blocks(ours, theirs, concepts, shard, kept, factor):
    tokens, lanes = ours.shape
    group = max(1, min(concepts, LOW // shard))
    return pl.pallas_call(
        functools.partial(gram_kernel, shard, group, factor),
        grid=(concepts // group,),
        in_specs=[pl.BlockSpec((tokens, lanes), lambda i: (0, 0))] * 2,
        out_specs=pl.BlockSpec((group * shard, kept), lambda i: (i, 0)),
        out_shape=jax.ShapeDtypeStruct((concepts * shard, kept), jnp.float32),
        scratch_shapes=[
            pltpu.VMEM((2 * tokens, kept), jnp.bfloat16),
            pltpu.VMEM((2 * tokens, group * shard), jnp.float32),
            pltpu.VMEM((2 * tokens, group * shard), jnp.int32),
        ],
        compiler_params=pltpu.CompilerParams(vmem_limit_bytes=VMEM_LIMIT),
        cost_estimate=pl.CostEstimate(
            flops=4 * tokens * concepts * shard * kept, bytes_accessed=4 * concepts * shard * kept, transcendentals=0
        ),
        name="gram",
    )(ours, theirs)


def swap(array, axis, offset):
    return lax.ppermute(array, axis, [(i, i ^ offset) for i in range(lax.axis_size(axis))])


def radices(count):
    out = [2] if (count.bit_length() - 1) % 2 else []
    return out + [4] * ((count.bit_length() - 1) // 2)


def scatter_sum(array, index, stride, radix):
    digit = index // stride % radix
    size = array.shape[0] // radix

    def piece(at):
        return lax.dynamic_slice_in_dim(array, at * size, size, 0)

    total = piece(digit)
    for other in range(1, radix):
        total = total + swap(piece(digit ^ other), "feat", other * stride)
    return total


def gather_rows(array, axis, stride, radix):
    received = [swap(array, axis, other * stride) for other in range(1, radix)]
    return jnp.concatenate([array] + received, axis=0)


def body(features, signs, columns, labels):
    rows, width = features.shape
    feat_count = lax.axis_size("feat")
    feat_index = lax.axis_index("feat")
    tok_count = lax.axis_size("tok")
    kept = columns.shape[0]
    shard = kept // feat_count
    stages = []
    stride = 2
    for radix in radices(feat_count // 2):
        stages.append((stride, radix))
        stride *= radix

    send, keep = partial_halves(features, signs, columns, feat_count)
    summed = keep + swap(send, "feat", 1)
    first, size = (feat_index & 1) * (rows // 2), rows // 2
    for stride, radix in stages:
        summed = scatter_sum(summed, feat_index, stride, radix)
        size //= radix
        first = first + feat_index // stride % radix * size
    sketch = (summed * (1.0 / math.sqrt(width * feat_count))).astype(jnp.bfloat16)

    own_labels = lax.dynamic_slice_in_dim(labels, first, size, 0).astype(jnp.bfloat16)
    ours = jnp.concatenate([sketch, jnp.broadcast_to(own_labels, (size, LANES))], axis=1)
    for stride, radix in reversed(stages[1:]):
        ours = gather_rows(ours, "feat", stride, radix)
    stride = 1
    for radix in radices(tok_count):
        ours = gather_rows(ours, "tok", stride, radix)
        stride *= radix
    ours = gather_rows(ours, "feat", *stages[0])
    theirs = swap(ours, "feat", 1)
    concepts = C // tok_count
    gram = gram_blocks(ours, theirs, concepts, shard, kept, C / (rows * tok_count))
    return gram.reshape(concepts, shard, kept)


def solution(mesh):
    in_specs = (P("tok", "feat"), P("feat"), P(), P("tok", None))
    out_specs = P("tok", "feat", None)
    return jax.shard_map(body, mesh=mesh, in_specs=in_specs, out_specs=out_specs, check_vma=False)
```

```python
import functools
import math

import jax
import jax.numpy as jnp
from jax import lax
from jax.experimental import pallas as pl
from jax.experimental.pallas import tpu as pltpu
from jax.sharding import PartitionSpec as P

C = 32
LOW = 256
LANES = 128
VMEM_LIMIT = 48 * 1024 * 1024


def parity_sign(number, bit_count):
    shift = 1
    while shift < bit_count:
        shift *= 2
    while shift > 1:
        shift //= 2
        number = number ^ (number >> shift)
    return (1 - 2 * (number & 1)).astype(jnp.float32)


def partial_kernel(high_count, total_bits, parts, x_hbm, s_hbm, col_hbm, send_ref, keep_ref, x_buf, s_buf, col_buf, low, high, acc, sems):
    kept = col_hbm.shape[1]
    wide = x_hbm.shape[1] // parts
    me = lax.axis_index("feat")
    col_copy = pltpu.make_async_copy(col_hbm, col_buf, sems.at[parts])
    sign_copy = pltpu.make_async_copy(s_hbm, s_buf, sems.at[parts + 1])
    col_copy.start()
    sign_copy.start()
    copies = []
    for part in range(parts):
        cols = pl.ds(part * wide, wide)
        copies.append(pltpu.make_async_copy(x_hbm.at[:, cols], x_buf.at[:, cols], sems.at[part]))
        copies[-1].start()
    col_copy.wait()
    col = col_buf[...]
    index = lax.broadcasted_iota(jnp.int32, (16, kept), 0)
    inner = parity_sign(index & col, 4)
    outer = parity_sign(index & (col >> 4), 4)
    for row in range(LOW // 16):
        low[row * 16:(row + 1) * 16] = (inner * outer[row:row + 1]).astype(jnp.bfloat16)
    high_index = lax.broadcasted_iota(jnp.int32, high.shape, 0) + me * high_count
    high[...] = parity_sign(high_index & (col >> 8), total_bits - 8)
    sign_copy.wait()
    blocks = wide // LOW
    rows = x_hbm.shape[0]
    for part in range(parts):
        copies[part].wait()
        stack = []
        for block in range(part * blocks, (part + 1) * blocks):
            cols = slice(block * LOW, (block + 1) * LOW)
            stack.append(x_buf[:, cols] * s_buf[:, cols].astype(jnp.bfloat16))
        stack = jnp.concatenate(stack, axis=0)
        for group in range(kept // LOW):
            cols = slice(group * LOW, (group + 1) * LOW)
            products = jnp.dot(stack, low[:, cols], preferred_element_type=jnp.float32)
            total = None
            for at in range(blocks):
                row = part * blocks + at
                term = products[at * rows:(at + 1) * rows] * high[row:row + 1, cols]
                total = term if total is None else total + term
            if part > 0:
                total = total + acc[:, cols]
            acc[:, cols] = total
    half = keep_ref.shape[0]
    mine = lax.rem(me, 2)
    keep_ref[...] = acc[pl.ds(pl.multiple_of(mine * half, half), half), :]
    send_ref[...] = acc[pl.ds(pl.multiple_of((1 - mine) * half, half), half), :]


def partial_halves(features, signs, columns, feat_count):
    rows, width = features.shape
    kept = columns.shape[0]
    parts = max(1, width // 2048)
    high_count = width // LOW
    total_bits = (width * feat_count).bit_length() - 1
    half = jax.ShapeDtypeStruct((rows // 2, kept), jnp.float32)
    return pl.pallas_call(
        functools.partial(partial_kernel, high_count, total_bits, parts),
        in_specs=[pl.BlockSpec(memory_space=pltpu.HBM)] * 3,
        out_specs=[pl.BlockSpec(memory_space=pltpu.VMEM)] * 2,
        out_shape=[half, half],
        scratch_shapes=[
            pltpu.VMEM((rows, width), jnp.bfloat16),
            pltpu.VMEM((1, width), jnp.int32),
            pltpu.VMEM((1, kept), jnp.int32),
            pltpu.VMEM((LOW, kept), jnp.bfloat16),
            pltpu.VMEM((high_count, kept), jnp.float32),
            pltpu.VMEM((rows, kept), jnp.float32),
            pltpu.SemaphoreType.DMA((parts + 2,)),
        ],
        compiler_params=pltpu.CompilerParams(vmem_limit_bytes=VMEM_LIMIT),
        cost_estimate=pl.CostEstimate(
            flops=2 * rows * width * kept, bytes_accessed=2 * rows * width + 4 * rows * kept, transcendentals=0
        ),
        name="partial_transform",
    )(*(
        pltpu.with_memory_space_constraint(operand, pltpu.HBM)
        for operand in (features, signs.reshape(1, width), columns.reshape(1, kept))
    ))


def gram_kernel(shard, group, factor, a_ref, b_ref, out_ref, rows, own, label):
    step = pl.program_id(0)
    kept = out_ref.shape[1]
    wide = group * shard
    steps = pl.num_programs(0)
    half = a_ref.shape[0]

    @pl.when(step == 0)
    def _():
        first = lax.axis_index("feat") * shard
        source = lax.broadcasted_iota(jnp.int32, (kept, wide), 0)
        lane = lax.broadcasted_iota(jnp.int32, (kept, wide), 1)
        pick = jnp.where(source == first + (lane & (shard - 1)), 1.0, 0.0).astype(jnp.bfloat16)
        lane = lax.broadcasted_iota(jnp.int32, (half, wide), 1)
        for at, ref in enumerate((a_ref, b_ref)):
            span = slice(at * half, (at + 1) * half)
            rows[span] = ref[:, :kept]
            named = ref[:, kept:kept + 1].astype(jnp.float32).astype(jnp.int32)
            label[span] = named - lane // shard
        own[...] = jnp.dot(rows[...], pick, preferred_element_type=jnp.float32)

    first = (lax.axis_index("tok") * steps + step) * group
    chosen = jnp.where(label[...] == first, own[...], 0.0).astype(jnp.bfloat16)
    gram = lax.dot_general(chosen, rows[...], (((0,), (0,)), ((), ())), preferred_element_type=jnp.float32)
    out_ref[...] = gram * factor


def gram_blocks(ours, theirs, concepts, shard, kept, factor):
    tokens, lanes = ours.shape
    group = max(1, min(concepts, LOW // shard))
    return pl.pallas_call(
        functools.partial(gram_kernel, shard, group, factor),
        grid=(concepts // group,),
        in_specs=[pl.BlockSpec((tokens, lanes), lambda i: (0, 0))] * 2,
        out_specs=pl.BlockSpec((group * shard, kept), lambda i: (i, 0)),
        out_shape=jax.ShapeDtypeStruct((concepts * shard, kept), jnp.float32),
        scratch_shapes=[
            pltpu.VMEM((2 * tokens, kept), jnp.bfloat16),
            pltpu.VMEM((2 * tokens, group * shard), jnp.float32),
            pltpu.VMEM((2 * tokens, group * shard), jnp.int32),
        ],
        compiler_params=pltpu.CompilerParams(vmem_limit_bytes=VMEM_LIMIT),
        cost_estimate=pl.CostEstimate(
            flops=4 * tokens * concepts * shard * kept, bytes_accessed=4 * concepts * shard * kept, transcendentals=0
        ),
        name="gram",
    )(ours, theirs)


def encode(values, word_ref):
    kept = values.shape[1]
    half = values.shape[0] // 2
    top = jnp.max(jnp.abs(values), axis=1, keepdims=True)
    power = jnp.ceil(jnp.log2(jnp.maximum(top, 2.0 ** -100)))
    whole = jnp.round(values * jnp.exp2(15.0 - power))
    whole = jnp.clip(whole, -32767.0, 32767.0).astype(jnp.int32)
    power = jnp.broadcast_to(power, (values.shape[0], LANES)).astype(jnp.int32)
    for cols, code in ((slice(0, kept), whole), (slice(kept, kept + LANES), power)):
        word_ref[:, cols] = (code[:half] & 0xFFFF) | (code[half:] << 16)


def decode(word_ref):
    word = word_ref[...]
    code = jnp.concatenate([(word << 16) >> 16, word >> 16], axis=0).astype(jnp.float32)
    return code[:, :-LANES] * jnp.exp2(code[:, -LANES:-LANES + 1] - 15.0)


def first_kernel(stride, keep_ref, got_ref, total_ref, word_ref):
    size = total_ref.shape[0]
    digit = lax.rem(lax.axis_index("feat") // stride, 2)

    def piece(at):
        span = pl.ds(pl.multiple_of(at * size, size), size)
        return keep_ref[span, :] + got_ref[span, :]

    total_ref[...] = piece(digit)
    encode(piece(1 - digit), word_ref)


def middle_kernel(total_ref, word_ref, sum_ref, out_ref):
    total = total_ref[...] + decode(word_ref)
    sum_ref[...] = total
    encode(total, out_ref)


def last_kernel(scale, total_ref, word_ref, label_ref, row_ref):
    total = total_ref[...] + decode(word_ref)
    kept = total.shape[1]
    row_ref[:, :kept] = (total * scale).astype(jnp.bfloat16)
    row_ref[:, kept:] = label_ref[...]


def local_call(kernel, name, *operands, out_shape):
    return pl.pallas_call(
        kernel,
        out_shape=out_shape,
        compiler_params=pltpu.CompilerParams(vmem_limit_bytes=VMEM_LIMIT),
        name=name,
    )(*operands)


def swap(array, axis, offset):
    return lax.ppermute(array, axis, [(i, i ^ offset) for i in range(lax.axis_size(axis))])


def body(features, signs, columns, labels):
    rows, width = features.shape
    feat_count = lax.axis_size("feat")
    feat_index = lax.axis_index("feat")
    tok_count = lax.axis_size("tok")
    kept = columns.shape[0]
    shard = kept // feat_count
    size = rows // 4
    total_type = jax.ShapeDtypeStruct((size, kept), jnp.float32)
    word_type = jax.ShapeDtypeStruct((size // 2, kept + LANES), jnp.int32)
    row_type = jax.ShapeDtypeStruct((size, kept + LANES), jnp.bfloat16)

    first = (feat_index & 1) * (rows // 2) + (feat_index >> 1 & 1) * size
    own_labels = lax.dynamic_slice_in_dim(labels, first, size, 0).astype(jnp.bfloat16)
    own_labels = jnp.broadcast_to(own_labels, (size, LANES))

    send, keep = partial_halves(features, signs, columns, feat_count)
    got = swap(send, "feat", 1)
    total, word = local_call(
        functools.partial(first_kernel, 2), "first_split", keep, got, out_shape=[total_type, word_type]
    )
    word = swap(word, "feat", 2)
    stride = 4
    while stride < feat_count:
        total, word = local_call(
            middle_kernel, "add_encode", total, word, out_shape=[total_type, word_type]
        )
        word = swap(word, "feat", stride)
        stride *= 2
    scale = 1.0 / math.sqrt(width * feat_count)
    ours = local_call(
        functools.partial(last_kernel, scale), "sketch_rows", total, word, own_labels, out_shape=row_type
    )

    stride = 1
    while stride < tok_count:
        ours = jnp.concatenate([ours, swap(ours, "tok", stride)], axis=0)
        stride *= 2
    ours = jnp.concatenate([ours, swap(ours, "feat", 2)], axis=0)
    theirs = swap(ours, "feat", 1)
    concepts = C // tok_count
    gram = gram_blocks(ours, theirs, concepts, shard, kept, C / (rows * tok_count))
    return gram.reshape(concepts, shard, kept)


def solution(mesh):
    in_specs = (P("tok", "feat"), P("feat"), P(), P("tok", None))
    out_specs = P("tok", "feat", None)
    return jax.shard_map(body, mesh=mesh, in_specs=in_specs, out_specs=out_specs, check_vma=False)
```

```python
import functools
import math

import jax
import jax.numpy as jnp
from jax import lax
from jax.experimental import pallas as pl
from jax.experimental.pallas import tpu as pltpu
from jax.sharding import PartitionSpec as P

C = 32
LOW = 256
LANES = 128
CHAINS = 2
VMEM_LIMIT = 48 * 1024 * 1024


def parity_sign(number, bit_count):
    shift = 1
    while shift < bit_count:
        shift *= 2
    while shift > 1:
        shift //= 2
        number = number ^ (number >> shift)
    return (1 - 2 * (number & 1)).astype(jnp.float32)


def partial_kernel(high_count, total_bits, parts, x_hbm, s_hbm, col_hbm, *refs):
    out_refs, (x_buf, s_buf, col_buf, low, high, acc, sems) = refs[:2 * CHAINS], refs[2 * CHAINS:]
    kept = col_hbm.shape[1]
    wide = x_hbm.shape[1] // parts
    me = lax.axis_index("feat")
    col_copy = pltpu.make_async_copy(col_hbm, col_buf, sems.at[parts])
    sign_copy = pltpu.make_async_copy(s_hbm, s_buf, sems.at[parts + 1])
    col_copy.start()
    sign_copy.start()
    copies = []
    for part in range(parts):
        cols = pl.ds(part * wide, wide)
        copies.append(pltpu.make_async_copy(x_hbm.at[:, cols], x_buf.at[:, cols], sems.at[part]))
        copies[-1].start()
    col_copy.wait()
    col = col_buf[...]
    index = lax.broadcasted_iota(jnp.int32, (16, kept), 0)
    inner = parity_sign(index & col, 4)
    outer = parity_sign(index & (col >> 4), 4)
    for row in range(LOW // 16):
        low[row * 16:(row + 1) * 16] = (inner * outer[row:row + 1]).astype(jnp.bfloat16)
    high_index = lax.broadcasted_iota(jnp.int32, high.shape, 0) + me * high_count
    high[...] = parity_sign(high_index & (col >> 8), total_bits - 8)
    sign_copy.wait()
    blocks = wide // LOW
    rows = x_hbm.shape[0]
    for part in range(parts):
        copies[part].wait()
        stack = []
        for block in range(part * blocks, (part + 1) * blocks):
            cols = slice(block * LOW, (block + 1) * LOW)
            stack.append(x_buf[:, cols] * s_buf[:, cols].astype(jnp.bfloat16))
        stack = jnp.concatenate(stack, axis=0)
        for group in range(kept // LOW):
            cols = slice(group * LOW, (group + 1) * LOW)
            products = jnp.dot(stack, low[:, cols], preferred_element_type=jnp.float32)
            total = None
            for at in range(blocks):
                row = part * blocks + at
                term = products[at * rows:(at + 1) * rows] * high[row:row + 1, cols]
                total = term if total is None else total + term
            if part > 0:
                total = total + acc[:, cols]
            acc[:, cols] = total
    size = out_refs[0].shape[0]
    mine = lax.rem(me, 2)
    for chain in range(CHAINS):
        for at, half in enumerate((1 - mine, mine)):
            first = pl.multiple_of((half * CHAINS + chain) * size, size)
            out_refs[2 * chain + at][...] = acc[pl.ds(first, size), :]


def partial_halves(features, signs, columns, feat_count):
    rows, width = features.shape
    kept = columns.shape[0]
    parts = max(1, width // 2048)
    high_count = width // LOW
    total_bits = (width * feat_count).bit_length() - 1
    piece = jax.ShapeDtypeStruct((rows // (2 * CHAINS), kept), jnp.float32)
    return pl.pallas_call(
        functools.partial(partial_kernel, high_count, total_bits, parts),
        in_specs=[pl.BlockSpec(memory_space=pltpu.HBM)] * 3,
        out_specs=[pl.BlockSpec(memory_space=pltpu.VMEM)] * (2 * CHAINS),
        out_shape=[piece] * (2 * CHAINS),
        scratch_shapes=[
            pltpu.VMEM((rows, width), jnp.bfloat16),
            pltpu.VMEM((1, width), jnp.int32),
            pltpu.VMEM((1, kept), jnp.int32),
            pltpu.VMEM((LOW, kept), jnp.bfloat16),
            pltpu.VMEM((high_count, kept), jnp.float32),
            pltpu.VMEM((rows, kept), jnp.float32),
            pltpu.SemaphoreType.DMA((parts + 2,)),
        ],
        compiler_params=pltpu.CompilerParams(vmem_limit_bytes=VMEM_LIMIT),
        cost_estimate=pl.CostEstimate(
            flops=2 * rows * width * kept, bytes_accessed=2 * rows * width + 4 * rows * kept, transcendentals=0
        ),
        name="partial_transform",
    )(*(
        pltpu.with_memory_space_constraint(operand, pltpu.HBM)
        for operand in (features, signs.reshape(1, width), columns.reshape(1, kept))
    ))


def gram_kernel(shard, group, factor, *refs):
    pieces, (out_ref, rows, own, label) = refs[:-4], refs[-4:]
    step = pl.program_id(0)
    kept = out_ref.shape[1]
    wide = group * shard
    steps = pl.num_programs(0)
    size = pieces[0].shape[0]

    @pl.when(step == 0)
    def _():
        first = lax.axis_index("feat") * shard
        source = lax.broadcasted_iota(jnp.int32, (kept, wide), 0)
        lane = lax.broadcasted_iota(jnp.int32, (kept, wide), 1)
        pick = jnp.where(source == first + (lane & (shard - 1)), 1.0, 0.0).astype(jnp.bfloat16)
        lane = lax.broadcasted_iota(jnp.int32, (size, wide), 1)
        for at, ref in enumerate(pieces):
            span = slice(at * size, (at + 1) * size)
            rows[span] = ref[:, :kept]
            named = ref[:, kept:kept + 1].astype(jnp.float32).astype(jnp.int32)
            label[span] = named - lane // shard
        own[...] = jnp.dot(rows[...], pick, preferred_element_type=jnp.float32)

    first = (lax.axis_index("tok") * steps + step) * group
    chosen = jnp.where(label[...] == first, own[...], 0.0).astype(jnp.bfloat16)
    gram = lax.dot_general(chosen, rows[...], (((0,), (0,)), ((), ())), preferred_element_type=jnp.float32)
    out_ref[...] = gram * factor


def gram_blocks(pieces, concepts, shard, kept, factor):
    size, lanes = pieces[0].shape
    tokens = size * len(pieces)
    group = max(1, min(concepts, LOW // shard))
    return pl.pallas_call(
        functools.partial(gram_kernel, shard, group, factor),
        grid=(concepts // group,),
        in_specs=[pl.BlockSpec((size, lanes), lambda i: (0, 0))] * len(pieces),
        out_specs=pl.BlockSpec((group * shard, kept), lambda i: (i, 0)),
        out_shape=jax.ShapeDtypeStruct((concepts * shard, kept), jnp.float32),
        scratch_shapes=[
            pltpu.VMEM((tokens, kept), jnp.bfloat16),
            pltpu.VMEM((tokens, group * shard), jnp.float32),
            pltpu.VMEM((tokens, group * shard), jnp.int32),
        ],
        compiler_params=pltpu.CompilerParams(vmem_limit_bytes=VMEM_LIMIT),
        cost_estimate=pl.CostEstimate(
            flops=2 * tokens * concepts * shard * kept, bytes_accessed=4 * concepts * shard * kept, transcendentals=0
        ),
        name="gram",
    )(*pieces)


def encode(values, word_ref):
    kept = values.shape[1]
    half = values.shape[0] // 2
    top = jnp.max(jnp.abs(values), axis=1, keepdims=True)
    power = jnp.ceil(jnp.log2(jnp.maximum(top, 2.0 ** -100)))
    whole = jnp.round(values * jnp.exp2(15.0 - power))
    whole = jnp.clip(whole, -32767.0, 32767.0).astype(jnp.int32)
    power = jnp.broadcast_to(power, (values.shape[0], LANES)).astype(jnp.int32)
    for cols, code in ((slice(0, kept), whole), (slice(kept, kept + LANES), power)):
        word_ref[:, cols] = (code[:half] & 0xFFFF) | (code[half:] << 16)


def decode(word_ref):
    word = word_ref[...]
    code = jnp.concatenate([(word << 16) >> 16, word >> 16], axis=0).astype(jnp.float32)
    return code[:, :-LANES] * jnp.exp2(code[:, -LANES:-LANES + 1] - 15.0)


def first_kernel(stride, keep_ref, got_ref, total_ref, word_ref):
    size = total_ref.shape[0]
    digit = lax.rem(lax.axis_index("feat") // stride, 2)

    def piece(at):
        span = pl.ds(pl.multiple_of(at * size, size), size)
        return keep_ref[span, :] + got_ref[span, :]

    total_ref[...] = piece(digit)
    encode(piece(1 - digit), word_ref)


def middle_kernel(total_ref, word_ref, sum_ref, out_ref):
    total = total_ref[...] + decode(word_ref)
    sum_ref[...] = total
    encode(total, out_ref)


def last_kernel(scale, total_ref, word_ref, label_ref, row_ref):
    total = total_ref[...] + decode(word_ref)
    kept = total.shape[1]
    row_ref[:, :kept] = (total * scale).astype(jnp.bfloat16)
    row_ref[:, kept:] = label_ref[...]


def local_call(kernel, name, *operands, out_shape):
    return pl.pallas_call(
        kernel,
        out_shape=out_shape,
        compiler_params=pltpu.CompilerParams(vmem_limit_bytes=VMEM_LIMIT),
        name=name,
    )(*operands)


def swap(array, axis, offset):
    return lax.ppermute(array, axis, [(i, i ^ offset) for i in range(lax.axis_size(axis))])


def body(features, signs, columns, labels):
    rows, width = features.shape
    feat_count = lax.axis_size("feat")
    feat_index = lax.axis_index("feat")
    tok_count = lax.axis_size("tok")
    kept = columns.shape[0]
    shard = kept // feat_count
    size = rows // (4 * CHAINS)
    total_type = jax.ShapeDtypeStruct((size, kept), jnp.float32)
    word_type = jax.ShapeDtypeStruct((size // 2, kept + LANES), jnp.int32)
    row_type = jax.ShapeDtypeStruct((size, kept + LANES), jnp.bfloat16)
    scale = 1.0 / math.sqrt(width * feat_count)

    pieces = partial_halves(features, signs, columns, feat_count)
    chains = []
    for chain in range(CHAINS):
        first = ((feat_index & 1) * CHAINS + chain) * 2 * size + (feat_index >> 1 & 1) * size
        own_labels = lax.dynamic_slice_in_dim(labels, first, size, 0).astype(jnp.bfloat16)
        own_labels = jnp.broadcast_to(own_labels, (size, LANES))
        chains.append([own_labels, pieces[2 * chain + 1], swap(pieces[2 * chain], "feat", 1)])
    for chain in chains:
        chain[1:] = local_call(
            functools.partial(first_kernel, 2), "first_split", *chain[1:], out_shape=[total_type, word_type]
        )
        chain[2] = swap(chain[2], "feat", 2)
    stride = 4
    while stride < feat_count:
        for chain in chains:
            chain[1:] = local_call(middle_kernel, "add_encode", *chain[1:], out_shape=[total_type, word_type])
            chain[2] = swap(chain[2], "feat", stride)
        stride *= 2
    rows_of = [
        local_call(
            functools.partial(last_kernel, scale), "sketch_rows", total, word, own_labels, out_shape=row_type
        )
        for own_labels, total, word in chains
    ]
    stride = 1
    while stride < tok_count:
        rows_of = [jnp.concatenate([ours, swap(ours, "tok", stride)], axis=0) for ours in rows_of]
        stride *= 2
    rows_of = [jnp.concatenate([ours, swap(ours, "feat", 2)], axis=0) for ours in rows_of]
    rows_of = rows_of + [swap(ours, "feat", 1) for ours in rows_of]
    concepts = C // tok_count
    gram = gram_blocks(rows_of, concepts, shard, kept, C / (rows * tok_count))
    return gram.reshape(concepts, shard, kept)


def solution(mesh):
    in_specs = (P("tok", "feat"), P("feat"), P(), P("tok", None))
    out_specs = P("tok", "feat", None)
    return jax.shard_map(body, mesh=mesh, in_specs=in_specs, out_specs=out_specs, check_vma=False)
```

```python
import functools
import math

import jax
import jax.numpy as jnp
from jax import lax
from jax.experimental import pallas as pl
from jax.experimental.pallas import tpu as pltpu
from jax.sharding import PartitionSpec as P

C = 32
LOW = 256
LANES = 128
VMEM_LIMIT = 48 * 1024 * 1024


def parity_sign(number, bit_count):
    shift = 1
    while shift < bit_count:
        shift *= 2
    while shift > 1:
        shift //= 2
        number = number ^ (number >> shift)
    return (1 - 2 * (number & 1)).astype(jnp.float32)


def partial_kernel(high_count, total_bits, parts, x_hbm, s_hbm, col_hbm, near_ref, far_ref, x_buf, s_buf, col_buf, low, high, sems):
    kept = col_hbm.shape[1]
    wide = x_hbm.shape[1] // parts
    me = lax.axis_index("feat")
    col_copy = pltpu.make_async_copy(col_hbm, col_buf, sems.at[parts])
    sign_copy = pltpu.make_async_copy(s_hbm, s_buf, sems.at[parts + 1])
    col_copy.start()
    sign_copy.start()
    copies = []
    for part in range(parts):
        cols = pl.ds(part * wide, wide)
        copies.append(pltpu.make_async_copy(x_hbm.at[:, cols], x_buf.at[:, cols], sems.at[part]))
        copies[-1].start()
    col_copy.wait()
    col = col_buf[...]
    index = lax.broadcasted_iota(jnp.int32, (16, kept), 0)
    inner = parity_sign(index & col, 4)
    outer = parity_sign(index & (col >> 4), 4)
    for row in range(LOW // 16):
        low[row * 16:(row + 1) * 16] = (inner * outer[row:row + 1]).astype(jnp.bfloat16)
    high_index = lax.broadcasted_iota(jnp.int32, high.shape, 0) + me * high_count
    high[...] = parity_sign(high_index & (col >> 8), total_bits - 8)
    sign_copy.wait()
    blocks = wide // LOW
    rows = x_hbm.shape[0]
    for part in range(parts):
        copies[part].wait()
        stack = []
        for block in range(part * blocks, (part + 1) * blocks):
            cols = slice(block * LOW, (block + 1) * LOW)
            stack.append(x_buf[:, cols] * s_buf[:, cols].astype(jnp.bfloat16))
        stack = jnp.concatenate(stack, axis=0)
        for group in range(kept // LOW):
            cols = slice(group * LOW, (group + 1) * LOW)
            products = jnp.dot(stack, low[:, cols], preferred_element_type=jnp.float32)
            total = None
            for at in range(blocks):
                row = part * blocks + at
                term = products[at * rows:(at + 1) * rows] * high[row:row + 1, cols]
                total = term if total is None else total + term
            for ref, span in ((near_ref, slice(0, near_ref.shape[0])), (far_ref, slice(near_ref.shape[0], rows))):
                if part > 0:
                    ref[:, cols] += total[span]
                else:
                    ref[:, cols] = total[span]


def partial_rows(features, signs, columns, feat_count, near):
    rows, width = features.shape
    kept = columns.shape[0]
    parts = max(1, width // 2048)
    high_count = width // LOW
    total_bits = (width * feat_count).bit_length() - 1
    return pl.pallas_call(
        functools.partial(partial_kernel, high_count, total_bits, parts),
        in_specs=[pl.BlockSpec(memory_space=pltpu.HBM)] * 3,
        out_specs=[pl.BlockSpec(memory_space=pltpu.VMEM)] * 2,
        out_shape=[jax.ShapeDtypeStruct((size, kept), jnp.float32) for size in (near, rows - near)],
        scratch_shapes=[
            pltpu.VMEM((rows, width), jnp.bfloat16),
            pltpu.VMEM((1, width), jnp.int32),
            pltpu.VMEM((1, kept), jnp.int32),
            pltpu.VMEM((LOW, kept), jnp.bfloat16),
            pltpu.VMEM((high_count, kept), jnp.float32),
            pltpu.SemaphoreType.DMA((parts + 2,)),
        ],
        compiler_params=pltpu.CompilerParams(vmem_limit_bytes=VMEM_LIMIT),
        cost_estimate=pl.CostEstimate(
            flops=2 * rows * width * kept, bytes_accessed=2 * rows * width + 4 * rows * kept, transcendentals=0
        ),
        name="partial_transform",
    )(*(
        pltpu.with_memory_space_constraint(operand, pltpu.HBM)
        for operand in (features, signs.reshape(1, width), columns.reshape(1, kept))
    ))


def gram_kernel(shard, group, factor, own0, got0, own1, got1, out_ref, rows, own, label):
    step = pl.program_id(0)
    kept = out_ref.shape[1]
    wide = group * shard
    steps = pl.num_programs(0)

    def load(ref, first):
        size = ref.shape[0]
        span = slice(first, first + size)
        rows[span] = ref[:, :kept]
        lane = lax.broadcasted_iota(jnp.int32, (size, wide), 1)
        named = ref[:, kept:kept + 1].astype(jnp.float32).astype(jnp.int32)
        label[span] = named - lane // shard

    @pl.when(step == 0)
    def _():
        core = lax.rem(lax.axis_index("feat"), 2)
        for this, pair in ((0, (own0, got1)), (1, (got0, own1))):
            @pl.when(core == this)
            def _():
                load(pair[0], 0)
                load(pair[1], own0.shape[0])
        first = lax.axis_index("feat") * shard
        source = lax.broadcasted_iota(jnp.int32, (kept, wide), 0)
        lane = lax.broadcasted_iota(jnp.int32, (kept, wide), 1)
        pick = jnp.where(source == first + (lane & (shard - 1)), 1.0, 0.0).astype(jnp.bfloat16)
        own[...] = jnp.dot(rows[...], pick, preferred_element_type=jnp.float32)

    first = (lax.axis_index("tok") * steps + step) * group
    chosen = jnp.where(label[...] == first, own[...], 0.0).astype(jnp.bfloat16)
    gram = lax.dot_general(chosen, rows[...], (((0,), (0,)), ((), ())), preferred_element_type=jnp.float32)
    out_ref[...] = gram * factor


def gram_blocks(pieces, concepts, shard, kept, factor):
    tokens = pieces[0].shape[0] + pieces[2].shape[0]
    group = max(1, min(concepts, LOW // shard))
    return pl.pallas_call(
        functools.partial(gram_kernel, shard, group, factor),
        grid=(concepts // group,),
        in_specs=[pl.BlockSpec(piece.shape, lambda i: (0, 0)) for piece in pieces],
        out_specs=pl.BlockSpec((group * shard, kept), lambda i: (i, 0)),
        out_shape=jax.ShapeDtypeStruct((concepts * shard, kept), jnp.float32),
        scratch_shapes=[
            pltpu.VMEM((tokens, kept), jnp.bfloat16),
            pltpu.VMEM((tokens, group * shard), jnp.float32),
            pltpu.VMEM((tokens, group * shard), jnp.int32),
        ],
        compiler_params=pltpu.CompilerParams(vmem_limit_bytes=VMEM_LIMIT),
        cost_estimate=pl.CostEstimate(
            flops=2 * tokens * concepts * shard * kept, bytes_accessed=4 * concepts * shard * kept, transcendentals=0
        ),
        name="gram",
    )(*pieces)


def encode(values, word_ref):
    kept = values.shape[1]
    half = values.shape[0] // 2
    top = jnp.max(jnp.abs(values), axis=1, keepdims=True)
    power = jnp.ceil(jnp.log2(jnp.maximum(top, 2.0 ** -100)))
    whole = jnp.round(values * jnp.exp2(15.0 - power))
    whole = jnp.clip(whole, -32767.0, 32767.0).astype(jnp.int32)
    power = jnp.broadcast_to(power, (values.shape[0], LANES)).astype(jnp.int32)
    for cols, code in ((slice(0, kept), whole), (slice(kept, kept + LANES), power)):
        word_ref[:, cols] = (code[:half] & 0xFFFF) | (code[half:] << 16)


def decode(word_ref):
    word = word_ref[...]
    code = jnp.concatenate([(word << 16) >> 16, word >> 16], axis=0).astype(jnp.float32)
    return code[:, :-LANES] * jnp.exp2(code[:, -LANES:-LANES + 1] - 15.0)


def on_core(core):
    return pl.when(lax.rem(lax.axis_index("feat"), 2) == core)


def both_cores(kernel):
    def combined(operands, *refs):
        results = (len(refs) - 2 * operands) // 2
        for core in range(2):
            taken = refs[core * operands:(core + 1) * operands]
            given = refs[2 * operands + core * results:2 * operands + (core + 1) * results]

            @pl.when(lax.rem(lax.axis_index("feat"), 2) == core)
            def _():
                kernel(*taken, *given)

    return combined


def first_step(keep_ref, got_ref, total_ref, word_ref):
    size = total_ref.shape[0]
    digit = lax.rem(lax.axis_index("feat") // 2, 2)

    def piece(at):
        span = pl.ds(pl.multiple_of(at * size, size), size)
        return keep_ref[span, :] + got_ref[span, :]

    total_ref[...] = piece(digit)
    encode(piece(1 - digit), word_ref)


def middle_step(total_ref, word_ref, sum_ref, out_ref):
    total = total_ref[...] + decode(word_ref)
    sum_ref[...] = total
    encode(total, out_ref)


def last_step(scale, total_ref, word_ref, label_ref, row_ref):
    total = total_ref[...] + decode(word_ref)
    kept = total.shape[1]
    row_ref[:, :kept] = (total * scale).astype(jnp.bfloat16)
    row_ref[:, kept:] = label_ref[...]


def local_call(step, name, chains, out_types):
    operands = len(chains[0])
    results = len(out_types[0])
    out = pl.pallas_call(
        functools.partial(both_cores(step), operands),
        out_shape=[*out_types[0], *out_types[1]],
        compiler_params=pltpu.CompilerParams(vmem_limit_bytes=VMEM_LIMIT),
        name=name,
    )(*chains[0], *chains[1])
    return [list(out[:results]), list(out[results:])]


def move(array, core, tok=0, feat=0):
    tok_count, feat_count = lax.axis_size("tok"), lax.axis_size("feat")
    pairs = [
        (f * tok_count + t, (f ^ feat) * tok_count + (t ^ tok))
        for f in range(core, feat_count, 2)
        for t in range(tok_count)
    ]
    return lax.ppermute(array, ("feat", "tok"), pairs)


def body(features, signs, columns, labels):
    rows, width = features.shape
    feat_count = lax.axis_size("feat")
    feat_index = lax.axis_index("feat")
    tok_count = lax.axis_size("tok")
    kept = columns.shape[0]
    shard = kept // feat_count
    scale = 1.0 / math.sqrt(width * feat_count)
    near = rows // 4

    partials = partial_rows(features, signs, columns, feat_count, near)
    chains, own_labels, out_types, row_types = [], [], [], []
    first = 0
    for core, keep in enumerate(partials):
        size = keep.shape[0] // 2
        chains.append([keep, move(keep, 1 - core, feat=1)])
        labels_at = first + (feat_index >> 1 & 1) * size
        label = lax.dynamic_slice_in_dim(labels, labels_at, size, 0).astype(jnp.bfloat16)
        own_labels.append(jnp.broadcast_to(label, (size, LANES)))
        out_types.append([
            jax.ShapeDtypeStruct((size, kept), jnp.float32),
            jax.ShapeDtypeStruct((size // 2, kept + LANES), jnp.int32),
        ])
        row_types.append([jax.ShapeDtypeStruct((size, kept + LANES), jnp.bfloat16)])
        first += 2 * size
    chains = local_call(first_step, "first_split", chains, out_types)
    chains = [[total, move(word, core, feat=2)] for core, (total, word) in enumerate(chains)]
    stride = 4
    while stride < feat_count:
        chains = local_call(middle_step, "add_encode", chains, out_types)
        chains = [[total, move(word, core, feat=stride)] for core, (total, word) in enumerate(chains)]
        stride *= 2
    chains = [[*chain, label] for chain, label in zip(chains, own_labels)]
    chains = local_call(functools.partial(last_step, scale), "sketch_rows", chains, row_types)
    pieces = []
    for core, (ours,) in enumerate(chains):
        stride = 2
        while stride < tok_count:
            ours = jnp.concatenate([ours, move(ours, core, tok=stride)], axis=0)
            stride *= 2
        received = [move(ours, core, tok=1, feat=2)] if tok_count > 1 else []
        received += [move(ours, core, feat=2)]
        received += [move(ours, core, tok=1)] if tok_count > 1 else []
        ours = jnp.concatenate([ours] + received, axis=0)
        pieces += [ours, move(ours, core, feat=1)]
    concepts = C // tok_count
    gram = gram_blocks(pieces, concepts, shard, kept, C / (rows * tok_count))
    return gram.reshape(concepts, shard, kept)


def solution(mesh):
    in_specs = (P("tok", "feat"), P("feat"), P(), P("tok", None))
    out_specs = P("tok", "feat", None)
    return jax.shard_map(body, mesh=mesh, in_specs=in_specs, out_specs=out_specs, check_vma=False)
```

```python
import functools
import math

import jax
import jax.numpy as jnp
from jax import lax
from jax.experimental import pallas as pl
from jax.experimental.pallas import tpu as pltpu
from jax.sharding import PartitionSpec as P

C = 32
LOW = 256
LANES = 128
VMEM_LIMIT = 48 * 1024 * 1024


def parity_sign(number, bit_count):
    shift = 1
    while shift < bit_count:
        shift *= 2
    while shift > 1:
        shift //= 2
        number = number ^ (number >> shift)
    return (1 - 2 * (number & 1)).astype(jnp.float32)


def own_half():
    bits = lax.axis_index("feat") ^ lax.axis_index("tok")
    total = bits & 1
    for position in range(1, max(lax.axis_size("feat"), lax.axis_size("tok")).bit_length() - 1):
        total = total ^ (bits >> position & 1)
    return total


def partial_kernel(high_count, total_bits, parts, x_hbm, s_hbm, col_hbm, send_ref, keep_ref, x_buf, s_buf, col_buf, low, high, acc, sems):
    kept = col_hbm.shape[1]
    wide = x_hbm.shape[1] // parts
    me = lax.axis_index("feat")
    col_copy = pltpu.make_async_copy(col_hbm, col_buf, sems.at[parts])
    sign_copy = pltpu.make_async_copy(s_hbm, s_buf, sems.at[parts + 1])
    col_copy.start()
    sign_copy.start()
    copies = []
    for part in range(parts):
        cols = pl.ds(part * wide, wide)
        copies.append(pltpu.make_async_copy(x_hbm.at[:, cols], x_buf.at[:, cols], sems.at[part]))
        copies[-1].start()
    col_copy.wait()
    col = col_buf[...]
    index = lax.broadcasted_iota(jnp.int32, (16, kept), 0)
    inner = parity_sign(index & col, 4)
    outer = parity_sign(index & (col >> 4), 4)
    for row in range(LOW // 16):
        low[row * 16:(row + 1) * 16] = (inner * outer[row:row + 1]).astype(jnp.bfloat16)
    high_index = lax.broadcasted_iota(jnp.int32, high.shape, 0) + me * high_count
    high[...] = parity_sign(high_index & (col >> 8), total_bits - 8)
    sign_copy.wait()
    blocks = wide // LOW
    rows = x_hbm.shape[0]
    for part in range(parts):
        copies[part].wait()
        stack = []
        for block in range(part * blocks, (part + 1) * blocks):
            cols = slice(block * LOW, (block + 1) * LOW)
            stack.append(x_buf[:, cols] * s_buf[:, cols].astype(jnp.bfloat16))
        stack = jnp.concatenate(stack, axis=0)
        for group in range(kept // LOW):
            cols = slice(group * LOW, (group + 1) * LOW)
            products = jnp.dot(stack, low[:, cols], preferred_element_type=jnp.float32)
            total = None
            for at in range(blocks):
                row = part * blocks + at
                term = products[at * rows:(at + 1) * rows] * high[row:row + 1, cols]
                total = term if total is None else total + term
            if part > 0:
                total = total + acc[:, cols]
            acc[:, cols] = total
    half = keep_ref.shape[0]
    mine = own_half()
    keep_ref[...] = acc[pl.ds(pl.multiple_of(mine * half, half), half), :]
    send_ref[...] = acc[pl.ds(pl.multiple_of((1 - mine) * half, half), half), :]


def partial_halves(features, signs, columns, feat_count):
    rows, width = features.shape
    kept = columns.shape[0]
    parts = max(1, width // 2048)
    high_count = width // LOW
    total_bits = (width * feat_count).bit_length() - 1
    half = jax.ShapeDtypeStruct((rows // 2, kept), jnp.float32)
    return pl.pallas_call(
        functools.partial(partial_kernel, high_count, total_bits, parts),
        in_specs=[pl.BlockSpec(memory_space=pltpu.HBM)] * 3,
        out_specs=[pl.BlockSpec(memory_space=pltpu.VMEM)] * 2,
        out_shape=[half, half],
        scratch_shapes=[
            pltpu.VMEM((rows, width), jnp.bfloat16),
            pltpu.VMEM((1, width), jnp.int32),
            pltpu.VMEM((1, kept), jnp.int32),
            pltpu.VMEM((LOW, kept), jnp.bfloat16),
            pltpu.VMEM((high_count, kept), jnp.float32),
            pltpu.VMEM((rows, kept), jnp.float32),
            pltpu.SemaphoreType.DMA((parts + 2,)),
        ],
        compiler_params=pltpu.CompilerParams(vmem_limit_bytes=VMEM_LIMIT),
        cost_estimate=pl.CostEstimate(
            flops=2 * rows * width * kept, bytes_accessed=2 * rows * width + 4 * rows * kept, transcendentals=0
        ),
        name="partial_transform",
    )(*(
        pltpu.with_memory_space_constraint(operand, pltpu.HBM)
        for operand in (features, signs.reshape(1, width), columns.reshape(1, kept))
    ))


def gram_kernel(shard, group, factor, a_ref, b_ref, out_ref, rows, own, label):
    step = pl.program_id(0)
    kept = out_ref.shape[1]
    wide = group * shard
    steps = pl.num_programs(0)
    half = a_ref.shape[0]

    @pl.when(step == 0)
    def _():
        first = lax.axis_index("feat") * shard
        source = lax.broadcasted_iota(jnp.int32, (kept, wide), 0)
        lane = lax.broadcasted_iota(jnp.int32, (kept, wide), 1)
        pick = jnp.where(source == first + (lane & (shard - 1)), 1.0, 0.0).astype(jnp.bfloat16)
        lane = lax.broadcasted_iota(jnp.int32, (half, wide), 1)
        for at, ref in enumerate((a_ref, b_ref)):
            span = slice(at * half, (at + 1) * half)
            rows[span] = ref[:, :kept]
            named = ref[:, kept:kept + 1].astype(jnp.float32).astype(jnp.int32)
            label[span] = named - lane // shard
        own[...] = jnp.dot(rows[...], pick, preferred_element_type=jnp.float32)

    first = (lax.axis_index("tok") * steps + step) * group
    chosen = jnp.where(label[...] == first, own[...], 0.0).astype(jnp.bfloat16)
    gram = lax.dot_general(chosen, rows[...], (((0,), (0,)), ((), ())), preferred_element_type=jnp.float32)
    out_ref[...] = gram * factor


def gram_blocks(ours, theirs, concepts, shard, kept, factor):
    tokens, lanes = ours.shape
    group = max(1, min(concepts, LOW // shard))
    return pl.pallas_call(
        functools.partial(gram_kernel, shard, group, factor),
        grid=(concepts // group,),
        in_specs=[pl.BlockSpec((tokens, lanes), lambda i: (0, 0))] * 2,
        out_specs=pl.BlockSpec((group * shard, kept), lambda i: (i, 0)),
        out_shape=jax.ShapeDtypeStruct((concepts * shard, kept), jnp.float32),
        scratch_shapes=[
            pltpu.VMEM((2 * tokens, kept), jnp.bfloat16),
            pltpu.VMEM((2 * tokens, group * shard), jnp.float32),
            pltpu.VMEM((2 * tokens, group * shard), jnp.int32),
        ],
        compiler_params=pltpu.CompilerParams(vmem_limit_bytes=VMEM_LIMIT),
        cost_estimate=pl.CostEstimate(
            flops=4 * tokens * concepts * shard * kept, bytes_accessed=4 * concepts * shard * kept, transcendentals=0
        ),
        name="gram",
    )(ours, theirs)


def encode(values, word_ref):
    kept = values.shape[1]
    half = values.shape[0] // 2
    top = jnp.max(jnp.abs(values), axis=1, keepdims=True)
    power = jnp.ceil(jnp.log2(jnp.maximum(top, 2.0 ** -100)))
    whole = jnp.round(values * jnp.exp2(15.0 - power))
    whole = jnp.clip(whole, -32767.0, 32767.0).astype(jnp.int32)
    power = jnp.broadcast_to(power, (values.shape[0], LANES)).astype(jnp.int32)
    for cols, code in ((slice(0, kept), whole), (slice(kept, kept + LANES), power)):
        word_ref[:, cols] = (code[:half] & 0xFFFF) | (code[half:] << 16)


def decode(word_ref):
    word = word_ref[...]
    code = jnp.concatenate([(word << 16) >> 16, word >> 16], axis=0).astype(jnp.float32)
    return code[:, :-LANES] * jnp.exp2(code[:, -LANES:-LANES + 1] - 15.0)


def first_kernel(stride, keep_ref, got_ref, total_ref, word_ref):
    size = total_ref.shape[0]
    digit = lax.rem(lax.axis_index("feat") // stride, 2)

    def piece(at):
        span = pl.ds(pl.multiple_of(at * size, size), size)
        return keep_ref[span, :] + got_ref[span, :]

    total_ref[...] = piece(digit)
    encode(piece(1 - digit), word_ref)


def middle_kernel(total_ref, word_ref, sum_ref, out_ref):
    total = total_ref[...] + decode(word_ref)
    sum_ref[...] = total
    encode(total, out_ref)


def last_kernel(scale, total_ref, word_ref, label_ref, row_ref):
    total = total_ref[...] + decode(word_ref)
    kept = total.shape[1]
    row_ref[:, :kept] = (total * scale).astype(jnp.bfloat16)
    row_ref[:, kept:] = label_ref[...]


def local_call(kernel, name, *operands, out_shape):
    return pl.pallas_call(
        kernel,
        out_shape=out_shape,
        compiler_params=pltpu.CompilerParams(vmem_limit_bytes=VMEM_LIMIT),
        name=name,
    )(*operands)


def swap(array, tok=0, feat=0):
    tok_count, feat_count = lax.axis_size("tok"), lax.axis_size("feat")
    pairs = [
        (f * tok_count + t, (f ^ feat) * tok_count + (t ^ tok))
        for f in range(feat_count)
        for t in range(tok_count)
    ]
    return lax.ppermute(array, ("feat", "tok"), pairs)


def body(features, signs, columns, labels):
    rows, width = features.shape
    feat_count = lax.axis_size("feat")
    feat_index = lax.axis_index("feat")
    tok_count = lax.axis_size("tok")
    kept = columns.shape[0]
    shard = kept // feat_count
    size = rows // 4
    total_type = jax.ShapeDtypeStruct((size, kept), jnp.float32)
    word_type = jax.ShapeDtypeStruct((size // 2, kept + LANES), jnp.int32)
    row_type = jax.ShapeDtypeStruct((size, kept + LANES), jnp.bfloat16)

    first = own_half() * (rows // 2) + (feat_index >> 1 & 1) * size
    own_labels = lax.dynamic_slice_in_dim(labels, first, size, 0).astype(jnp.bfloat16)
    own_labels = jnp.broadcast_to(own_labels, (size, LANES))

    send, keep = partial_halves(features, signs, columns, feat_count)
    got = swap(send, feat=1)
    total, word = local_call(
        functools.partial(first_kernel, 2), "first_split", keep, got, out_shape=[total_type, word_type]
    )
    word = swap(word, feat=3)
    stride = 4
    while stride < feat_count:
        total, word = local_call(
            middle_kernel, "add_encode", total, word, out_shape=[total_type, word_type]
        )
        word = swap(word, feat=stride | 1)
        stride *= 2
    scale = 1.0 / math.sqrt(width * feat_count)
    ours = local_call(
        functools.partial(last_kernel, scale), "sketch_rows", total, word, own_labels, out_shape=row_type
    )

    stride = 1
    while stride < tok_count:
        ours = jnp.concatenate([ours, swap(ours, tok=stride, feat=1)], axis=0)
        stride *= 2
    ours = jnp.concatenate([ours, swap(ours, feat=3)], axis=0)
    theirs = swap(ours, feat=1)
    concepts = C // tok_count
    gram = gram_blocks(ours, theirs, concepts, shard, kept, C / (rows * tok_count))
    return gram.reshape(concepts, shard, kept)


def solution(mesh):
    in_specs = (P("tok", "feat"), P("feat"), P(), P("tok", None))
    out_specs = P("tok", "feat", None)
    return jax.shard_map(body, mesh=mesh, in_specs=in_specs, out_specs=out_specs, check_vma=False)
```

```python
import functools
import math

import jax
import jax.numpy as jnp
from jax import lax
from jax.experimental import pallas as pl
from jax.experimental.pallas import tpu as pltpu
from jax.sharding import PartitionSpec as P

C = 32
LOW = 256
LANES = 128
VMEM_LIMIT = 48 * 1024 * 1024


def parity_sign(number, bit_count):
    shift = 1
    while shift < bit_count:
        shift *= 2
    while shift > 1:
        shift //= 2
        number = number ^ (number >> shift)
    return (1 - 2 * (number & 1)).astype(jnp.float32)


def partial_kernel(high_count, total_bits, parts, x_hbm, s_hbm, col_hbm, send_ref, keep_ref, x_buf, s_buf, col_buf, low, high, acc, sems):
    kept = col_hbm.shape[1]
    wide = x_hbm.shape[1] // parts
    me = lax.axis_index("feat")
    col_copy = pltpu.make_async_copy(col_hbm, col_buf, sems.at[parts])
    sign_copy = pltpu.make_async_copy(s_hbm, s_buf, sems.at[parts + 1])
    col_copy.start()
    sign_copy.start()
    copies = []
    for part in range(parts):
        cols = pl.ds(part * wide, wide)
        copies.append(pltpu.make_async_copy(x_hbm.at[:, cols], x_buf.at[:, cols], sems.at[part]))
        copies[-1].start()
    col_copy.wait()
    col = col_buf[...]
    index = lax.broadcasted_iota(jnp.int32, (16, kept), 0)
    inner = parity_sign(index & col, 4)
    outer = parity_sign(index & (col >> 4), 4)
    for row in range(LOW // 16):
        low[row * 16:(row + 1) * 16] = (inner * outer[row:row + 1]).astype(jnp.bfloat16)
    high_index = lax.broadcasted_iota(jnp.int32, high.shape, 0) + me * high_count
    high[...] = parity_sign(high_index & (col >> 8), total_bits - 8)
    sign_copy.wait()
    blocks = wide // LOW
    rows = x_hbm.shape[0]
    for part in range(parts):
        copies[part].wait()
        stack = []
        for block in range(part * blocks, (part + 1) * blocks):
            cols = slice(block * LOW, (block + 1) * LOW)
            stack.append(x_buf[:, cols] * s_buf[:, cols].astype(jnp.bfloat16))
        stack = jnp.concatenate(stack, axis=0)
        for group in range(kept // LOW):
            cols = slice(group * LOW, (group + 1) * LOW)
            products = jnp.dot(stack, low[:, cols], preferred_element_type=jnp.float32)
            total = None
            for at in range(blocks):
                row = part * blocks + at
                term = products[at * rows:(at + 1) * rows] * high[row:row + 1, cols]
                total = term if total is None else total + term
            if part > 0:
                total = total + acc[:, cols]
            acc[:, cols] = total
    half = keep_ref.shape[0]
    mine = lax.rem(me, 2)
    keep_ref[...] = acc[pl.ds(pl.multiple_of(mine * half, half), half), :]
    send_ref[...] = acc[pl.ds(pl.multiple_of((1 - mine) * half, half), half), :]


def partial_halves(features, signs, columns, feat_count):
    rows, width = features.shape
    kept = columns.shape[0]
    parts = max(1, width // 2048)
    high_count = width // LOW
    total_bits = (width * feat_count).bit_length() - 1
    half = jax.ShapeDtypeStruct((rows // 2, kept), jnp.float32)
    return pl.pallas_call(
        functools.partial(partial_kernel, high_count, total_bits, parts),
        in_specs=[pl.BlockSpec(memory_space=pltpu.HBM)] * 3,
        out_specs=[pl.BlockSpec(memory_space=pltpu.VMEM)] * 2,
        out_shape=[half, half],
        scratch_shapes=[
            pltpu.VMEM((rows, width), jnp.bfloat16),
            pltpu.VMEM((1, width), jnp.int32),
            pltpu.VMEM((1, kept), jnp.int32),
            pltpu.VMEM((LOW, kept), jnp.bfloat16),
            pltpu.VMEM((high_count, kept), jnp.float32),
            pltpu.VMEM((rows, kept), jnp.float32),
            pltpu.SemaphoreType.DMA((parts + 2,)),
        ],
        compiler_params=pltpu.CompilerParams(vmem_limit_bytes=VMEM_LIMIT),
        cost_estimate=pl.CostEstimate(
            flops=2 * rows * width * kept, bytes_accessed=2 * rows * width + 4 * rows * kept, transcendentals=0
        ),
        name="partial_transform",
    )(*(
        pltpu.with_memory_space_constraint(operand, pltpu.HBM)
        for operand in (features, signs.reshape(1, width), columns.reshape(1, kept))
    ))


def gram_kernel(shard, group, factor, a_ref, b_ref, out_ref, rows, own, label):
    step = pl.program_id(0)
    kept = out_ref.shape[1]
    wide = group * shard
    steps = pl.num_programs(0)
    half = a_ref.shape[0]

    @pl.when(step == 0)
    def _():
        first = lax.axis_index("feat") * shard
        source = lax.broadcasted_iota(jnp.int32, (kept, wide), 0)
        lane = lax.broadcasted_iota(jnp.int32, (kept, wide), 1)
        pick = jnp.where(source == first + (lane & (shard - 1)), 1.0, 0.0).astype(jnp.bfloat16)
        lane = lax.broadcasted_iota(jnp.int32, (half, wide), 1)
        for at, ref in enumerate((a_ref, b_ref)):
            span = slice(at * half, (at + 1) * half)
            rows[span] = ref[:, :kept]
            named = ref[:, kept:kept + 1].astype(jnp.float32).astype(jnp.int32)
            label[span] = named - lane // shard
        own[...] = jnp.dot(rows[...], pick, preferred_element_type=jnp.float32)

    first = (lax.axis_index("tok") * steps + step) * group
    chosen = jnp.where(label[...] == first, own[...], 0.0).astype(jnp.bfloat16)
    gram = lax.dot_general(chosen, rows[...], (((0,), (0,)), ((), ())), preferred_element_type=jnp.float32)
    out_ref[...] = gram * factor


def gram_blocks(ours, theirs, concepts, shard, kept, factor):
    tokens, lanes = ours.shape
    group = max(1, min(concepts, LOW // shard))
    return pl.pallas_call(
        functools.partial(gram_kernel, shard, group, factor),
        grid=(concepts // group,),
        in_specs=[pl.BlockSpec((tokens, lanes), lambda i: (0, 0))] * 2,
        out_specs=pl.BlockSpec((group * shard, kept), lambda i: (i, 0)),
        out_shape=jax.ShapeDtypeStruct((concepts * shard, kept), jnp.float32),
        scratch_shapes=[
            pltpu.VMEM((2 * tokens, kept), jnp.bfloat16),
            pltpu.VMEM((2 * tokens, group * shard), jnp.float32),
            pltpu.VMEM((2 * tokens, group * shard), jnp.int32),
        ],
        compiler_params=pltpu.CompilerParams(vmem_limit_bytes=VMEM_LIMIT),
        cost_estimate=pl.CostEstimate(
            flops=4 * tokens * concepts * shard * kept, bytes_accessed=4 * concepts * shard * kept, transcendentals=0
        ),
        name="gram",
    )(ours, theirs)


def encode(values, word_ref):
    kept = values.shape[1]
    half = values.shape[0] // 2
    top = jnp.max(jnp.abs(values), axis=1, keepdims=True)
    power = jnp.ceil(jnp.log2(jnp.maximum(top, 2.0 ** -100)))
    whole = jnp.round(values * jnp.exp2(15.0 - power))
    whole = jnp.clip(whole, -32767.0, 32767.0).astype(jnp.int32)
    power = jnp.broadcast_to(power, (values.shape[0], LANES)).astype(jnp.int32)
    for cols, code in ((slice(0, kept), whole), (slice(kept, kept + LANES), power)):
        word_ref[:, cols] = (code[:half] & 0xFFFF) | (code[half:] << 16)


def decode(word_ref):
    word = word_ref[...]
    code = jnp.concatenate([(word << 16) >> 16, word >> 16], axis=0).astype(jnp.float32)
    return code[:, :-LANES] * jnp.exp2(code[:, -LANES:-LANES + 1] - 15.0)


def first_kernel(stride, keep_ref, got_ref, total_ref, here_ref, there_ref):
    size = total_ref.shape[0]
    digit = lax.rem(lax.axis_index("feat") // stride, 2)

    def piece(at):
        span = pl.ds(pl.multiple_of(at * size, size), size)
        return keep_ref[span, :] + got_ref[span, :]

    total_ref[...] = piece(digit)
    encode(piece(digit), here_ref)
    encode(piece(1 - digit), there_ref)


def square_kernel(total_ref, x_ref, z_ref, both_ref, sum_ref, out_ref):
    total = (total_ref[...] + decode(x_ref)) + (decode(z_ref) + decode(both_ref))
    sum_ref[...] = total
    encode(total, out_ref)


def middle_kernel(total_ref, word_ref, sum_ref, out_ref):
    total = total_ref[...] + decode(word_ref)
    sum_ref[...] = total
    encode(total, out_ref)


def last_kernel(scale, total_ref, word_ref, label_ref, row_ref):
    total = total_ref[...] + decode(word_ref)
    kept = total.shape[1]
    row_ref[:, :kept] = (total * scale).astype(jnp.bfloat16)
    row_ref[:, kept:] = label_ref[...]


def local_call(kernel, name, *operands, out_shape):
    return pl.pallas_call(
        kernel,
        out_shape=out_shape,
        compiler_params=pltpu.CompilerParams(vmem_limit_bytes=VMEM_LIMIT),
        name=name,
    )(*operands)


def swap(array, tok=0, feat=0):
    tok_count, feat_count = lax.axis_size("tok"), lax.axis_size("feat")
    pairs = [
        (f * tok_count + t, (f ^ feat) * tok_count + (t ^ tok))
        for f in range(feat_count)
        for t in range(tok_count)
    ]
    return lax.ppermute(array, ("feat", "tok"), pairs)


def body(features, signs, columns, labels):
    rows, width = features.shape
    feat_count = lax.axis_size("feat")
    feat_index = lax.axis_index("feat")
    tok_count = lax.axis_size("tok")
    kept = columns.shape[0]
    shard = kept // feat_count
    size = rows // 4
    total_type = jax.ShapeDtypeStruct((size, kept), jnp.float32)
    word_type = jax.ShapeDtypeStruct((size // 2, kept + LANES), jnp.int32)
    row_type = jax.ShapeDtypeStruct((size, kept + LANES), jnp.bfloat16)

    first = (feat_index & 1) * (rows // 2) + (feat_index >> 1 & 1) * size
    own_labels = lax.dynamic_slice_in_dim(labels, first, size, 0).astype(jnp.bfloat16)
    own_labels = jnp.broadcast_to(own_labels, (size, LANES))

    send, keep = partial_halves(features, signs, columns, feat_count)
    got = swap(send, feat=1)
    total, here, there = local_call(
        functools.partial(first_kernel, 2), "first_split", keep, got, out_shape=[total_type, word_type, word_type]
    )
    total, word = local_call(
        square_kernel,
        "add_square",
        total,
        swap(there, feat=2),
        swap(here, feat=4),
        swap(there, feat=6),
        out_shape=[total_type, word_type],
    )
    word = swap(word, feat=8)
    stride = 16
    while stride < feat_count:
        total, word = local_call(
            middle_kernel, "add_encode", total, word, out_shape=[total_type, word_type]
        )
        word = swap(word, feat=stride)
        stride *= 2
    scale = 1.0 / math.sqrt(width * feat_count)
    ours = local_call(
        functools.partial(last_kernel, scale), "sketch_rows", total, word, own_labels, out_shape=row_type
    )

    stride = 2
    while stride < tok_count:
        ours = jnp.concatenate([ours, swap(ours, tok=stride)], axis=0)
        stride *= 2
    received = [swap(ours, tok=1, feat=2)] if tok_count > 1 else []
    received += [swap(ours, feat=2)]
    received += [swap(ours, tok=1)] if tok_count > 1 else []
    ours = jnp.concatenate([ours] + received, axis=0)
    theirs = swap(ours, feat=1)
    concepts = C // tok_count
    gram = gram_blocks(ours, theirs, concepts, shard, kept, C / (rows * tok_count))
    return gram.reshape(concepts, shard, kept)


def solution(mesh):
    in_specs = (P("tok", "feat"), P("feat"), P(), P("tok", None))
    out_specs = P("tok", "feat", None)
    return jax.shard_map(body, mesh=mesh, in_specs=in_specs, out_specs=out_specs, check_vma=False)
```

```python
import functools
import math

import jax
import jax.numpy as jnp
from jax import lax
from jax.experimental import pallas as pl
from jax.experimental.pallas import tpu as pltpu
from jax.sharding import PartitionSpec as P

C = 32
LOW = 256
LANES = 128
VMEM_LIMIT = 48 * 1024 * 1024


def parity_sign(number, bit_count):
    shift = 1
    while shift < bit_count:
        shift *= 2
    while shift > 1:
        shift //= 2
        number = number ^ (number >> shift)
    return (1 - 2 * (number & 1)).astype(jnp.float32)


def partial_kernel(high_count, total_bits, parts, x_hbm, s_hbm, col_hbm, send_ref, keep_ref, x_buf, s_buf, col_buf, low, high, acc, sems):
    kept = col_hbm.shape[1]
    wide = x_hbm.shape[1] // parts
    me = lax.axis_index("feat")
    col_copy = pltpu.make_async_copy(col_hbm, col_buf, sems.at[parts])
    sign_copy = pltpu.make_async_copy(s_hbm, s_buf, sems.at[parts + 1])
    col_copy.start()
    sign_copy.start()
    copies = []
    for part in range(parts):
        cols = pl.ds(part * wide, wide)
        copies.append(pltpu.make_async_copy(x_hbm.at[:, cols], x_buf.at[:, cols], sems.at[part]))
        copies[-1].start()
    col_copy.wait()
    col = col_buf[...]
    index = lax.broadcasted_iota(jnp.int32, (16, kept), 0)
    inner = parity_sign(index & col, 4)
    outer = parity_sign(index & (col >> 4), 4)
    for row in range(LOW // 16):
        low[row * 16:(row + 1) * 16] = (inner * outer[row:row + 1]).astype(jnp.bfloat16)
    high_index = lax.broadcasted_iota(jnp.int32, high.shape, 0) + me * high_count
    high[...] = parity_sign(high_index & (col >> 8), total_bits - 8)
    sign_copy.wait()
    blocks = wide // LOW
    rows = x_hbm.shape[0]
    for part in range(parts):
        copies[part].wait()
        stack = []
        for block in range(part * blocks, (part + 1) * blocks):
            cols = slice(block * LOW, (block + 1) * LOW)
            stack.append(x_buf[:, cols] * s_buf[:, cols].astype(jnp.bfloat16))
        stack = jnp.concatenate(stack, axis=0)
        for group in range(kept // LOW):
            cols = slice(group * LOW, (group + 1) * LOW)
            products = jnp.dot(stack, low[:, cols], preferred_element_type=jnp.float32)
            total = None
            for at in range(blocks):
                row = part * blocks + at
                term = products[at * rows:(at + 1) * rows] * high[row:row + 1, cols]
                total = term if total is None else total + term
            if part > 0:
                total = total + acc[:, cols]
            acc[:, cols] = total
    half = keep_ref.shape[0]
    mine = lax.rem(me, 2)
    keep_ref[...] = acc[pl.ds(pl.multiple_of(mine * half, half), half), :]
    send_ref[...] = acc[pl.ds(pl.multiple_of((1 - mine) * half, half), half), :]


def partial_halves(features, signs, columns, feat_count):
    rows, width = features.shape
    kept = columns.shape[0]
    parts = max(1, width // 2048)
    high_count = width // LOW
    total_bits = (width * feat_count).bit_length() - 1
    half = jax.ShapeDtypeStruct((rows // 2, kept), jnp.float32)
    return pl.pallas_call(
        functools.partial(partial_kernel, high_count, total_bits, parts),
        in_specs=[pl.BlockSpec(memory_space=pltpu.HBM)] * 3,
        out_specs=[pl.BlockSpec(memory_space=pltpu.VMEM)] * 2,
        out_shape=[half, half],
        scratch_shapes=[
            pltpu.VMEM((rows, width), jnp.bfloat16),
            pltpu.VMEM((1, width), jnp.int32),
            pltpu.VMEM((1, kept), jnp.int32),
            pltpu.VMEM((LOW, kept), jnp.bfloat16),
            pltpu.VMEM((high_count, kept), jnp.float32),
            pltpu.VMEM((rows, kept), jnp.float32),
            pltpu.SemaphoreType.DMA((parts + 2,)),
        ],
        compiler_params=pltpu.CompilerParams(vmem_limit_bytes=VMEM_LIMIT),
        cost_estimate=pl.CostEstimate(
            flops=2 * rows * width * kept, bytes_accessed=2 * rows * width + 4 * rows * kept, transcendentals=0
        ),
        name="partial_transform",
    )(*(
        pltpu.with_memory_space_constraint(operand, pltpu.HBM)
        for operand in (features, signs.reshape(1, width), columns.reshape(1, kept))
    ))


def mask_operands(shard, wide, factor, row_ref):
    kept = row_ref.shape[1] - LANES
    first = lax.axis_index("feat") * shard
    start = pl.multiple_of(first // LANES * LANES, LANES)
    window = row_ref[:, pl.ds(start, LANES)].astype(jnp.float32) * factor
    window = pltpu.roll(window, lax.rem(LANES - (first - start), LANES), 1)
    lane = lax.broadcasted_iota(jnp.int32, window.shape, 1)
    own = jnp.where(lane < shard, window, 0.0)
    step = shard
    while step < LANES:
        own = own + pltpu.roll(own, step, 1)
        step *= 2
    own = jnp.concatenate([own] * -(-wide // LANES), axis=1)[:, :wide]
    named = row_ref[:, kept:kept + 1].astype(jnp.float32).astype(jnp.int32)
    label = named - lax.broadcasted_iota(jnp.int32, own.shape, 1) // shard
    return own, label


def mask_kernel(shard, wide, factor, row_ref, own_ref, label_ref):
    own_ref[...], label_ref[...] = mask_operands(shard, wide, factor, row_ref)


def gram_kernel(shard, group, factor, ours, own_ref, label_ref, theirs, out_hbm, rows, blocks, sems):
    kept = rows.shape[1]
    half = ours.shape[0]
    wide = group * shard
    steps = blocks.shape[0]
    rows[:half] = ours[:, :kept]
    rows[half:] = theirs[:, :kept]
    parts = ((own_ref[...], label_ref[...]), mask_operands(shard, wide, factor, theirs))
    base = lax.axis_index("tok") * steps * group
    copies = []
    for step in range(steps):
        chosen = jnp.concatenate(
            [jnp.where(label == base + step * group, own, 0.0).astype(jnp.bfloat16) for own, label in parts], axis=0
        )
        blocks[step] = lax.dot_general(
            chosen, rows[...], (((0,), (0,)), ((), ())), preferred_element_type=jnp.float32
        )
        copies.append(
            pltpu.make_async_copy(blocks.at[step], out_hbm.at[pl.ds(step * wide, wide), :], sems.at[step])
        )
        copies[-1].start()
    for copy in copies:
        copy.wait()


def gram_blocks(ours, theirs, concepts, shard, kept, factor):
    tokens = ours.shape[0]
    group = max(1, min(concepts, LOW // shard))
    wide = group * shard
    steps = concepts // group
    params = pltpu.CompilerParams(vmem_limit_bytes=VMEM_LIMIT)
    own, label = pl.pallas_call(
        functools.partial(mask_kernel, shard, wide, factor),
        out_shape=[jax.ShapeDtypeStruct((tokens, wide), dtype) for dtype in (jnp.float32, jnp.int32)],
        compiler_params=params,
        name="mask_ours",
    )(ours)
    return pl.pallas_call(
        functools.partial(gram_kernel, shard, group, factor),
        in_specs=[pl.BlockSpec(memory_space=pltpu.VMEM)] * 4,
        out_specs=pl.BlockSpec(memory_space=pltpu.HBM),
        out_shape=jax.ShapeDtypeStruct((concepts * shard, kept), jnp.float32),
        scratch_shapes=[
            pltpu.VMEM((2 * tokens, kept), jnp.bfloat16),
            pltpu.VMEM((steps, wide, kept), jnp.float32),
            pltpu.SemaphoreType.DMA((steps,)),
        ],
        compiler_params=params,
        cost_estimate=pl.CostEstimate(
            flops=4 * tokens * concepts * shard * kept, bytes_accessed=4 * concepts * shard * kept, transcendentals=0
        ),
        name="gram",
    )(ours, own, label, theirs)


def encode(values, word_ref):
    kept = values.shape[1]
    half = values.shape[0] // 2
    top = jnp.max(jnp.abs(values), axis=1, keepdims=True)
    power = jnp.ceil(jnp.log2(jnp.maximum(top, 2.0 ** -100)))
    whole = jnp.round(values * jnp.exp2(15.0 - power))
    whole = jnp.clip(whole, -32767.0, 32767.0).astype(jnp.int32)
    power = jnp.broadcast_to(power, (values.shape[0], LANES)).astype(jnp.int32)
    for cols, code in ((slice(0, kept), whole), (slice(kept, kept + LANES), power)):
        word_ref[:, cols] = (code[:half] & 0xFFFF) | (code[half:] << 16)


def decode(word_ref):
    word = word_ref[...]
    code = jnp.concatenate([(word << 16) >> 16, word >> 16], axis=0).astype(jnp.float32)
    return code[:, :-LANES] * jnp.exp2(code[:, -LANES:-LANES + 1] - 15.0)


def first_kernel(stride, keep_ref, got_ref, total_ref, there_ref, here_ref, again_ref):
    size = total_ref.shape[0]
    digit = lax.rem(lax.axis_index("feat") // stride, 2)

    def piece(at):
        span = pl.ds(pl.multiple_of(at * size, size), size)
        return keep_ref[span, :] + got_ref[span, :]

    total_ref[...] = piece(digit)
    encode(piece(1 - digit), there_ref)
    again_ref[...] = there_ref[...]
    encode(piece(digit), here_ref)


def square_kernel(total_ref, both_ref, x_ref, z_ref, sum_ref, out_ref):
    total = (total_ref[...] + decode(x_ref)) + (decode(z_ref) + decode(both_ref))
    sum_ref[...] = total
    encode(total, out_ref)


def middle_kernel(total_ref, word_ref, sum_ref, out_ref):
    total = total_ref[...] + decode(word_ref)
    sum_ref[...] = total
    encode(total, out_ref)


def last_kernel(scale, total_ref, word_ref, label_ref, row_ref):
    total = total_ref[...] + decode(word_ref)
    kept = total.shape[1]
    row_ref[:, :kept] = (total * scale).astype(jnp.bfloat16)
    row_ref[:, kept:] = label_ref[...]


def local_call(kernel, name, *operands, out_shape):
    return pl.pallas_call(
        kernel,
        out_shape=out_shape,
        compiler_params=pltpu.CompilerParams(vmem_limit_bytes=VMEM_LIMIT),
        name=name,
    )(*operands)


def swap(array, tok=0, feat=0):
    tok_count, feat_count = lax.axis_size("tok"), lax.axis_size("feat")
    pairs = [
        (f * tok_count + t, (f ^ feat) * tok_count + (t ^ tok))
        for f in range(feat_count)
        for t in range(tok_count)
    ]
    return lax.ppermute(array, ("feat", "tok"), pairs)


def body(features, signs, columns, labels):
    rows, width = features.shape
    feat_count = lax.axis_size("feat")
    feat_index = lax.axis_index("feat")
    tok_count = lax.axis_size("tok")
    kept = columns.shape[0]
    shard = kept // feat_count
    size = rows // 4
    total_type = jax.ShapeDtypeStruct((size, kept), jnp.float32)
    word_type = jax.ShapeDtypeStruct((size // 2, kept + LANES), jnp.int32)
    row_type = jax.ShapeDtypeStruct((size, kept + LANES), jnp.bfloat16)

    first = (feat_index & 1) * (rows // 2) + (feat_index >> 1 & 1) * size
    own_labels = lax.dynamic_slice_in_dim(labels, first, size, 0).astype(jnp.bfloat16)
    own_labels = jnp.broadcast_to(own_labels, (size, LANES))

    send, keep = partial_halves(features, signs, columns, feat_count)
    got = swap(send, feat=1)
    total, there, here, again = local_call(
        functools.partial(first_kernel, 2), "first_split", keep, got, out_shape=[total_type, word_type, word_type, word_type]
    )
    total, word = local_call(
        square_kernel,
        "add_square",
        total,
        swap(again, feat=6),
        swap(there, feat=2),
        swap(here, feat=4),
        out_shape=[total_type, word_type],
    )
    word = swap(word, feat=8)
    stride = 16
    while stride < feat_count:
        total, word = local_call(
            middle_kernel, "add_encode", total, word, out_shape=[total_type, word_type]
        )
        word = swap(word, feat=stride)
        stride *= 2
    scale = 1.0 / math.sqrt(width * feat_count)
    ours = local_call(
        functools.partial(last_kernel, scale), "sketch_rows", total, word, own_labels, out_shape=row_type
    )

    stride = 2
    while stride < tok_count:
        ours = jnp.concatenate([ours, swap(ours, tok=stride)], axis=0)
        stride *= 2
    received = [swap(ours, tok=1, feat=2)] if tok_count > 1 else []
    received += [swap(ours, feat=2)]
    received += [swap(ours, tok=1)] if tok_count > 1 else []
    ours = jnp.concatenate([ours] + received, axis=0)
    theirs = swap(ours, feat=1)
    concepts = C // tok_count
    gram = gram_blocks(ours, theirs, concepts, shard, kept, C / (rows * tok_count))
    return gram.reshape(concepts, shard, kept)


def solution(mesh):
    in_specs = (P("tok", "feat"), P("feat"), P(), P("tok", None))
    out_specs = P("tok", "feat", None)
    return jax.shard_map(body, mesh=mesh, in_specs=in_specs, out_specs=out_specs, check_vma=False)
```

```python
import functools
import math

import jax
import jax.numpy as jnp
from jax import lax
from jax.experimental import pallas as pl
from jax.experimental.pallas import tpu as pltpu
from jax.sharding import PartitionSpec as P

C = 32
LOW = 256
LANES = 128
VMEM_LIMIT = 48 * 1024 * 1024


def parity_sign(number, bit_count):
    shift = 1
    while shift < bit_count:
        shift *= 2
    while shift > 1:
        shift //= 2
        number = number ^ (number >> shift)
    return (1 - 2 * (number & 1)).astype(jnp.float32)


def add_products(x_ref, sign_ref, low, high, out_ref, part, wide):
    rows, kept = out_ref.shape
    blocks = wide // LOW
    stack = []
    for block in range(part * blocks, (part + 1) * blocks):
        cols = slice(block * LOW, (block + 1) * LOW)
        stack.append(x_ref[:, cols] * sign_ref[:, cols].astype(jnp.bfloat16))
    stack = jnp.concatenate(stack, axis=0)
    for group in range(kept // LOW):
        cols = slice(group * LOW, (group + 1) * LOW)
        products = jnp.dot(stack, low[:, cols], preferred_element_type=jnp.float32)
        total = None
        for at in range(blocks):
            row = part * blocks + at
            term = products[at * rows:(at + 1) * rows] * high[row:row + 1, cols]
            total = term if total is None else total + term
        if part > 0:
            total = total + out_ref[:, cols]
        out_ref[:, cols] = total


def send_kernel(total_bits, parts, x_hbm, s_hbm, col_hbm, send_ref, x_keep, signs, low, high, x_buf, col_buf, sems):
    half, kept = send_ref.shape
    wide = x_hbm.shape[1] // parts
    me = lax.axis_index("feat")
    mine = lax.rem(me, 2)
    col_copy = pltpu.make_async_copy(col_hbm, col_buf, sems.at[parts])
    sign_copy = pltpu.make_async_copy(s_hbm, signs, sems.at[parts + 1])
    col_copy.start()
    sign_copy.start()
    copies = []
    for part in range(parts):
        cols = pl.ds(part * wide, wide)
        rows = pl.ds(pl.multiple_of((1 - mine) * half, half), half)
        copies.append(pltpu.make_async_copy(x_hbm.at[rows, cols], x_buf.at[:, cols], sems.at[part]))
        copies[-1].start()
    rows = pl.ds(pl.multiple_of(mine * half, half), half)
    keep_copy = pltpu.make_async_copy(x_hbm.at[rows, :], x_keep, sems.at[parts + 2])
    keep_copy.start()
    col_copy.wait()
    col = col_buf[...]
    index = lax.broadcasted_iota(jnp.int32, (16, kept), 0)
    inner = parity_sign(index & col, 4)
    outer = parity_sign(index & (col >> 4), 4)
    for row in range(LOW // 16):
        low[row * 16:(row + 1) * 16] = (inner * outer[row:row + 1]).astype(jnp.bfloat16)
    high_index = lax.broadcasted_iota(jnp.int32, high.shape, 0) + me * high.shape[0]
    high[...] = parity_sign(high_index & (col >> 8), total_bits - 8)
    sign_copy.wait()
    for part in range(parts):
        copies[part].wait()
        add_products(x_buf, signs, low, high, send_ref, part, wide)
    keep_copy.wait()


def keep_kernel(parts, x_keep, signs, low, high, keep_ref):
    wide = x_keep.shape[1] // parts
    for part in range(parts):
        add_products(x_keep, signs, low, high, keep_ref, part, wide)


def partial_halves(features, signs, columns, feat_count):
    rows, width = features.shape
    kept = columns.shape[0]
    parts = max(1, width // 2048)
    half = rows // 2
    total_bits = (width * feat_count).bit_length() - 1
    params = pltpu.CompilerParams(vmem_limit_bytes=VMEM_LIMIT)
    cost = pl.CostEstimate(
        flops=2 * half * width * kept, bytes_accessed=2 * rows * width + 4 * half * kept, transcendentals=0
    )
    total_type = jax.ShapeDtypeStruct((half, kept), jnp.float32)
    send, *held = pl.pallas_call(
        functools.partial(send_kernel, total_bits, parts),
        in_specs=[pl.BlockSpec(memory_space=pltpu.HBM)] * 3,
        out_specs=[pl.BlockSpec(memory_space=pltpu.VMEM)] * 5,
        out_shape=[
            total_type,
            jax.ShapeDtypeStruct((half, width), jnp.bfloat16),
            jax.ShapeDtypeStruct((1, width), jnp.int32),
            jax.ShapeDtypeStruct((LOW, kept), jnp.bfloat16),
            jax.ShapeDtypeStruct((width // LOW, kept), jnp.float32),
        ],
        scratch_shapes=[
            pltpu.VMEM((half, width), jnp.bfloat16),
            pltpu.VMEM((1, kept), jnp.int32),
            pltpu.SemaphoreType.DMA((parts + 3,)),
        ],
        compiler_params=params,
        cost_estimate=cost,
        name="partial_sent",
    )(*(
        pltpu.with_memory_space_constraint(operand, pltpu.HBM)
        for operand in (features, signs.reshape(1, width), columns.reshape(1, kept))
    ))
    got = swap(send, feat=1)
    keep = pl.pallas_call(
        functools.partial(keep_kernel, parts),
        out_shape=total_type,
        compiler_params=params,
        cost_estimate=cost,
        name="partial_kept",
    )(*held)
    return keep, got


def mask_operands(shard, wide, factor, row_ref):
    kept = row_ref.shape[1] - LANES
    first = lax.axis_index("feat") * shard
    start = pl.multiple_of(first // LANES * LANES, LANES)
    window = row_ref[:, pl.ds(start, LANES)].astype(jnp.float32) * factor
    window = pltpu.roll(window, lax.rem(LANES - (first - start), LANES), 1)
    lane = lax.broadcasted_iota(jnp.int32, window.shape, 1)
    own = jnp.where(lane < shard, window, 0.0)
    step = shard
    while step < LANES:
        own = own + pltpu.roll(own, step, 1)
        step *= 2
    own = jnp.concatenate([own] * -(-wide // LANES), axis=1)[:, :wide]
    named = row_ref[:, kept:kept + 1].astype(jnp.float32).astype(jnp.int32)
    label = named - lax.broadcasted_iota(jnp.int32, own.shape, 1) // shard
    return own.T, label.T


def mask_kernel(shard, wide, factor, row_ref, own_ref, label_ref):
    own_ref[...], label_ref[...] = mask_operands(shard, wide, factor, row_ref)


def gram_kernel(shard, group, factor, ours, own_ref, label_ref, theirs, out_hbm, rows, chosen, blocks, sems):
    kept = rows.shape[1]
    half = ours.shape[0]
    wide = group * shard
    steps = chosen.shape[0] // wide
    chunks = blocks.shape[0]
    rows[:half] = ours[:, :kept]
    rows[half:] = theirs[:, :kept]
    parts = ((own_ref[...], label_ref[...]), mask_operands(shard, wide, factor, theirs))
    base = lax.axis_index("tok") * steps * group
    for step in range(steps):
        for at, (own, label) in enumerate(parts):
            masked = jnp.where(label == base + step * group, own, 0.0).astype(jnp.bfloat16)
            chosen[step * wide:(step + 1) * wide, at * half:(at + 1) * half] = masked
    copies = []
    size = kept // chunks
    for chunk in range(chunks):
        cols = slice(chunk * size, (chunk + 1) * size)
        blocks[chunk] = jnp.dot(chosen[...], rows[:, cols], preferred_element_type=jnp.float32)
        copies.append(
            pltpu.make_async_copy(blocks.at[chunk], out_hbm.at[:, pl.ds(chunk * size, size)], sems.at[chunk])
        )
        copies[-1].start()
    for copy in copies:
        copy.wait()


def gram_blocks(ours, theirs, concepts, shard, kept, factor):
    tokens = ours.shape[0]
    group = max(1, min(concepts, LOW // shard))
    wide = group * shard
    chunks = kept // LOW
    params = pltpu.CompilerParams(vmem_limit_bytes=VMEM_LIMIT)
    own, label = pl.pallas_call(
        functools.partial(mask_kernel, shard, wide, factor),
        out_shape=[jax.ShapeDtypeStruct((wide, tokens), dtype) for dtype in (jnp.float32, jnp.int32)],
        compiler_params=params,
        name="mask_ours",
    )(ours)
    return pl.pallas_call(
        functools.partial(gram_kernel, shard, group, factor),
        in_specs=[pl.BlockSpec(memory_space=pltpu.VMEM)] * 4,
        out_specs=pl.BlockSpec(memory_space=pltpu.HBM),
        out_shape=jax.ShapeDtypeStruct((concepts * shard, kept), jnp.float32),
        scratch_shapes=[
            pltpu.VMEM((2 * tokens, kept), jnp.bfloat16),
            pltpu.VMEM((concepts * shard, 2 * tokens), jnp.bfloat16),
            pltpu.VMEM((chunks, concepts * shard, LOW), jnp.float32),
            pltpu.SemaphoreType.DMA((chunks,)),
        ],
        compiler_params=params,
        cost_estimate=pl.CostEstimate(
            flops=4 * tokens * concepts * shard * kept, bytes_accessed=4 * concepts * shard * kept, transcendentals=0
        ),
        name="gram",
    )(ours, own, label, theirs)


def encode(values, word_ref):
    kept = values.shape[1]
    half = values.shape[0] // 2
    top = jnp.max(jnp.abs(values), axis=1, keepdims=True)
    power = jnp.ceil(jnp.log2(jnp.maximum(top, 2.0 ** -100)))
    whole = jnp.round(values * jnp.exp2(15.0 - power))
    whole = jnp.clip(whole, -32767.0, 32767.0).astype(jnp.int32)
    power = jnp.broadcast_to(power, (values.shape[0], LANES)).astype(jnp.int32)
    for cols, code in ((slice(0, kept), whole), (slice(kept, kept + LANES), power)):
        word_ref[:, cols] = (code[:half] & 0xFFFF) | (code[half:] << 16)


def decode(word_ref):
    word = word_ref[...]
    code = jnp.concatenate([(word << 16) >> 16, word >> 16], axis=0).astype(jnp.float32)
    return code[:, :-LANES] * jnp.exp2(code[:, -LANES:-LANES + 1] - 15.0)


def first_kernel(stride, keep_ref, got_ref, total_ref, there_ref, here_ref, again_ref):
    size = total_ref.shape[0]
    digit = lax.rem(lax.axis_index("feat") // stride, 2)

    def piece(at):
        span = pl.ds(pl.multiple_of(at * size, size), size)
        return keep_ref[span, :] + got_ref[span, :]

    total_ref[...] = piece(digit)
    encode(piece(1 - digit), there_ref)
    again_ref[...] = there_ref[...]
    encode(piece(digit), here_ref)


def square_kernel(total_ref, both_ref, x_ref, z_ref, sum_ref, out_ref):
    total = (total_ref[...] + decode(x_ref)) + (decode(z_ref) + decode(both_ref))
    sum_ref[...] = total
    encode(total, out_ref)


def middle_kernel(total_ref, word_ref, sum_ref, out_ref):
    total = total_ref[...] + decode(word_ref)
    sum_ref[...] = total
    encode(total, out_ref)


def last_kernel(scale, total_ref, word_ref, label_ref, *row_refs):
    total = total_ref[...] + decode(word_ref)
    kept = total.shape[1]
    row = (total * scale).astype(jnp.bfloat16)
    for row_ref in row_refs:
        row_ref[:, :kept] = row
        row_ref[:, kept:] = label_ref[...]


def local_call(kernel, name, *operands, out_shape):
    return pl.pallas_call(
        kernel,
        out_shape=out_shape,
        compiler_params=pltpu.CompilerParams(vmem_limit_bytes=VMEM_LIMIT),
        name=name,
    )(*operands)


def swap(array, tok=0, feat=0):
    tok_count, feat_count = lax.axis_size("tok"), lax.axis_size("feat")
    pairs = [
        (f * tok_count + t, (f ^ feat) * tok_count + (t ^ tok))
        for f in range(feat_count)
        for t in range(tok_count)
    ]
    return lax.ppermute(array, ("feat", "tok"), pairs)


def body(features, signs, columns, labels):
    rows, width = features.shape
    feat_count = lax.axis_size("feat")
    feat_index = lax.axis_index("feat")
    tok_count = lax.axis_size("tok")
    kept = columns.shape[0]
    shard = kept // feat_count
    size = rows // 4
    total_type = jax.ShapeDtypeStruct((size, kept), jnp.float32)
    word_type = jax.ShapeDtypeStruct((size // 2, kept + LANES), jnp.int32)
    row_type = jax.ShapeDtypeStruct((size, kept + LANES), jnp.bfloat16)

    first = (feat_index & 1) * (rows // 2) + (feat_index >> 1 & 1) * size
    own_labels = lax.dynamic_slice_in_dim(labels, first, size, 0).astype(jnp.bfloat16)
    own_labels = jnp.broadcast_to(own_labels, (size, LANES))

    keep, got = partial_halves(features, signs, columns, feat_count)
    total, there, here, again = local_call(
        functools.partial(first_kernel, 2), "first_split", keep, got, out_shape=[total_type, word_type, word_type, word_type]
    )
    total, word = local_call(
        square_kernel,
        "add_square",
        total,
        swap(again, feat=6),
        swap(there, feat=2),
        swap(here, feat=4),
        out_shape=[total_type, word_type],
    )
    word = swap(word, feat=8)
    stride = 16
    while stride < feat_count:
        total, word = local_call(
            middle_kernel, "add_encode", total, word, out_shape=[total_type, word_type]
        )
        word = swap(word, feat=stride)
        stride *= 2
    scale = 1.0 / math.sqrt(width * feat_count)
    copies = local_call(
        functools.partial(last_kernel, scale), "sketch_rows", total, word, own_labels, out_shape=[row_type] * 3
    )

    stride = 2
    while stride < tok_count:
        copies = [jnp.concatenate([copies[0], swap(copies[0], tok=stride)], axis=0)] * 3
        stride *= 2
    received = [swap(copies[0], tok=1, feat=2)] if tok_count > 1 else []
    received += [swap(copies[1], feat=2)]
    received += [swap(copies[2], tok=1)] if tok_count > 1 else []
    ours = jnp.concatenate([copies[0]] + received, axis=0)
    theirs = swap(ours, feat=1)
    concepts = C // tok_count
    gram = gram_blocks(ours, theirs, concepts, shard, kept, C / (rows * tok_count))
    return gram.reshape(concepts, shard, kept)


def solution(mesh):
    in_specs = (P("tok", "feat"), P("feat"), P(), P("tok", None))
    out_specs = P("tok", "feat", None)
    return jax.shard_map(body, mesh=mesh, in_specs=in_specs, out_specs=out_specs, check_vma=False)
```

```python
import functools
import math

import jax
import jax.numpy as jnp
from jax import lax
from jax.experimental import pallas as pl
from jax.experimental.pallas import tpu as pltpu
from jax.sharding import PartitionSpec as P

C = 32
LOW = 256
LANES = 128
VMEM_LIMIT = 48 * 1024 * 1024


def parity_sign(number, bit_count):
    shift = 1
    while shift < bit_count:
        shift *= 2
    while shift > 1:
        shift //= 2
        number = number ^ (number >> shift)
    return (1 - 2 * (number & 1)).astype(jnp.float32)


def add_products(x_ref, sign_ref, low, high, out_ref, part, wide):
    rows, kept = out_ref.shape
    blocks = wide // LOW
    stack = []
    for block in range(part * blocks, (part + 1) * blocks):
        cols = slice(block * LOW, (block + 1) * LOW)
        stack.append(x_ref[:, cols] * sign_ref[:, cols].astype(jnp.bfloat16))
    stack = jnp.concatenate(stack, axis=0)
    for group in range(kept // LOW):
        cols = slice(group * LOW, (group + 1) * LOW)
        products = jnp.dot(stack, low[:, cols], preferred_element_type=jnp.float32)
        total = None
        for at in range(blocks):
            row = part * blocks + at
            term = products[at * rows:(at + 1) * rows] * high[row:row + 1, cols]
            total = term if total is None else total + term
        if part > 0:
            total = total + out_ref[:, cols]
        out_ref[:, cols] = total


def send_kernel(total_bits, parts, x_hbm, s_hbm, col_hbm, send_ref, x_keep, signs, low, high, x_buf, col_buf, sems):
    half, kept = send_ref.shape
    wide = x_hbm.shape[1] // parts
    me = lax.axis_index("feat")
    mine = lax.rem(me, 2)
    col_copy = pltpu.make_async_copy(col_hbm, col_buf, sems.at[parts])
    sign_copy = pltpu.make_async_copy(s_hbm, signs, sems.at[parts + 1])
    col_copy.start()
    sign_copy.start()
    copies = []
    for part in range(parts):
        cols = pl.ds(part * wide, wide)
        rows = pl.ds(pl.multiple_of((1 - mine) * half, half), half)
        copies.append(pltpu.make_async_copy(x_hbm.at[rows, cols], x_buf.at[:, cols], sems.at[part]))
        copies[-1].start()
    rows = pl.ds(pl.multiple_of(mine * half, half), half)
    keep_copy = pltpu.make_async_copy(x_hbm.at[rows, :], x_keep, sems.at[parts + 2])
    keep_copy.start()
    col_copy.wait()
    col = col_buf[...]
    index = lax.broadcasted_iota(jnp.int32, (16, kept), 0)
    inner = parity_sign(index & col, 4)
    outer = parity_sign(index & (col >> 4), 4)
    for row in range(LOW // 16):
        low[row * 16:(row + 1) * 16] = (inner * outer[row:row + 1]).astype(jnp.bfloat16)
    high_index = lax.broadcasted_iota(jnp.int32, high.shape, 0) + me * high.shape[0]
    high[...] = parity_sign(high_index & (col >> 8), total_bits - 8)
    sign_copy.wait()
    for part in range(parts):
        copies[part].wait()
        add_products(x_buf, signs, low, high, send_ref, part, wide)
    keep_copy.wait()


def keep_kernel(parts, x_keep, signs, low, high, keep_ref):
    wide = x_keep.shape[1] // parts
    for part in range(parts):
        add_products(x_keep, signs, low, high, keep_ref, part, wide)


def partial_halves(features, signs, columns, feat_count):
    rows, width = features.shape
    kept = columns.shape[0]
    parts = max(1, width // 2048)
    half = rows // 2
    total_bits = (width * feat_count).bit_length() - 1
    params = pltpu.CompilerParams(vmem_limit_bytes=VMEM_LIMIT)
    cost = pl.CostEstimate(
        flops=2 * half * width * kept, bytes_accessed=2 * rows * width + 4 * half * kept, transcendentals=0
    )
    total_type = jax.ShapeDtypeStruct((half, kept), jnp.float32)
    send, *held = pl.pallas_call(
        functools.partial(send_kernel, total_bits, parts),
        in_specs=[pl.BlockSpec(memory_space=pltpu.HBM)] * 3,
        out_specs=[pl.BlockSpec(memory_space=pltpu.VMEM)] * 5,
        out_shape=[
            total_type,
            jax.ShapeDtypeStruct((half, width), jnp.bfloat16),
            jax.ShapeDtypeStruct((1, width), jnp.int32),
            jax.ShapeDtypeStruct((LOW, kept), jnp.bfloat16),
            jax.ShapeDtypeStruct((width // LOW, kept), jnp.float32),
        ],
        scratch_shapes=[
            pltpu.VMEM((half, width), jnp.bfloat16),
            pltpu.VMEM((1, kept), jnp.int32),
            pltpu.SemaphoreType.DMA((parts + 3,)),
        ],
        compiler_params=params,
        cost_estimate=cost,
        name="partial_sent",
    )(*(
        pltpu.with_memory_space_constraint(operand, pltpu.HBM)
        for operand in (features, signs.reshape(1, width), columns.reshape(1, kept))
    ))
    got = swap(send, feat=1)
    keep = pl.pallas_call(
        functools.partial(keep_kernel, parts),
        out_shape=total_type,
        compiler_params=params,
        cost_estimate=cost,
        name="partial_kept",
    )(*held)
    return keep, got


def gram_kernel(shard, group, factor, label_ref, *refs):
    pieces, (out_hbm, rows, blocks, sems) = refs[:-4], refs[-4:]
    steps, wide, _ = blocks.shape
    place = 0
    for piece in pieces:
        rows[place:place + piece.shape[0]] = piece[...]
        place += piece.shape[0]
    first = lax.axis_index("feat") * shard
    start = pl.multiple_of(first // LANES * LANES, LANES)
    window = rows[:, pl.ds(start, LANES)].astype(jnp.float32) * factor
    window = pltpu.roll(window, lax.rem(LANES - (first - start), LANES), 1)
    own = jnp.concatenate([window.T[:shard]] * group, axis=0)
    label = label_ref[...] - lax.broadcasted_iota(jnp.int32, own.shape, 0) // shard
    base = lax.axis_index("tok") * steps * group
    copies = []
    for step in range(steps):
        chosen = jnp.where(label == base + step * group, own, 0.0).astype(jnp.bfloat16)
        blocks[step] = jnp.dot(chosen, rows[...], preferred_element_type=jnp.float32)
        copies.append(
            pltpu.make_async_copy(blocks.at[step], out_hbm.at[pl.ds(step * wide, wide), :], sems.at[step])
        )
        copies[-1].start()
    for copy in copies:
        copy.wait()


def gram_blocks(pieces, label_row, concepts, shard, factor):
    tokens = sum(piece.shape[0] for piece in pieces)
    kept = pieces[0].shape[1]
    group = max(1, min(concepts, LOW // shard))
    wide = group * shard
    steps = concepts // group
    return pl.pallas_call(
        functools.partial(gram_kernel, shard, group, factor),
        in_specs=[pl.BlockSpec(memory_space=pltpu.VMEM)] * (1 + len(pieces)),
        out_specs=pl.BlockSpec(memory_space=pltpu.HBM),
        out_shape=jax.ShapeDtypeStruct((concepts * shard, kept), jnp.float32),
        scratch_shapes=[
            pltpu.VMEM((tokens, kept), jnp.bfloat16),
            pltpu.VMEM((steps, wide, kept), jnp.float32),
            pltpu.SemaphoreType.DMA((steps,)),
        ],
        compiler_params=pltpu.CompilerParams(vmem_limit_bytes=VMEM_LIMIT),
        cost_estimate=pl.CostEstimate(
            flops=2 * tokens * concepts * shard * kept, bytes_accessed=4 * concepts * shard * kept, transcendentals=0
        ),
        name="gram",
    )(label_row, *pieces)


def encode(values, word_ref):
    size, kept = values.shape
    half = size // 2
    top = jnp.max(jnp.abs(values), axis=1, keepdims=True)
    power = jnp.ceil(jnp.log2(jnp.maximum(top, 2.0 ** -100)))
    whole = jnp.round(values * jnp.exp2(15.0 - power))
    whole = jnp.clip(whole, -32767.0, 32767.0).astype(jnp.int32)
    word = (whole[:half] & 0xFFFF) | (whole[half:] << 16)
    for column in range(kept // LANES):
        word_ref[column * half:(column + 1) * half] = word[:, column * LANES:(column + 1) * LANES]
    group = lax.broadcasted_iota(jnp.int32, (8, LANES), 1) // (LANES * 8 // size)
    tile = jnp.zeros((8, LANES), jnp.int32)
    for at in range(size // 8):
        tile = jnp.where(group == at, power[at * 8:(at + 1) * 8].astype(jnp.int32), tile)
    word_ref[kept // LANES * half:] = tile


def decode(word_ref, size):
    half = size // 2
    columns = word_ref.shape[0] // half
    word = jnp.concatenate([word_ref[at * half:(at + 1) * half] for at in range(columns)], axis=1)
    code = jnp.concatenate([(word << 16) >> 16, word >> 16], axis=0).astype(jnp.float32)
    tile = jnp.exp2(word_ref[columns * half:].astype(jnp.float32) - 15.0)
    lanes = LANES * 8 // size
    scale = jnp.concatenate([tile[:, at * lanes:at * lanes + 1] for at in range(size // 8)], axis=0)
    return code * scale


def first_kernel(stride, keep_ref, got_ref, label_ref, total_ref, there_ref, here_ref, again_ref, label_out):
    size = total_ref.shape[0]
    digit = lax.rem(lax.axis_index("feat") // stride, 2)

    def piece(at):
        span = pl.ds(pl.multiple_of(at * size, size), size)
        return keep_ref[span, :] + got_ref[span, :]

    encode(piece(1 - digit), there_ref)
    again_ref[...] = there_ref[...]
    total = piece(digit)
    total_ref[...] = total
    encode(total, here_ref)
    label_out[...] = label_ref[...]


def square_kernel(total_ref, both_ref, x_ref, z_ref, sum_ref, out_ref):
    size = total_ref.shape[0]
    total = (total_ref[...] + decode(x_ref, size)) + (decode(z_ref, size) + decode(both_ref, size))
    sum_ref[...] = total
    encode(total, out_ref)


def middle_kernel(total_ref, word_ref, sum_ref, out_ref):
    total = total_ref[...] + decode(word_ref, total_ref.shape[0])
    sum_ref[...] = total
    encode(total, out_ref)


def last_kernel(scale, blocks, total_ref, word_ref, *refs):
    label_refs, (label_out, *row_refs) = refs[:-5], refs[-5:]
    size = total_ref.shape[0]
    row = ((total_ref[...] + decode(word_ref, size)) * scale).astype(jnp.bfloat16)
    for row_ref in row_refs:
        row_ref[...] = row
    core = lax.rem(lax.axis_index("feat"), 2)
    digit = lax.rem(lax.axis_index("feat") // 2, 2)
    groups = LANES // size
    lane = lax.broadcasted_iota(jnp.int32, (8, LANES), 1)
    for place in range(0, 2 * len(blocks), groups):
        out = jnp.zeros((8, LANES), jnp.int32)
        for at in range(groups):
            half, (tok, x) = (place + at) // len(blocks), blocks[(place + at) % len(blocks)]
            source = (core ^ half) * 2 * size + (digit ^ x) * size
            moved = pltpu.roll(
                jnp.broadcast_to(label_refs[tok][...], out.shape), lax.rem(at * size - source + LANES, LANES), 1
            )
            out = jnp.where(lane // size == at, moved, out)
        label_out[:, place * size:(place + groups) * size] = out[:1]


def local_call(kernel, name, *operands, out_shape):
    return pl.pallas_call(
        kernel,
        out_shape=out_shape,
        compiler_params=pltpu.CompilerParams(vmem_limit_bytes=VMEM_LIMIT),
        name=name,
    )(*operands)


def swap(array, tok=0, feat=0):
    tok_count, feat_count = lax.axis_size("tok"), lax.axis_size("feat")
    pairs = [
        (f * tok_count + t, (f ^ feat) * tok_count + (t ^ tok))
        for f in range(feat_count)
        for t in range(tok_count)
    ]
    return lax.ppermute(array, ("feat", "tok"), pairs)


def body(features, signs, columns, labels):
    rows, width = features.shape
    feat_count = lax.axis_size("feat")
    feat_index = lax.axis_index("feat")
    tok_count = lax.axis_size("tok")
    kept = columns.shape[0]
    shard = kept // feat_count
    size = rows // 4
    total_type = jax.ShapeDtypeStruct((size, kept), jnp.float32)
    word_type = jax.ShapeDtypeStruct((kept // LANES * (size // 2) + 8, LANES), jnp.int32)
    row_type = jax.ShapeDtypeStruct((size, kept), jnp.bfloat16)
    label_type = jax.ShapeDtypeStruct((1, rows), jnp.int32)

    keep, got = partial_halves(features, signs, columns, feat_count)
    total, there, here, again, label = local_call(
        functools.partial(first_kernel, 2),
        "first_split",
        keep,
        got,
        labels.reshape(1, rows),
        out_shape=[total_type, word_type, word_type, word_type, label_type],
    )
    both = swap(again, feat=6)
    x_word = swap(there, feat=2)
    z_word = swap(here, feat=4)
    all_labels = [label] + [swap(label, tok=tok) for tok in range(1, tok_count)]
    total, word = local_call(
        square_kernel, "add_square", total, both, x_word, z_word, out_shape=[total_type, word_type]
    )
    word = swap(word, feat=8)
    stride = 16
    while stride < feat_count:
        total, word = local_call(middle_kernel, "add_encode", total, word, out_shape=[total_type, word_type])
        word = swap(word, feat=stride)
        stride *= 2

    blocks = [(0, 0)]
    stride = 2
    while stride < tok_count:
        blocks = blocks + [(tok ^ stride, x) for tok, x in blocks]
        stride *= 2
    blocks = [(tok ^ flip, x) for flip, x in ((0, 0), (1, 1), (0, 1), (1, 0)) for tok, _ in blocks]
    scale = 1.0 / math.sqrt(width * feat_count)
    label_row, *copies = local_call(
        functools.partial(last_kernel, scale, blocks),
        "sketch_rows",
        total,
        word,
        *all_labels,
        out_shape=[jax.ShapeDtypeStruct((1, 2 * len(blocks) * size), jnp.int32)] + [row_type] * 4,
    )
    stride = 2
    while stride < tok_count:
        copies = [jnp.concatenate([copies[0], swap(copies[0], tok=stride)], axis=0)] * 4
        stride *= 2
    received = [swap(copies[0], tok=1, feat=2), swap(copies[1], feat=2), swap(copies[2], tok=1)]
    ours = copies[3:] + received
    theirs = [swap(block, feat=1) for block in ours]
    concepts = C // tok_count
    gram = gram_blocks(ours + theirs, label_row, concepts, shard, C / (rows * tok_count))
    return gram.reshape(concepts, shard, kept)


def solution(mesh):
    in_specs = (P("tok", "feat"), P("feat"), P(), P("tok", None))
    out_specs = P("tok", "feat", None)
    return jax.shard_map(body, mesh=mesh, in_specs=in_specs, out_specs=out_specs, check_vma=False)
```

```python
import functools
import math

import jax
import jax.numpy as jnp
from jax import lax
from jax.experimental import pallas as pl
from jax.experimental.pallas import tpu as pltpu
from jax.sharding import PartitionSpec as P

C = 32
LOW = 256
LANES = 128
SPLIT = 4
VMEM_LIMIT = 48 * 1024 * 1024


def parity_sign(number, bit_count):
    shift = 1
    while shift < bit_count:
        shift *= 2
    while shift > 1:
        shift //= 2
        number = number ^ (number >> shift)
    return (1 - 2 * (number & 1)).astype(jnp.float32)


def add_products(x_ref, sign_ref, low, high, out_ref, part, wide):
    rows, kept = out_ref.shape
    blocks = wide // LOW
    stack = []
    for block in range(part * blocks, (part + 1) * blocks):
        cols = slice(block * LOW, (block + 1) * LOW)
        stack.append(x_ref[:, cols] * sign_ref[:, cols].astype(jnp.bfloat16))
    stack = jnp.concatenate(stack, axis=0)
    for group in range(kept // LOW):
        cols = slice(group * LOW, (group + 1) * LOW)
        products = jnp.dot(stack, low[:, cols], preferred_element_type=jnp.float32)
        total = None
        for at in range(blocks):
            row = part * blocks + at
            term = products[at * rows:(at + 1) * rows] * high[row:row + 1, cols]
            total = term if total is None else total + term
        if part > 0:
            total = total + out_ref[:, cols]
        out_ref[:, cols] = total


def send_kernel(total_bits, parts, x_hbm, s_hbm, col_hbm, send_ref, x_keep, signs, low, high, x_buf, col_buf, sems):
    half, kept = send_ref.shape
    wide = x_hbm.shape[1] // parts
    me = lax.axis_index("feat")
    mine = lax.rem(me, 2)
    col_copy = pltpu.make_async_copy(col_hbm, col_buf, sems.at[parts])
    sign_copy = pltpu.make_async_copy(s_hbm, signs, sems.at[parts + 1])
    col_copy.start()
    sign_copy.start()
    copies = []
    for part in range(parts):
        cols = pl.ds(part * wide, wide)
        rows = pl.ds(pl.multiple_of((1 - mine) * half, half), half)
        copies.append(pltpu.make_async_copy(x_hbm.at[rows, cols], x_buf.at[:, cols], sems.at[part]))
        copies[-1].start()
    rows = pl.ds(pl.multiple_of(mine * half, half), half)
    keep_copy = pltpu.make_async_copy(x_hbm.at[rows, :], x_keep, sems.at[parts + 2])
    col_copy.wait()
    col = col_buf[...]
    index = lax.broadcasted_iota(jnp.int32, (16, kept), 0)
    inner = parity_sign(index & col, 4)
    outer = parity_sign(index & (col >> 4), 4)
    for row in range(LOW // 16):
        low[row * 16:(row + 1) * 16] = (inner * outer[row:row + 1]).astype(jnp.bfloat16)
    high_index = lax.broadcasted_iota(jnp.int32, high.shape, 0) + me * high.shape[0]
    high[...] = parity_sign(high_index & (col >> 8), total_bits - 8)
    sign_copy.wait()
    for part in range(parts):
        copies[part].wait()
        if part == 0:
            keep_copy.start()
        add_products(x_buf, signs, low, high, send_ref, part, wide)
    keep_copy.wait()


def keep_kernel(parts, x_keep, signs, low, high, keep_ref):
    wide = x_keep.shape[1] // parts
    for part in range(parts):
        add_products(x_keep, signs, low, high, keep_ref, part, wide)


def partial_halves(features, signs, columns, feat_count):
    rows, width = features.shape
    kept = columns.shape[0]
    parts = max(1, width // 2048)
    half = rows // 2
    total_bits = (width * feat_count).bit_length() - 1
    params = pltpu.CompilerParams(vmem_limit_bytes=VMEM_LIMIT)
    cost = pl.CostEstimate(
        flops=2 * half * width * kept, bytes_accessed=2 * rows * width + 4 * half * kept, transcendentals=0
    )
    total_type = jax.ShapeDtypeStruct((half, kept), jnp.float32)
    send, *held = pl.pallas_call(
        functools.partial(send_kernel, total_bits, parts),
        in_specs=[pl.BlockSpec(memory_space=pltpu.HBM)] * 3,
        out_specs=[pl.BlockSpec(memory_space=pltpu.VMEM)] * 5,
        out_shape=[
            total_type,
            jax.ShapeDtypeStruct((half, width), jnp.bfloat16),
            jax.ShapeDtypeStruct((1, width), jnp.int32),
            jax.ShapeDtypeStruct((LOW, kept), jnp.bfloat16),
            jax.ShapeDtypeStruct((width // LOW, kept), jnp.float32),
        ],
        scratch_shapes=[
            pltpu.VMEM((half, width), jnp.bfloat16),
            pltpu.VMEM((1, kept), jnp.int32),
            pltpu.SemaphoreType.DMA((parts + 3,)),
        ],
        compiler_params=params,
        cost_estimate=cost,
        name="partial_sent",
    )(*(
        pltpu.with_memory_space_constraint(operand, pltpu.HBM)
        for operand in (features, signs.reshape(1, width), columns.reshape(1, kept))
    ))
    got = swap(send, feat=1)
    keep = pl.pallas_call(
        functools.partial(keep_kernel, parts),
        out_shape=total_type,
        compiler_params=params,
        cost_estimate=cost,
        name="partial_kept",
    )(*held)
    return keep, got


def gram_kernel(shard, group, factor, label_ref, *refs):
    pieces, (out_hbm, rows, blocks, sems) = refs[:-4], refs[-4:]
    steps, wide, _ = blocks.shape
    place = 0
    for piece in pieces:
        rows[place:place + piece.shape[0]] = piece[...]
        place += piece.shape[0]
    first = lax.axis_index("feat") * shard
    start = pl.multiple_of(first // LANES * LANES, LANES)
    window = rows[:, pl.ds(start, LANES)].astype(jnp.float32) * factor
    window = pltpu.roll(window, lax.rem(LANES - (first - start), LANES), 1)
    own = jnp.concatenate([window.T[:shard]] * group, axis=0)
    label = label_ref[...] - lax.broadcasted_iota(jnp.int32, own.shape, 0) // shard
    base = lax.axis_index("tok") * steps * group
    copies = []
    for step in range(steps):
        chosen = jnp.where(label == base + step * group, own, 0.0).astype(jnp.bfloat16)
        blocks[step] = jnp.dot(chosen, rows[...], preferred_element_type=jnp.float32)
        size = wide // SPLIT
        for at in range(SPLIT):
            copies.append(
                pltpu.make_async_copy(
                    blocks.at[step, pl.ds(at * size, size), :],
                    out_hbm.at[pl.ds(step * wide + at * size, size), :],
                    sems.at[step * SPLIT + at],
                )
            )
            copies[-1].start()
    for copy in copies:
        copy.wait()


def gram_blocks(pieces, label_row, concepts, shard, factor):
    tokens = sum(piece.shape[0] for piece in pieces)
    kept = pieces[0].shape[1]
    group = max(1, min(concepts, LOW // shard))
    wide = group * shard
    steps = concepts // group
    return pl.pallas_call(
        functools.partial(gram_kernel, shard, group, factor),
        in_specs=[pl.BlockSpec(memory_space=pltpu.VMEM)] * (1 + len(pieces)),
        out_specs=pl.BlockSpec(memory_space=pltpu.HBM),
        out_shape=jax.ShapeDtypeStruct((concepts * shard, kept), jnp.float32),
        scratch_shapes=[
            pltpu.VMEM((tokens, kept), jnp.bfloat16),
            pltpu.VMEM((steps, wide, kept), jnp.float32),
            pltpu.SemaphoreType.DMA((steps * SPLIT,)),
        ],
        compiler_params=pltpu.CompilerParams(vmem_limit_bytes=VMEM_LIMIT),
        cost_estimate=pl.CostEstimate(
            flops=2 * tokens * concepts * shard * kept, bytes_accessed=4 * concepts * shard * kept, transcendentals=0
        ),
        name="gram",
    )(label_row, *pieces)


def encode(values, word_ref):
    size, kept = values.shape
    half = size // 2
    top = jnp.max(jnp.abs(values), axis=1, keepdims=True)
    power = jnp.ceil(jnp.log2(jnp.maximum(top, 2.0 ** -100)))
    whole = jnp.round(values * jnp.exp2(15.0 - power))
    whole = jnp.clip(whole, -32767.0, 32767.0).astype(jnp.int32)
    word = (whole[:half] & 0xFFFF) | (whole[half:] << 16)
    for column in range(kept // LANES):
        word_ref[column * half:(column + 1) * half] = word[:, column * LANES:(column + 1) * LANES]
    group = lax.broadcasted_iota(jnp.int32, (8, LANES), 1) // (LANES * 8 // size)
    tile = jnp.zeros((8, LANES), jnp.int32)
    for at in range(size // 8):
        tile = jnp.where(group == at, power[at * 8:(at + 1) * 8].astype(jnp.int32), tile)
    word_ref[kept // LANES * half:] = tile


def decode(word_ref, size):
    half = size // 2
    columns = word_ref.shape[0] // half
    word = jnp.concatenate([word_ref[at * half:(at + 1) * half] for at in range(columns)], axis=1)
    code = jnp.concatenate([(word << 16) >> 16, word >> 16], axis=0).astype(jnp.float32)
    tile = jnp.exp2(word_ref[columns * half:].astype(jnp.float32) - 15.0)
    lanes = LANES * 8 // size
    scale = jnp.concatenate([tile[:, at * lanes:at * lanes + 1] for at in range(size // 8)], axis=0)
    return code * scale


def first_kernel(stride, keep_ref, got_ref, label_ref, total_ref, far_ref, even_ref, odd_ref, label_out):
    size = total_ref.shape[0]
    digit = lax.rem(lax.axis_index("feat") // stride, 2)

    def piece(at):
        span = pl.ds(pl.multiple_of(at * size, size), size)
        return keep_ref[span, :] + got_ref[span, :]

    encode(piece(1 - digit), far_ref)
    total = piece(digit)
    total_ref[...] = total
    core = lax.rem(lax.axis_index("feat"), 2)
    for this, there_ref, here_ref in ((0, even_ref, odd_ref), (1, odd_ref, even_ref)):
        @pl.when(core == this)
        def _():
            there_ref[...] = far_ref[...]
            encode(total, here_ref)

    label_out[...] = label_ref[...]


def square_kernel(total_ref, far_ref, even_ref, odd_ref, sum_ref, out_ref):
    size = total_ref.shape[0]
    total = (total_ref[...] + decode(far_ref, size)) + (decode(even_ref, size) + decode(odd_ref, size))
    sum_ref[...] = total
    encode(total, out_ref)


def middle_kernel(total_ref, word_ref, sum_ref, out_ref):
    total = total_ref[...] + decode(word_ref, total_ref.shape[0])
    sum_ref[...] = total
    encode(total, out_ref)


def last_kernel(scale, blocks, total_ref, word_ref, *refs):
    label_refs, (label_out, *row_refs) = refs[:-5], refs[-5:]
    size = total_ref.shape[0]
    row = ((total_ref[...] + decode(word_ref, size)) * scale).astype(jnp.bfloat16)
    for row_ref in row_refs:
        row_ref[...] = row
    core = lax.rem(lax.axis_index("feat"), 2)
    digit = lax.rem(lax.axis_index("feat") // 2, 2)
    groups = LANES // size
    lane = lax.broadcasted_iota(jnp.int32, (8, LANES), 1)
    for place in range(0, 2 * len(blocks), groups):
        out = jnp.zeros((8, LANES), jnp.int32)
        for at in range(groups):
            half = core ^ ((place + at) // len(blocks))
            for this, (tok, x) in enumerate(blocks[(place + at) % len(blocks)]):
                source = half * 2 * size + (digit ^ x) * size
                row = jnp.broadcast_to(label_refs[tok][...], out.shape)
                moved = pltpu.roll(row, lax.rem(at * size - source + LANES, LANES), 1)
                out = jnp.where((lane // size == at) & (half == this), moved, out)
        label_out[:, place * size:(place + groups) * size] = out[:1]


def local_call(kernel, name, *operands, out_shape):
    return pl.pallas_call(
        kernel,
        out_shape=out_shape,
        compiler_params=pltpu.CompilerParams(vmem_limit_bytes=VMEM_LIMIT),
        name=name,
    )(*operands)


def swap(array, tok=0, feat=0, odd=None):
    tok_count, feat_count = lax.axis_size("tok"), lax.axis_size("feat")
    bits = ((tok, feat), odd or (tok, feat))
    pairs = [
        (f * tok_count + t, (f ^ bits[f & 1][1]) * tok_count + (t ^ bits[f & 1][0]))
        for f in range(feat_count)
        for t in range(tok_count)
    ]
    return lax.ppermute(array, ("feat", "tok"), pairs)


def body(features, signs, columns, labels):
    rows, width = features.shape
    feat_count = lax.axis_size("feat")
    feat_index = lax.axis_index("feat")
    tok_count = lax.axis_size("tok")
    kept = columns.shape[0]
    shard = kept // feat_count
    size = rows // 4
    total_type = jax.ShapeDtypeStruct((size, kept), jnp.float32)
    word_type = jax.ShapeDtypeStruct((kept // LANES * (size // 2) + 8, LANES), jnp.int32)
    row_type = jax.ShapeDtypeStruct((size, kept), jnp.bfloat16)
    label_type = jax.ShapeDtypeStruct((1, rows), jnp.int32)

    keep, got = partial_halves(features, signs, columns, feat_count)
    total, far, even, odd, label = local_call(
        functools.partial(first_kernel, 2),
        "first_split",
        keep,
        got,
        labels.reshape(1, rows),
        out_shape=[total_type, word_type, word_type, word_type, label_type],
    )
    far = swap(far, feat=6)
    even = swap(even, feat=2, odd=(0, 4))
    odd = swap(odd, feat=4, odd=(0, 2))
    all_labels = [label] + [swap(label, tok=tok) for tok in range(1, tok_count)]
    total, word = local_call(
        square_kernel, "add_square", total, far, even, odd, out_shape=[total_type, word_type]
    )
    word = swap(word, feat=8)
    stride = 16
    while stride < feat_count:
        total, word = local_call(middle_kernel, "add_encode", total, word, out_shape=[total_type, word_type])
        word = swap(word, feat=stride)
        stride *= 2

    blocks = [(0, 0)]
    stride = 2
    while stride < tok_count:
        blocks = blocks + [(tok ^ stride, x) for tok, x in blocks]
        stride *= 2
    flips = (((0, 0), (1, 1), (0, 1), (1, 0)), ((0, 0), (1, 1), (1, 0), (0, 1)))
    blocks = [
        ((tok ^ even[0], even[1]), (tok ^ odd[0], odd[1])) for even, odd in zip(*flips) for tok, _ in blocks
    ]
    scale = 1.0 / math.sqrt(width * feat_count)
    label_row, *copies = local_call(
        functools.partial(last_kernel, scale, blocks),
        "sketch_rows",
        total,
        word,
        *all_labels,
        out_shape=[jax.ShapeDtypeStruct((1, 2 * len(blocks) * size), jnp.int32)] + [row_type] * 4,
    )
    stride = 2
    while stride < tok_count:
        copies = [jnp.concatenate([copies[0], swap(copies[0], tok=stride)], axis=0)] * 4
        stride *= 2
    received = [
        swap(copies[0], tok=1, feat=2),
        swap(copies[1], feat=2, odd=(1, 0)),
        swap(copies[2], tok=1, odd=(0, 2)),
    ]
    ours = copies[3:] + received
    theirs = [swap(block, feat=1) for block in ours]
    concepts = C // tok_count
    gram = gram_blocks(ours + theirs, label_row, concepts, shard, C / (rows * tok_count))
    return gram.reshape(concepts, shard, kept)


def solution(mesh):
    in_specs = (P("tok", "feat"), P("feat"), P(), P("tok", None))
    out_specs = P("tok", "feat", None)
    return jax.shard_map(body, mesh=mesh, in_specs=in_specs, out_specs=out_specs, check_vma=False)
```

```python
import functools
import math

import jax
import jax.numpy as jnp
from jax import lax
from jax.experimental import pallas as pl
from jax.experimental.pallas import tpu as pltpu
from jax.sharding import PartitionSpec as P

C = 32
LOW = 256
LANES = 128
DEPTH_BITS = 9
VMEM_LIMIT = 48 * 1024 * 1024


def parity_sign(number, bit_count):
    shift = 1
    while shift < bit_count:
        shift *= 2
    while shift > 1:
        shift //= 2
        number = number ^ (number >> shift)
    return (1 - 2 * (number & 1)).astype(jnp.float32)


def add_products(x_ref, sign_ref, low, high, out_ref, part, wide):
    rows, kept = out_ref.shape
    depth = low.shape[0]
    blocks = wide // depth
    stack = []
    for block in range(part * blocks, (part + 1) * blocks):
        cols = slice(block * depth, (block + 1) * depth)
        stack.append(x_ref[:, cols] * sign_ref[:, cols].astype(jnp.bfloat16))
    stack = jnp.concatenate(stack, axis=0)
    for group in range(kept // LOW):
        cols = slice(group * LOW, (group + 1) * LOW)
        products = jnp.dot(stack, low[:, cols], preferred_element_type=jnp.float32)
        total = None
        for at in range(blocks):
            row = part * blocks + at
            term = products[at * rows:(at + 1) * rows] * high[row:row + 1, cols]
            total = term if total is None else total + term
        if part > 0:
            total = total + out_ref[:, cols]
        out_ref[:, cols] = total


def send_kernel(total_bits, parts, x_hbm, s_hbm, col_hbm, send_ref, x_keep, signs, low, high, x_buf, col_buf, sems):
    half, kept = send_ref.shape
    wide = x_hbm.shape[1] // parts
    me = lax.axis_index("feat")
    mine = lax.rem(me, 2)
    col_copy = pltpu.make_async_copy(col_hbm, col_buf, sems.at[parts])
    sign_copy = pltpu.make_async_copy(s_hbm, signs, sems.at[parts + 1])
    col_copy.start()
    sign_copy.start()
    copies = []
    for part in range(parts):
        cols = pl.ds(part * wide, wide)
        rows = pl.ds(pl.multiple_of((1 - mine) * half, half), half)
        copies.append(pltpu.make_async_copy(x_hbm.at[rows, cols], x_buf.at[:, cols], sems.at[part]))
        copies[-1].start(priority=part % 2)
    rows = pl.ds(pl.multiple_of(mine * half, half), half)
    keep_copy = pltpu.make_async_copy(x_hbm.at[rows, :], x_keep, sems.at[parts + 2])
    keep_copy.start(priority=1)
    col_copy.wait()
    col = col_buf[...]
    index = lax.broadcasted_iota(jnp.int32, (16, kept), 0)
    inner = parity_sign(index & col, 4)
    index = lax.broadcasted_iota(jnp.int32, (low.shape[0] // 16, kept), 0)
    outer = parity_sign(index & (col >> 4), DEPTH_BITS - 4)
    for row in range(low.shape[0] // 16):
        low[row * 16:(row + 1) * 16] = (inner * outer[row:row + 1]).astype(jnp.bfloat16)
    high_index = lax.broadcasted_iota(jnp.int32, high.shape, 0) + me * high.shape[0]
    high[...] = parity_sign(high_index & (col >> DEPTH_BITS), total_bits - DEPTH_BITS)
    sign_copy.wait()
    for part in range(parts):
        copies[part].wait()
        add_products(x_buf, signs, low, high, send_ref, part, wide)
    keep_copy.wait()


def keep_kernel(parts, x_keep, signs, low, high, keep_ref):
    wide = x_keep.shape[1] // parts
    for part in range(parts):
        add_products(x_keep, signs, low, high, keep_ref, part, wide)


def partial_halves(features, signs, columns, feat_count):
    rows, width = features.shape
    kept = columns.shape[0]
    parts = max(1, width // 2048)
    half = rows // 2
    total_bits = (width * feat_count).bit_length() - 1
    params = pltpu.CompilerParams(vmem_limit_bytes=VMEM_LIMIT)
    cost = pl.CostEstimate(
        flops=2 * half * width * kept, bytes_accessed=2 * rows * width + 4 * half * kept, transcendentals=0
    )
    total_type = jax.ShapeDtypeStruct((half, kept), jnp.float32)
    send, *held = pl.pallas_call(
        functools.partial(send_kernel, total_bits, parts),
        in_specs=[pl.BlockSpec(memory_space=pltpu.HBM)] * 3,
        out_specs=[pl.BlockSpec(memory_space=pltpu.VMEM)] * 5,
        out_shape=[
            total_type,
            jax.ShapeDtypeStruct((half, width), jnp.bfloat16),
            jax.ShapeDtypeStruct((1, width), jnp.int32),
            jax.ShapeDtypeStruct((1 << DEPTH_BITS, kept), jnp.bfloat16),
            jax.ShapeDtypeStruct((width >> DEPTH_BITS, kept), jnp.float32),
        ],
        scratch_shapes=[
            pltpu.VMEM((half, width), jnp.bfloat16),
            pltpu.VMEM((1, kept), jnp.int32),
            pltpu.SemaphoreType.DMA((parts + 3,)),
        ],
        compiler_params=params,
        cost_estimate=cost,
        name="partial_sent",
    )(*(
        pltpu.with_memory_space_constraint(operand, pltpu.HBM)
        for operand in (features, signs.reshape(1, width), columns.reshape(1, kept))
    ))
    got = swap(send, feat=1)
    keep = pl.pallas_call(
        functools.partial(keep_kernel, parts),
        out_shape=total_type,
        compiler_params=params,
        cost_estimate=cost,
        name="partial_kept",
    )(*held)
    return keep, got


def gram_kernel(shard, group, factor, label_ref, *refs):
    pieces, (out_hbm, rows, blocks, sems) = refs[:-4], refs[-4:]
    steps, wide, _ = blocks.shape
    place = 0
    for piece in pieces:
        rows[place:place + piece.shape[0]] = piece[...]
        place += piece.shape[0]
    first = lax.axis_index("feat") * shard
    start = pl.multiple_of(first // LANES * LANES, LANES)
    window = rows[:, pl.ds(start, LANES)].astype(jnp.float32) * factor
    window = pltpu.roll(window, lax.rem(LANES - (first - start), LANES), 1)
    own = jnp.concatenate([window.T[:shard]] * group, axis=0)
    label = label_ref[...] - lax.broadcasted_iota(jnp.int32, own.shape, 0) // shard
    base = lax.axis_index("tok") * steps * group
    copies = []
    for step in range(steps):
        chosen = jnp.where(label == base + step * group, own, 0.0).astype(jnp.bfloat16)
        blocks[step] = jnp.dot(chosen, rows[...], preferred_element_type=jnp.float32)
        size = wide // 2
        for at in range(2):
            copies.append(
                pltpu.make_async_copy(
                    blocks.at[step, pl.ds(at * size, size), :],
                    out_hbm.at[pl.ds(step * wide + at * size, size), :],
                    sems.at[step * 2 + at],
                )
            )
            copies[-1].start(priority=at)
    for copy in copies:
        copy.wait()


def gram_blocks(pieces, label_row, concepts, shard, factor):
    tokens = sum(piece.shape[0] for piece in pieces)
    kept = pieces[0].shape[1]
    group = max(1, min(concepts, LOW // shard))
    wide = group * shard
    steps = concepts // group
    return pl.pallas_call(
        functools.partial(gram_kernel, shard, group, factor),
        in_specs=[pl.BlockSpec(memory_space=pltpu.VMEM)] * (1 + len(pieces)),
        out_specs=pl.BlockSpec(memory_space=pltpu.HBM),
        out_shape=jax.ShapeDtypeStruct((concepts * shard, kept), jnp.float32),
        scratch_shapes=[
            pltpu.VMEM((tokens, kept), jnp.bfloat16),
            pltpu.VMEM((steps, wide, kept), jnp.float32),
            pltpu.SemaphoreType.DMA((2 * steps,)),
        ],
        compiler_params=pltpu.CompilerParams(vmem_limit_bytes=VMEM_LIMIT),
        cost_estimate=pl.CostEstimate(
            flops=2 * tokens * concepts * shard * kept, bytes_accessed=4 * concepts * shard * kept, transcendentals=0
        ),
        name="gram",
    )(label_row, *pieces)


def encode(values, word_ref):
    size, kept = values.shape
    half = size // 2
    top = jnp.max(jnp.abs(values), axis=1, keepdims=True)
    power = jnp.ceil(jnp.log2(jnp.maximum(top, 2.0 ** -100)))
    whole = jnp.round(values * jnp.exp2(15.0 - power))
    whole = jnp.clip(whole, -32767.0, 32767.0).astype(jnp.int32)
    word = (whole[:half] & 0xFFFF) | (whole[half:] << 16)
    for column in range(kept // LANES):
        word_ref[column * half:(column + 1) * half] = word[:, column * LANES:(column + 1) * LANES]
    group = lax.broadcasted_iota(jnp.int32, (8, LANES), 1) // (LANES * 8 // size)
    tile = jnp.zeros((8, LANES), jnp.int32)
    for at in range(size // 8):
        tile = jnp.where(group == at, power[at * 8:(at + 1) * 8].astype(jnp.int32), tile)
    word_ref[kept // LANES * half:] = tile


def decode(word_ref, size):
    half = size // 2
    columns = word_ref.shape[0] // half
    word = jnp.concatenate([word_ref[at * half:(at + 1) * half] for at in range(columns)], axis=1)
    code = jnp.concatenate([(word << 16) >> 16, word >> 16], axis=0).astype(jnp.float32)
    tile = jnp.exp2(word_ref[columns * half:].astype(jnp.float32) - 15.0)
    lanes = LANES * 8 // size
    scale = jnp.concatenate([tile[:, at * lanes:at * lanes + 1] for at in range(size // 8)], axis=0)
    return code * scale


def first_kernel(stride, keep_ref, got_ref, label_ref, total_ref, there_ref, here_ref, again_ref, label_out):
    size = total_ref.shape[0]
    digit = lax.rem(lax.axis_index("feat") // stride, 2)

    def piece(at):
        span = pl.ds(pl.multiple_of(at * size, size), size)
        return keep_ref[span, :] + got_ref[span, :]

    encode(piece(1 - digit), there_ref)
    again_ref[...] = there_ref[...]
    total = piece(digit)
    total_ref[...] = total
    encode(total, here_ref)
    label_out[...] = label_ref[...]


def square_kernel(total_ref, both_ref, x_ref, z_ref, sum_ref, out_ref):
    size = total_ref.shape[0]
    total = (total_ref[...] + decode(x_ref, size)) + (decode(z_ref, size) + decode(both_ref, size))
    sum_ref[...] = total
    encode(total, out_ref)


def middle_kernel(total_ref, word_ref, sum_ref, out_ref):
    total = total_ref[...] + decode(word_ref, total_ref.shape[0])
    sum_ref[...] = total
    encode(total, out_ref)


def last_kernel(scale, blocks, total_ref, word_ref, *refs):
    label_refs, (label_out, *row_refs) = refs[:-5], refs[-5:]
    size = total_ref.shape[0]
    row = ((total_ref[...] + decode(word_ref, size)) * scale).astype(jnp.bfloat16)
    for row_ref in row_refs:
        row_ref[...] = row
    core = lax.rem(lax.axis_index("feat"), 2)
    digit = lax.rem(lax.axis_index("feat") // 2, 2)
    groups = LANES // size
    lane = lax.broadcasted_iota(jnp.int32, (8, LANES), 1)
    for place in range(0, 2 * len(blocks), groups):
        out = jnp.zeros((8, LANES), jnp.int32)
        for at in range(groups):
            half, (tok, x) = (place + at) // len(blocks), blocks[(place + at) % len(blocks)]
            source = (core ^ half) * 2 * size + (digit ^ x) * size
            moved = pltpu.roll(
                jnp.broadcast_to(label_refs[tok][...], out.shape), lax.rem(at * size - source + LANES, LANES), 1
            )
            out = jnp.where(lane // size == at, moved, out)
        label_out[:, place * size:(place + groups) * size] = out[:1]


def local_call(kernel, name, *operands, out_shape):
    return pl.pallas_call(
        kernel,
        out_shape=out_shape,
        compiler_params=pltpu.CompilerParams(vmem_limit_bytes=VMEM_LIMIT),
        name=name,
    )(*operands)


def swap(array, tok=0, feat=0, odd=None):
    tok_count, feat_count = lax.axis_size("tok"), lax.axis_size("feat")
    bits = (feat, odd or feat)
    pairs = [
        (f * tok_count + t, (f ^ bits[f & 1]) * tok_count + (t ^ tok))
        for f in range(feat_count)
        for t in range(tok_count)
    ]
    return lax.ppermute(array, ("feat", "tok"), pairs)


def body(features, signs, columns, labels):
    rows, width = features.shape
    feat_count = lax.axis_size("feat")
    feat_index = lax.axis_index("feat")
    tok_count = lax.axis_size("tok")
    kept = columns.shape[0]
    shard = kept // feat_count
    size = rows // 4
    total_type = jax.ShapeDtypeStruct((size, kept), jnp.float32)
    word_type = jax.ShapeDtypeStruct((kept // LANES * (size // 2) + 8, LANES), jnp.int32)
    row_type = jax.ShapeDtypeStruct((size, kept), jnp.bfloat16)
    label_type = jax.ShapeDtypeStruct((1, rows), jnp.int32)

    keep, got = partial_halves(features, signs, columns, feat_count)
    total, there, here, again, label = local_call(
        functools.partial(first_kernel, 2),
        "first_split",
        keep,
        got,
        labels.reshape(1, rows),
        out_shape=[total_type, word_type, word_type, word_type, label_type],
    )
    both = swap(again, feat=6, odd=10)
    x_word = swap(there, feat=2)
    z_word = swap(here, feat=4, odd=8)
    all_labels = [label] + [swap(label, tok=tok) for tok in range(1, tok_count)]
    total, word = local_call(
        square_kernel, "add_square", total, both, x_word, z_word, out_shape=[total_type, word_type]
    )
    word = swap(word, feat=8, odd=4)
    stride = 16
    while stride < feat_count:
        total, word = local_call(middle_kernel, "add_encode", total, word, out_shape=[total_type, word_type])
        word = swap(word, feat=stride)
        stride *= 2

    blocks = [(0, 0)]
    stride = 2
    while stride < tok_count:
        blocks = blocks + [(tok ^ stride, x) for tok, x in blocks]
        stride *= 2
    blocks = [(tok ^ flip, x) for flip, x in ((0, 0), (1, 1), (0, 1), (1, 0)) for tok, _ in blocks]
    scale = 1.0 / math.sqrt(width * feat_count)
    label_row, *copies = local_call(
        functools.partial(last_kernel, scale, blocks),
        "sketch_rows",
        total,
        word,
        *all_labels,
        out_shape=[jax.ShapeDtypeStruct((1, 2 * len(blocks) * size), jnp.int32)] + [row_type] * 4,
    )
    stride = 2
    while stride < tok_count:
        copies = [jnp.concatenate([copies[0], swap(copies[0], tok=stride)], axis=0)] * 4
        stride *= 2
    received = [swap(copies[0], tok=1, feat=2), swap(copies[1], feat=2), swap(copies[2], tok=1)]
    ours = copies[3:] + received
    theirs = [swap(block, feat=1) for block in ours]
    concepts = C // tok_count
    gram = gram_blocks(ours + theirs, label_row, concepts, shard, C / (rows * tok_count))
    return gram.reshape(concepts, shard, kept)


def solution(mesh):
    in_specs = (P("tok", "feat"), P("feat"), P(), P("tok", None))
    out_specs = P("tok", "feat", None)
    return jax.shard_map(body, mesh=mesh, in_specs=in_specs, out_specs=out_specs, check_vma=False)
```

```python
import functools
import math

import jax
import jax.numpy as jnp
from jax import lax
from jax.experimental import pallas as pl
from jax.experimental.pallas import tpu as pltpu
from jax.sharding import PartitionSpec as P

C = 32
LOW = 256
LANES = 128
VMEM_LIMIT = 48 * 1024 * 1024


def parity_sign(number, bit_count):
    shift = 1
    while shift < bit_count:
        shift *= 2
    while shift > 1:
        shift //= 2
        number = number ^ (number >> shift)
    return (1 - 2 * (number & 1)).astype(jnp.float32)


def add_products(x_ref, sign_ref, low, high, out_ref, part, wide):
    rows, kept = out_ref.shape
    blocks = wide // LOW
    stack = []
    for block in range(part * blocks, (part + 1) * blocks):
        cols = slice(block * LOW, (block + 1) * LOW)
        stack.append(x_ref[:, cols] * sign_ref[:, cols].astype(jnp.bfloat16))
    stack = jnp.concatenate(stack, axis=0)
    for group in range(kept // LOW):
        cols = slice(group * LOW, (group + 1) * LOW)
        products = jnp.dot(stack, low[:, cols], preferred_element_type=jnp.float32)
        total = None
        for at in range(blocks):
            row = part * blocks + at
            term = products[at * rows:(at + 1) * rows] * high[row:row + 1, cols]
            total = term if total is None else total + term
        if part > 0:
            total = total + out_ref[:, cols]
        out_ref[:, cols] = total


def send_kernel(total_bits, parts, x_hbm, s_hbm, col_hbm, send_ref, x_keep, signs, low, high, x_buf, col_buf, sems):
    half, kept = send_ref.shape
    wide = x_hbm.shape[1] // parts
    me = lax.axis_index("feat")
    mine = lax.rem(me, 2)
    col_copy = pltpu.make_async_copy(col_hbm, col_buf, sems.at[parts])
    sign_copy = pltpu.make_async_copy(s_hbm, signs, sems.at[parts + 1])
    col_copy.start()
    sign_copy.start()
    copies = []
    for part in range(parts):
        cols = pl.ds(part * wide, wide)
        rows = pl.ds(pl.multiple_of((1 - mine) * half, half), half)
        copies.append(pltpu.make_async_copy(x_hbm.at[rows, cols], x_buf.at[:, cols], sems.at[part]))
        copies[-1].start()
    rows = pl.ds(pl.multiple_of(mine * half, half), half)
    keep_copy = pltpu.make_async_copy(x_hbm.at[rows, :], x_keep, sems.at[parts + 2])
    keep_copy.start()
    col_copy.wait()
    col = col_buf[...]
    index = lax.broadcasted_iota(jnp.int32, (16, kept), 0)
    inner = parity_sign(index & col, 4)
    outer = parity_sign(index & (col >> 4), 4)
    for row in range(LOW // 16):
        low[row * 16:(row + 1) * 16] = (inner * outer[row:row + 1]).astype(jnp.bfloat16)
    high_index = lax.broadcasted_iota(jnp.int32, high.shape, 0) + me * high.shape[0]
    high[...] = parity_sign(high_index & (col >> 8), total_bits - 8)
    sign_copy.wait()
    for part in range(parts):
        copies[part].wait()
        add_products(x_buf, signs, low, high, send_ref, part, wide)
    keep_copy.wait()


def keep_kernel(parts, x_keep, signs, low, high, keep_ref):
    wide = x_keep.shape[1] // parts
    for part in range(parts):
        add_products(x_keep, signs, low, high, keep_ref, part, wide)


def partial_halves(features, signs, columns, feat_count):
    rows, width = features.shape
    kept = columns.shape[0]
    parts = max(1, width // 2048)
    half = rows // 2
    total_bits = (width * feat_count).bit_length() - 1
    params = pltpu.CompilerParams(vmem_limit_bytes=VMEM_LIMIT)
    cost = pl.CostEstimate(
        flops=2 * half * width * kept, bytes_accessed=2 * rows * width + 4 * half * kept, transcendentals=0
    )
    total_type = jax.ShapeDtypeStruct((half, kept), jnp.float32)
    send, *held = pl.pallas_call(
        functools.partial(send_kernel, total_bits, parts),
        in_specs=[pl.BlockSpec(memory_space=pltpu.HBM)] * 3,
        out_specs=[pl.BlockSpec(memory_space=pltpu.VMEM)] * 5,
        out_shape=[
            total_type,
            jax.ShapeDtypeStruct((half, width), jnp.bfloat16),
            jax.ShapeDtypeStruct((1, width), jnp.int32),
            jax.ShapeDtypeStruct((LOW, kept), jnp.bfloat16),
            jax.ShapeDtypeStruct((width // LOW, kept), jnp.float32),
        ],
        scratch_shapes=[
            pltpu.VMEM((half, width), jnp.bfloat16),
            pltpu.VMEM((1, kept), jnp.int32),
            pltpu.SemaphoreType.DMA((parts + 3,)),
        ],
        compiler_params=params,
        cost_estimate=cost,
        name="partial_sent",
    )(*(
        pltpu.with_memory_space_constraint(operand, pltpu.HBM)
        for operand in (features, signs.reshape(1, width), columns.reshape(1, kept))
    ))
    got = swap(send, feat=1)
    keep = pl.pallas_call(
        functools.partial(keep_kernel, parts),
        out_shape=total_type,
        compiler_params=params,
        cost_estimate=cost,
        name="partial_kept",
    )(*held)
    return keep, got


def gram_kernel(shard, group, factor, label_ref, *refs):
    pieces, (out_hbm, rows, blocks, sems) = refs[:-4], refs[-4:]
    steps, wide, _ = blocks.shape
    place = 0
    for piece in pieces:
        rows[place:place + piece.shape[0]] = piece[...]
        place += piece.shape[0]
    first = lax.axis_index("feat") * shard
    start = pl.multiple_of(first // LANES * LANES, LANES)
    window = rows[:, pl.ds(start, LANES)].astype(jnp.float32) * factor
    window = pltpu.roll(window, lax.rem(LANES - (first - start), LANES), 1)
    own = jnp.concatenate([window.T[:shard]] * group, axis=0)
    label = label_ref[...] - lax.broadcasted_iota(jnp.int32, own.shape, 0) // shard
    base = lax.axis_index("tok") * steps * group
    copies = []
    for step in range(steps):
        chosen = jnp.where(label == base + step * group, own, 0.0).astype(jnp.bfloat16)
        blocks[step] = jnp.dot(chosen, rows[...], preferred_element_type=jnp.float32)
        copies.append(
            pltpu.make_async_copy(blocks.at[step], out_hbm.at[pl.ds(step * wide, wide), :], sems.at[step])
        )
        copies[-1].start()
    for copy in copies:
        copy.wait()


def gram_blocks(pieces, label_row, concepts, shard, factor):
    tokens = sum(piece.shape[0] for piece in pieces)
    kept = pieces[0].shape[1]
    group = max(1, min(concepts, LOW // shard))
    wide = group * shard
    steps = concepts // group
    return pl.pallas_call(
        functools.partial(gram_kernel, shard, group, factor),
        in_specs=[pl.BlockSpec(memory_space=pltpu.VMEM)] * (1 + len(pieces)),
        out_specs=pl.BlockSpec(memory_space=pltpu.HBM),
        out_shape=jax.ShapeDtypeStruct((concepts * shard, kept), jnp.float32),
        scratch_shapes=[
            pltpu.VMEM((tokens, kept), jnp.bfloat16),
            pltpu.VMEM((steps, wide, kept), jnp.float32),
            pltpu.SemaphoreType.DMA((steps,)),
        ],
        compiler_params=pltpu.CompilerParams(vmem_limit_bytes=VMEM_LIMIT),
        cost_estimate=pl.CostEstimate(
            flops=2 * tokens * concepts * shard * kept, bytes_accessed=4 * concepts * shard * kept, transcendentals=0
        ),
        name="gram",
    )(label_row, *pieces)


def encode(values, word_ref):
    size, kept = values.shape
    half = size // 2
    top = jnp.max(jnp.abs(values), axis=1, keepdims=True)
    power = jnp.ceil(jnp.log2(jnp.maximum(top, 2.0 ** -100)))
    whole = jnp.round(values * jnp.exp2(15.0 - power))
    whole = jnp.clip(whole, -32767.0, 32767.0).astype(jnp.int32)
    word = (whole[:half] & 0xFFFF) | (whole[half:] << 16)
    for column in range(kept // LANES):
        word_ref[column * half:(column + 1) * half] = word[:, column * LANES:(column + 1) * LANES]
    group = lax.broadcasted_iota(jnp.int32, (8, LANES), 1) // (LANES * 8 // size)
    tile = jnp.zeros((8, LANES), jnp.int32)
    for at in range(size // 8):
        tile = jnp.where(group == at, power[at * 8:(at + 1) * 8].astype(jnp.int32), tile)
    word_ref[kept // LANES * half:] = tile


def decode(word_ref, size):
    half = size // 2
    columns = word_ref.shape[0] // half
    word = jnp.concatenate([word_ref[at * half:(at + 1) * half] for at in range(columns)], axis=1)
    code = jnp.concatenate([(word << 16) >> 16, word >> 16], axis=0).astype(jnp.float32)
    tile = jnp.exp2(word_ref[columns * half:].astype(jnp.float32) - 15.0)
    lanes = LANES * 8 // size
    scale = jnp.concatenate([tile[:, at * lanes:at * lanes + 1] for at in range(size // 8)], axis=0)
    return code * scale


def first_kernel(stride, keep_ref, got_ref, label_ref, total_ref, there_ref, here_ref, again_ref, label_out):
    size = total_ref.shape[0]
    digit = lax.rem(lax.axis_index("feat") // stride, 2)

    def piece(at):
        span = pl.ds(pl.multiple_of(at * size, size), size)
        return keep_ref[span, :] + got_ref[span, :]

    encode(piece(1 - digit), there_ref)
    again_ref[...] = there_ref[...]
    total = piece(digit)
    total_ref[...] = total
    encode(total, here_ref)
    label_out[...] = label_ref[...]


def square_kernel(total_ref, both_ref, x_ref, z_ref, sum_ref, out_ref):
    size = total_ref.shape[0]
    total = (total_ref[...] + decode(x_ref, size)) + (decode(z_ref, size) + decode(both_ref, size))
    sum_ref[...] = total
    encode(total, out_ref)


def middle_kernel(total_ref, word_ref, sum_ref, out_ref):
    total = total_ref[...] + decode(word_ref, total_ref.shape[0])
    sum_ref[...] = total
    encode(total, out_ref)


def last_kernel(scale, blocks, total_ref, word_ref, *refs):
    label_refs, (label_out, *row_refs) = refs[:-6], refs[-6:]
    size = total_ref.shape[0]
    row = ((total_ref[...] + decode(word_ref, size)) * scale).astype(jnp.bfloat16)
    for row_ref in row_refs:
        row_ref[...] = row
    core = lax.rem(lax.axis_index("feat"), 2)
    digit = lax.rem(lax.axis_index("feat") // 2, 2)
    groups = LANES // size
    lane = lax.broadcasted_iota(jnp.int32, (8, LANES), 1)
    for place in range(0, 2 * len(blocks), groups):
        out = jnp.zeros((8, LANES), jnp.int32)
        for at in range(groups):
            half, (tok, x) = (place + at) // len(blocks), blocks[(place + at) % len(blocks)]
            source = (core ^ half) * 2 * size + (digit ^ x) * size
            moved = pltpu.roll(
                jnp.broadcast_to(label_refs[tok][...], out.shape), lax.rem(at * size - source + LANES, LANES), 1
            )
            out = jnp.where(lane // size == at, moved, out)
        label_out[:, place * size:(place + groups) * size] = out[:1]


def local_call(kernel, name, *operands, out_shape):
    return pl.pallas_call(
        kernel,
        out_shape=out_shape,
        compiler_params=pltpu.CompilerParams(vmem_limit_bytes=VMEM_LIMIT),
        name=name,
    )(*operands)


def swap(array, tok=0, feat=0):
    tok_count, feat_count = lax.axis_size("tok"), lax.axis_size("feat")
    pairs = [
        (f * tok_count + t, (f ^ feat) * tok_count + (t ^ tok))
        for f in range(feat_count)
        for t in range(tok_count)
    ]
    return lax.ppermute(array, ("feat", "tok"), pairs)


def body(features, signs, columns, labels):
    rows, width = features.shape
    feat_count = lax.axis_size("feat")
    feat_index = lax.axis_index("feat")
    tok_count = lax.axis_size("tok")
    kept = columns.shape[0]
    shard = kept // feat_count
    size = rows // 4
    total_type = jax.ShapeDtypeStruct((size, kept), jnp.float32)
    word_type = jax.ShapeDtypeStruct((kept // LANES * (size // 2) + 8, LANES), jnp.int32)
    row_type = jax.ShapeDtypeStruct((size, kept), jnp.bfloat16)
    label_type = jax.ShapeDtypeStruct((1, rows), jnp.int32)

    keep, got = partial_halves(features, signs, columns, feat_count)
    total, there, here, again, label = local_call(
        functools.partial(first_kernel, 2),
        "first_split",
        keep,
        got,
        labels.reshape(1, rows),
        out_shape=[total_type, word_type, word_type, word_type, label_type],
    )
    both = swap(again, feat=6)
    x_word = swap(there, feat=2)
    z_word = swap(here, feat=4)
    all_labels = [label] + [swap(label, tok=tok) for tok in range(1, tok_count)]
    total, word = local_call(
        square_kernel, "add_square", total, both, x_word, z_word, out_shape=[total_type, word_type]
    )
    word = swap(word, feat=8)
    stride = 16
    while stride < feat_count:
        total, word = local_call(middle_kernel, "add_encode", total, word, out_shape=[total_type, word_type])
        word = swap(word, feat=stride)
        stride *= 2

    blocks = [(0, 0)]
    stride = 2
    while stride < tok_count:
        blocks = blocks + [(tok ^ stride, x) for tok, x in blocks]
        stride *= 2
    blocks = [(tok ^ flip, x) for flip, x in ((0, 0), (1, 1), (0, 1), (1, 0)) for tok, _ in blocks]
    scale = 1.0 / math.sqrt(width * feat_count)
    label_row, *copies = local_call(
        functools.partial(last_kernel, scale, blocks),
        "sketch_rows",
        total,
        word,
        *all_labels,
        out_shape=[jax.ShapeDtypeStruct((1, 2 * len(blocks) * size), jnp.int32)] + [row_type] * 5,
    )
    stride = 2
    while stride < tok_count:
        copies = [jnp.concatenate([copies[0], swap(copies[0], tok=stride)], axis=0)] * 5
        stride *= 2
    received = [swap(copies[0], tok=1, feat=2), swap(copies[1], feat=2), swap(copies[2], tok=1)]
    last = swap(copies[3], tok=1, feat=1)
    ours = copies[4:] + received
    theirs = [swap(block, feat=1) for block in ours[:3]] + [last]
    concepts = C // tok_count
    gram = gram_blocks(ours + theirs, label_row, concepts, shard, C / (rows * tok_count))
    return gram.reshape(concepts, shard, kept)


def solution(mesh):
    in_specs = (P("tok", "feat"), P("feat"), P(), P("tok", None))
    out_specs = P("tok", "feat", None)
    return jax.shard_map(body, mesh=mesh, in_specs=in_specs, out_specs=out_specs, check_vma=False)
```

```python
import functools
import math

import jax
import jax.numpy as jnp
from jax import lax
from jax.experimental import pallas as pl
from jax.experimental.pallas import tpu as pltpu
from jax.sharding import PartitionSpec as P

C = 32
LOW = 256
LANES = 128
VMEM_LIMIT = 48 * 1024 * 1024


def parity_sign(number, bit_count):
    shift = 1
    while shift < bit_count:
        shift *= 2
    while shift > 1:
        shift //= 2
        number = number ^ (number >> shift)
    return (1 - 2 * (number & 1)).astype(jnp.float32)


def add_products(x_ref, sign_ref, low, high, out_ref, part, wide):
    rows, kept = out_ref.shape
    blocks = wide // LOW
    stack = []
    for block in range(part * blocks, (part + 1) * blocks):
        cols = slice(block * LOW, (block + 1) * LOW)
        stack.append(x_ref[:, cols] * sign_ref[:, cols].astype(jnp.bfloat16))
    stack = jnp.concatenate(stack, axis=0)
    for group in range(kept // LOW):
        cols = slice(group * LOW, (group + 1) * LOW)
        products = jnp.dot(stack, low[:, cols], preferred_element_type=jnp.float32)
        total = None
        for at in range(blocks):
            row = part * blocks + at
            term = products[at * rows:(at + 1) * rows] * high[row:row + 1, cols]
            total = term if total is None else total + term
        if part > 0:
            total = total + out_ref[:, cols]
        out_ref[:, cols] = total


def send_kernel(total_bits, parts, x_hbm, s_hbm, col_hbm, send_ref, x_keep, signs, low, high, x_buf, col_buf, sems):
    half, kept = send_ref.shape
    wide = x_hbm.shape[1] // parts
    me = lax.axis_index("feat")
    mine = lax.rem(me, 2)
    col_copy = pltpu.make_async_copy(col_hbm, col_buf, sems.at[parts])
    sign_copy = pltpu.make_async_copy(s_hbm, signs, sems.at[parts + 1])
    col_copy.start()
    sign_copy.start()
    copies = []
    for part in range(parts):
        cols = pl.ds(part * wide, wide)
        rows = pl.ds(pl.multiple_of((1 - mine) * half, half), half)
        copies.append(pltpu.make_async_copy(x_hbm.at[rows, cols], x_buf.at[:, cols], sems.at[part]))
        copies[-1].start()
    rows = pl.ds(pl.multiple_of(mine * half, half), half)
    keep_copy = pltpu.make_async_copy(x_hbm.at[rows, :], x_keep, sems.at[parts + 2])
    keep_copy.start()
    col_copy.wait()
    col = col_buf[...]
    index = lax.broadcasted_iota(jnp.int32, (16, kept), 0)
    inner = parity_sign(index & col, 4)
    outer = parity_sign(index & (col >> 4), 4)
    for row in range(LOW // 16):
        low[row * 16:(row + 1) * 16] = (inner * outer[row:row + 1]).astype(jnp.bfloat16)
    high_index = lax.broadcasted_iota(jnp.int32, high.shape, 0) + me * high.shape[0]
    high[...] = parity_sign(high_index & (col >> 8), total_bits - 8)
    sign_copy.wait()
    for part in range(parts):
        copies[part].wait()
        add_products(x_buf, signs, low, high, send_ref, part, wide)
    keep_copy.wait()


def keep_kernel(parts, x_keep, signs, low, high, keep_ref):
    wide = x_keep.shape[1] // parts
    for part in range(parts):
        add_products(x_keep, signs, low, high, keep_ref, part, wide)


def partial_halves(features, signs, columns, feat_count):
    rows, width = features.shape
    kept = columns.shape[0]
    parts = max(1, width // 2048)
    half = rows // 2
    total_bits = (width * feat_count).bit_length() - 1
    params = pltpu.CompilerParams(vmem_limit_bytes=VMEM_LIMIT)
    cost = pl.CostEstimate(
        flops=2 * half * width * kept, bytes_accessed=2 * rows * width + 4 * half * kept, transcendentals=0
    )
    total_type = jax.ShapeDtypeStruct((half, kept), jnp.float32)
    send, *held = pl.pallas_call(
        functools.partial(send_kernel, total_bits, parts),
        in_specs=[pl.BlockSpec(memory_space=pltpu.HBM)] * 3,
        out_specs=[pl.BlockSpec(memory_space=pltpu.VMEM)] * 5,
        out_shape=[
            total_type,
            jax.ShapeDtypeStruct((half, width), jnp.bfloat16),
            jax.ShapeDtypeStruct((1, width), jnp.int32),
            jax.ShapeDtypeStruct((LOW, kept), jnp.bfloat16),
            jax.ShapeDtypeStruct((width // LOW, kept), jnp.float32),
        ],
        scratch_shapes=[
            pltpu.VMEM((half, width), jnp.bfloat16),
            pltpu.VMEM((1, kept), jnp.int32),
            pltpu.SemaphoreType.DMA((parts + 3,)),
        ],
        compiler_params=params,
        cost_estimate=cost,
        name="partial_sent",
    )(*(
        pltpu.with_memory_space_constraint(operand, pltpu.HBM)
        for operand in (features, signs.reshape(1, width), columns.reshape(1, kept))
    ))
    got = swap(send, feat=1)
    keep = pl.pallas_call(
        functools.partial(keep_kernel, parts),
        out_shape=total_type,
        compiler_params=params,
        cost_estimate=cost,
        name="partial_kept",
    )(*held)
    return keep, got


def gram_kernel(shard, group, factor, label_ref, *refs):
    pieces, (out_hbm, rows, blocks, sems) = refs[:-4], refs[-4:]
    steps, wide, _ = blocks.shape
    place = 0
    for piece in pieces:
        rows[place:place + piece.shape[0]] = piece[...]
        place += piece.shape[0]
    first = lax.axis_index("feat") * shard
    start = pl.multiple_of(first // LANES * LANES, LANES)
    window = rows[:, pl.ds(start, LANES)].astype(jnp.float32) * factor
    window = pltpu.roll(window, lax.rem(LANES - (first - start), LANES), 1)
    own = jnp.concatenate([window.T[:shard]] * group, axis=0)
    label = label_ref[...] - lax.broadcasted_iota(jnp.int32, own.shape, 0) // shard
    base = lax.axis_index("tok") * steps * group
    copies = []
    for step in range(steps):
        chosen = jnp.where(label == base + step * group, own, 0.0).astype(jnp.bfloat16)
        blocks[step] = jnp.dot(chosen, rows[...], preferred_element_type=jnp.float32)
        copies.append(
            pltpu.make_async_copy(blocks.at[step], out_hbm.at[pl.ds(step * wide, wide), :], sems.at[step])
        )
        copies[-1].start()
    for copy in copies:
        copy.wait()


def gram_blocks(pieces, label_row, concepts, shard, factor):
    tokens = sum(piece.shape[0] for piece in pieces)
    kept = pieces[0].shape[1]
    group = max(1, min(concepts, LOW // shard))
    wide = group * shard
    steps = concepts // group
    return pl.pallas_call(
        functools.partial(gram_kernel, shard, group, factor),
        in_specs=[pl.BlockSpec(memory_space=pltpu.VMEM)] * (1 + len(pieces)),
        out_specs=pl.BlockSpec(memory_space=pltpu.HBM),
        out_shape=jax.ShapeDtypeStruct((concepts * shard, kept), jnp.float32),
        scratch_shapes=[
            pltpu.VMEM((tokens, kept), jnp.bfloat16),
            pltpu.VMEM((steps, wide, kept), jnp.float32),
            pltpu.SemaphoreType.DMA((steps,)),
        ],
        compiler_params=pltpu.CompilerParams(vmem_limit_bytes=VMEM_LIMIT),
        cost_estimate=pl.CostEstimate(
            flops=2 * tokens * concepts * shard * kept, bytes_accessed=4 * concepts * shard * kept, transcendentals=0
        ),
        name="gram",
    )(label_row, *pieces)


def encode(values, word_ref):
    size, kept = values.shape
    half = size // 2
    top = jnp.max(jnp.abs(values), axis=1, keepdims=True)
    power = jnp.ceil(jnp.log2(jnp.maximum(top, 2.0 ** -100)))
    whole = jnp.round(values * jnp.exp2(15.0 - power))
    whole = jnp.clip(whole, -32767.0, 32767.0).astype(jnp.int32)
    word = (whole[:half] & 0xFFFF) | (whole[half:] << 16)
    for column in range(kept // LANES):
        word_ref[column * half:(column + 1) * half] = word[:, column * LANES:(column + 1) * LANES]
    group = lax.broadcasted_iota(jnp.int32, (8, LANES), 1) // (LANES * 8 // size)
    tile = jnp.zeros((8, LANES), jnp.int32)
    for at in range(size // 8):
        tile = jnp.where(group == at, power[at * 8:(at + 1) * 8].astype(jnp.int32), tile)
    word_ref[kept // LANES * half:] = tile


def decode(word_ref, size):
    half = size // 2
    columns = word_ref.shape[0] // half
    word = jnp.concatenate([word_ref[at * half:(at + 1) * half] for at in range(columns)], axis=1)
    code = jnp.concatenate([(word << 16) >> 16, word >> 16], axis=0).astype(jnp.float32)
    tile = jnp.exp2(word_ref[columns * half:].astype(jnp.float32) - 15.0)
    lanes = LANES * 8 // size
    scale = jnp.concatenate([tile[:, at * lanes:at * lanes + 1] for at in range(size // 8)], axis=0)
    return code * scale


def first_kernel(stride, keep_ref, got_ref, label_ref, total_ref, there_ref, here_ref, again_ref, label_out):
    size = total_ref.shape[0]
    digit = lax.rem(lax.axis_index("feat") // stride, 2)

    def piece(at):
        span = pl.ds(pl.multiple_of(at * size, size), size)
        return keep_ref[span, :] + got_ref[span, :]

    encode(piece(1 - digit), there_ref)
    again_ref[...] = there_ref[...]
    total = piece(digit)
    total_ref[...] = total
    encode(total, here_ref)
    label_out[...] = label_ref[...]


def square_kernel(total_ref, both_ref, x_ref, z_ref, sum_ref, out_ref):
    size = total_ref.shape[0]
    total = (total_ref[...] + decode(x_ref, size)) + (decode(z_ref, size) + decode(both_ref, size))
    sum_ref[...] = total
    encode(total, out_ref)


def middle_kernel(total_ref, word_ref, sum_ref, out_ref):
    total = total_ref[...] + decode(word_ref, total_ref.shape[0])
    sum_ref[...] = total
    encode(total, out_ref)


def last_kernel(scale, blocks, total_ref, word_ref, *refs):
    label_refs, (label_out, *row_refs) = refs[:-6], refs[-6:]
    size = total_ref.shape[0]
    row = ((total_ref[...] + decode(word_ref, size)) * scale).astype(jnp.bfloat16)
    for row_ref in row_refs:
        row_ref[...] = row
    core = lax.rem(lax.axis_index("feat"), 2)
    digit = lax.rem(lax.axis_index("feat") // 2, 2)
    groups = LANES // size
    lane = lax.broadcasted_iota(jnp.int32, (8, LANES), 1)
    for place in range(0, 2 * len(blocks), groups):
        out = jnp.zeros((8, LANES), jnp.int32)
        for at in range(groups):
            half, (tok, x) = (place + at) // len(blocks), blocks[(place + at) % len(blocks)]
            source = (core ^ half) * 2 * size + (digit ^ x) * size
            moved = pltpu.roll(
                jnp.broadcast_to(label_refs[tok][...], out.shape), lax.rem(at * size - source + LANES, LANES), 1
            )
            out = jnp.where(lane // size == at, moved, out)
        label_out[:, place * size:(place + groups) * size] = out[:1]


def local_call(kernel, name, *operands, out_shape):
    return pl.pallas_call(
        kernel,
        out_shape=out_shape,
        compiler_params=pltpu.CompilerParams(vmem_limit_bytes=VMEM_LIMIT),
        name=name,
    )(*operands)


def swap(array, tok=0, feat=0):
    tok_count, feat_count = lax.axis_size("tok"), lax.axis_size("feat")
    pairs = [
        (f * tok_count + t, (f ^ feat) * tok_count + (t ^ tok))
        for f in range(feat_count)
        for t in range(tok_count)
    ]
    return lax.ppermute(array, ("feat", "tok"), pairs)


def body(features, signs, columns, labels):
    rows, width = features.shape
    feat_count = lax.axis_size("feat")
    feat_index = lax.axis_index("feat")
    tok_count = lax.axis_size("tok")
    kept = columns.shape[0]
    shard = kept // feat_count
    size = rows // 4
    total_type = jax.ShapeDtypeStruct((size, kept), jnp.float32)
    word_type = jax.ShapeDtypeStruct((kept // LANES * (size // 2) + 8, LANES), jnp.int32)
    row_type = jax.ShapeDtypeStruct((size, kept), jnp.bfloat16)
    label_type = jax.ShapeDtypeStruct((1, rows), jnp.int32)

    keep, got = partial_halves(features, signs, columns, feat_count)
    total, there, here, again, label = local_call(
        functools.partial(first_kernel, 2),
        "first_split",
        keep,
        got,
        labels.reshape(1, rows),
        out_shape=[total_type, word_type, word_type, word_type, label_type],
    )
    both = swap(again, feat=6)
    x_word = swap(there, feat=2)
    z_word = swap(here, feat=4)
    all_labels = [label] + [swap(label, tok=tok) for tok in range(1, tok_count)]
    total, word = local_call(
        square_kernel, "add_square", total, both, x_word, z_word, out_shape=[total_type, word_type]
    )
    word = swap(word, feat=8)
    stride = 16
    while stride < feat_count:
        total, word = local_call(middle_kernel, "add_encode", total, word, out_shape=[total_type, word_type])
        word = swap(word, feat=stride)
        stride *= 2

    blocks = [(0, 0)]
    stride = 2
    while stride < tok_count:
        blocks = blocks + [(tok ^ stride, x) for tok, x in blocks]
        stride *= 2
    blocks = [(tok ^ flip, x) for flip, x in ((0, 0), (1, 1), (0, 1), (1, 0)) for tok, _ in blocks]
    scale = 1.0 / math.sqrt(width * feat_count)
    label_row, *copies = local_call(
        functools.partial(last_kernel, scale, blocks),
        "sketch_rows",
        total,
        word,
        *all_labels,
        out_shape=[jax.ShapeDtypeStruct((1, 2 * len(blocks) * size), jnp.int32)] + [row_type] * 5,
    )
    stride = 2
    while stride < tok_count:
        copies = [jnp.concatenate([copies[0], swap(copies[0], tok=stride)], axis=0)] * 5
        stride *= 2
    far = swap(copies[0], tok=1, feat=2)
    crossed = swap(copies[1], tok=1, feat=1)
    received = [far, swap(copies[2], feat=2), swap(copies[3], tok=1)]
    ours = copies[4:] + received
    theirs = [swap(block, feat=1) for block in ours[:3]] + [crossed]
    concepts = C // tok_count
    gram = gram_blocks(ours + theirs, label_row, concepts, shard, C / (rows * tok_count))
    return gram.reshape(concepts, shard, kept)


def solution(mesh):
    in_specs = (P("tok", "feat"), P("feat"), P(), P("tok", None))
    out_specs = P("tok", "feat", None)
    return jax.shard_map(body, mesh=mesh, in_specs=in_specs, out_specs=out_specs, check_vma=False)
```

```python
import functools
import math

import jax
import jax.numpy as jnp
from jax import lax
from jax.experimental import pallas as pl
from jax.experimental.pallas import tpu as pltpu
from jax.sharding import PartitionSpec as P

C = 32
LOW = 256
LANES = 128
VMEM_LIMIT = 48 * 1024 * 1024


def parity_sign(number, bit_count):
    shift = 1
    while shift < bit_count:
        shift *= 2
    while shift > 1:
        shift //= 2
        number = number ^ (number >> shift)
    return (1 - 2 * (number & 1)).astype(jnp.float32)


def add_products(x_ref, sign_ref, low, high, out_ref, part, wide):
    rows, kept = out_ref.shape
    blocks = wide // LOW
    stack = []
    for block in range(part * blocks, (part + 1) * blocks):
        cols = slice(block * LOW, (block + 1) * LOW)
        stack.append(x_ref[:, cols] * sign_ref[:, cols].astype(jnp.bfloat16))
    stack = jnp.concatenate(stack, axis=0)
    for group in range(kept // LOW):
        cols = slice(group * LOW, (group + 1) * LOW)
        products = jnp.dot(stack, low[:, cols], preferred_element_type=jnp.float32)
        total = None
        for at in range(blocks):
            row = part * blocks + at
            term = products[at * rows:(at + 1) * rows] * high[row:row + 1, cols]
            total = term if total is None else total + term
        if part > 0:
            total = total + out_ref[:, cols]
        out_ref[:, cols] = total


def send_kernel(total_bits, parts, x_hbm, s_hbm, col_hbm, send_ref, x_keep, signs, low, high, x_buf, col_buf, sems):
    half, kept = send_ref.shape
    wide = x_hbm.shape[1] // parts
    me = lax.axis_index("feat")
    mine = lax.rem(me, 2)
    col_copy = pltpu.make_async_copy(col_hbm, col_buf, sems.at[parts])
    sign_copy = pltpu.make_async_copy(s_hbm, signs, sems.at[parts + 1])
    col_copy.start()
    sign_copy.start()
    copies = []
    for part in range(parts):
        cols = pl.ds(part * wide, wide)
        rows = pl.ds(pl.multiple_of((1 - mine) * half, half), half)
        copies.append(pltpu.make_async_copy(x_hbm.at[rows, cols], x_buf.at[:, cols], sems.at[part]))
        copies[-1].start()
    rows = pl.ds(pl.multiple_of(mine * half, half), half)
    keep_copy = pltpu.make_async_copy(x_hbm.at[rows, :], x_keep, sems.at[parts + 2])
    keep_copy.start()
    col_copy.wait()
    col = col_buf[...]
    index = lax.broadcasted_iota(jnp.int32, (16, kept), 0)
    inner = parity_sign(index & col, 4)
    outer = parity_sign(index & (col >> 4), 4)
    for row in range(LOW // 16):
        low[row * 16:(row + 1) * 16] = (inner * outer[row:row + 1]).astype(jnp.bfloat16)
    high_index = lax.broadcasted_iota(jnp.int32, high.shape, 0) + me * high.shape[0]
    high[...] = parity_sign(high_index & (col >> 8), total_bits - 8)
    sign_copy.wait()
    for part in range(parts):
        copies[part].wait()
        add_products(x_buf, signs, low, high, send_ref, part, wide)
    keep_copy.wait()


def keep_kernel(parts, x_keep, signs, low, high, keep_ref):
    wide = x_keep.shape[1] // parts
    for part in range(parts):
        add_products(x_keep, signs, low, high, keep_ref, part, wide)


def partial_halves(features, signs, columns, feat_count):
    rows, width = features.shape
    kept = columns.shape[0]
    parts = max(1, width // 2048)
    half = rows // 2
    total_bits = (width * feat_count).bit_length() - 1
    params = pltpu.CompilerParams(vmem_limit_bytes=VMEM_LIMIT)
    cost = pl.CostEstimate(
        flops=2 * half * width * kept, bytes_accessed=2 * rows * width + 4 * half * kept, transcendentals=0
    )
    total_type = jax.ShapeDtypeStruct((half, kept), jnp.float32)
    send, *held = pl.pallas_call(
        functools.partial(send_kernel, total_bits, parts),
        in_specs=[pl.BlockSpec(memory_space=pltpu.HBM)] * 3,
        out_specs=[pl.BlockSpec(memory_space=pltpu.VMEM)] * 5,
        out_shape=[
            total_type,
            jax.ShapeDtypeStruct((half, width), jnp.bfloat16),
            jax.ShapeDtypeStruct((1, width), jnp.int32),
            jax.ShapeDtypeStruct((LOW, kept), jnp.bfloat16),
            jax.ShapeDtypeStruct((width // LOW, kept), jnp.float32),
        ],
        scratch_shapes=[
            pltpu.VMEM((half, width), jnp.bfloat16),
            pltpu.VMEM((1, kept), jnp.int32),
            pltpu.SemaphoreType.DMA((parts + 3,)),
        ],
        compiler_params=params,
        cost_estimate=cost,
        name="partial_sent",
    )(*(
        pltpu.with_memory_space_constraint(operand, pltpu.HBM)
        for operand in (features, signs.reshape(1, width), columns.reshape(1, kept))
    ))
    got = swap(send, feat=1)
    keep = pl.pallas_call(
        functools.partial(keep_kernel, parts),
        out_shape=total_type,
        compiler_params=params,
        cost_estimate=cost,
        name="partial_kept",
    )(*held)
    return keep, got


def gram_kernel(shard, group, factor, label_ref, *refs):
    pieces, (out_hbm, rows, blocks, sems) = refs[:-4], refs[-4:]
    steps, wide, _ = blocks.shape
    place = 0
    for piece in pieces:
        rows[place:place + piece.shape[0]] = piece[...]
        place += piece.shape[0]
    first = lax.axis_index("feat") * shard
    start = pl.multiple_of(first // LANES * LANES, LANES)
    window = rows[:, pl.ds(start, LANES)].astype(jnp.float32) * factor
    window = pltpu.roll(window, lax.rem(LANES - (first - start), LANES), 1)
    own = jnp.concatenate([window.T[:shard]] * group, axis=0)
    label = label_ref[...] - lax.broadcasted_iota(jnp.int32, own.shape, 0) // shard
    base = lax.axis_index("tok") * steps * group
    copies = []
    for step in range(steps):
        chosen = jnp.where(label == base + step * group, own, 0.0).astype(jnp.bfloat16)
        blocks[step] = jnp.dot(chosen, rows[...], preferred_element_type=jnp.float32)
        copies.append(
            pltpu.make_async_copy(blocks.at[step], out_hbm.at[pl.ds(step * wide, wide), :], sems.at[step])
        )
        copies[-1].start()
    for copy in copies:
        copy.wait()


def gram_blocks(pieces, label_row, concepts, shard, factor):
    tokens = sum(piece.shape[0] for piece in pieces)
    kept = pieces[0].shape[1]
    group = max(1, min(concepts, LOW // shard))
    wide = group * shard
    steps = concepts // group
    return pl.pallas_call(
        functools.partial(gram_kernel, shard, group, factor),
        in_specs=[pl.BlockSpec(memory_space=pltpu.VMEM)] * (1 + len(pieces)),
        out_specs=pl.BlockSpec(memory_space=pltpu.HBM),
        out_shape=jax.ShapeDtypeStruct((concepts * shard, kept), jnp.float32),
        scratch_shapes=[
            pltpu.VMEM((tokens, kept), jnp.bfloat16),
            pltpu.VMEM((steps, wide, kept), jnp.float32),
            pltpu.SemaphoreType.DMA((steps,)),
        ],
        compiler_params=pltpu.CompilerParams(vmem_limit_bytes=VMEM_LIMIT),
        cost_estimate=pl.CostEstimate(
            flops=2 * tokens * concepts * shard * kept, bytes_accessed=4 * concepts * shard * kept, transcendentals=0
        ),
        name="gram",
    )(label_row, *pieces)


def encode(values, word_ref):
    size, kept = values.shape
    half = size // 2
    top = jnp.max(jnp.abs(values), axis=1, keepdims=True)
    power = jnp.ceil(jnp.log2(jnp.maximum(top, 2.0 ** -100)))
    whole = jnp.round(values * jnp.exp2(15.0 - power))
    whole = jnp.clip(whole, -32767.0, 32767.0).astype(jnp.int32)
    word = (whole[:half] & 0xFFFF) | (whole[half:] << 16)
    for column in range(kept // LANES):
        word_ref[column * half:(column + 1) * half] = word[:, column * LANES:(column + 1) * LANES]
    group = lax.broadcasted_iota(jnp.int32, (8, LANES), 1) // (LANES * 8 // size)
    tile = jnp.zeros((8, LANES), jnp.int32)
    for at in range(size // 8):
        tile = jnp.where(group == at, power[at * 8:(at + 1) * 8].astype(jnp.int32), tile)
    word_ref[kept // LANES * half:] = tile


def decode(word_ref, size):
    half = size // 2
    columns = word_ref.shape[0] // half
    word = jnp.concatenate([word_ref[at * half:(at + 1) * half] for at in range(columns)], axis=1)
    code = jnp.concatenate([(word << 16) >> 16, word >> 16], axis=0).astype(jnp.float32)
    tile = jnp.exp2(word_ref[columns * half:].astype(jnp.float32) - 15.0)
    lanes = LANES * 8 // size
    scale = jnp.concatenate([tile[:, at * lanes:at * lanes + 1] for at in range(size // 8)], axis=0)
    return code * scale


def first_kernel(stride, keep_ref, got_ref, label_ref, total_ref, there_ref, here_ref, again_ref, label_out):
    size = total_ref.shape[0]
    digit = lax.rem(lax.axis_index("feat") // stride, 2)

    def piece(at):
        span = pl.ds(pl.multiple_of(at * size, size), size)
        return keep_ref[span, :] + got_ref[span, :]

    encode(piece(1 - digit), there_ref)
    again_ref[...] = there_ref[...]
    total = piece(digit)
    total_ref[...] = total
    encode(total, here_ref)
    label_out[...] = label_ref[...]


def square_kernel(total_ref, both_ref, x_ref, z_ref, sum_ref, out_ref):
    size = total_ref.shape[0]
    total = (total_ref[...] + decode(x_ref, size)) + (decode(z_ref, size) + decode(both_ref, size))
    sum_ref[...] = total
    encode(total, out_ref)


def middle_kernel(total_ref, word_ref, sum_ref, out_ref):
    total = total_ref[...] + decode(word_ref, total_ref.shape[0])
    sum_ref[...] = total
    encode(total, out_ref)


def last_kernel(scale, blocks, total_ref, word_ref, *refs):
    label_refs, (label_out, *row_refs) = refs[:-6], refs[-6:]
    size = total_ref.shape[0]
    row = ((total_ref[...] + decode(word_ref, size)) * scale).astype(jnp.bfloat16)
    for row_ref in row_refs:
        row_ref[...] = row
    core = lax.rem(lax.axis_index("feat"), 2)
    digit = lax.rem(lax.axis_index("feat") // 2, 2)
    groups = LANES // size
    lane = lax.broadcasted_iota(jnp.int32, (8, LANES), 1)
    for place in range(0, len(blocks), groups):
        out = jnp.zeros((8, LANES), jnp.int32)
        for at, (half, tok, x) in enumerate(blocks[place:place + groups]):
            source = (core ^ half) * 2 * size + (digit ^ x) * size
            moved = pltpu.roll(
                jnp.broadcast_to(label_refs[tok][...], out.shape), lax.rem(at * size - source + LANES, LANES), 1
            )
            out = jnp.where(lane // size == at, moved, out)
        label_out[:, place * size:(place + groups) * size] = out[:1]


def local_call(kernel, name, *operands, out_shape):
    return pl.pallas_call(
        kernel,
        out_shape=out_shape,
        compiler_params=pltpu.CompilerParams(vmem_limit_bytes=VMEM_LIMIT),
        name=name,
    )(*operands)


def swap(array, tok=0, feat=0):
    tok_count, feat_count = lax.axis_size("tok"), lax.axis_size("feat")
    pairs = [
        (f * tok_count + t, (f ^ feat) * tok_count + (t ^ tok))
        for f in range(feat_count)
        for t in range(tok_count)
    ]
    return lax.ppermute(array, ("feat", "tok"), pairs)


def body(features, signs, columns, labels):
    rows, width = features.shape
    feat_count = lax.axis_size("feat")
    feat_index = lax.axis_index("feat")
    tok_count = lax.axis_size("tok")
    kept = columns.shape[0]
    shard = kept // feat_count
    size = rows // 4
    total_type = jax.ShapeDtypeStruct((size, kept), jnp.float32)
    word_type = jax.ShapeDtypeStruct((kept // LANES * (size // 2) + 8, LANES), jnp.int32)
    row_type = jax.ShapeDtypeStruct((size, kept), jnp.bfloat16)
    label_type = jax.ShapeDtypeStruct((1, rows), jnp.int32)

    keep, got = partial_halves(features, signs, columns, feat_count)
    total, there, here, again, label = local_call(
        functools.partial(first_kernel, 2),
        "first_split",
        keep,
        got,
        labels.reshape(1, rows),
        out_shape=[total_type, word_type, word_type, word_type, label_type],
    )
    both = swap(again, feat=6)
    x_word = swap(there, feat=2)
    z_word = swap(here, feat=4)
    all_labels = [label] + [swap(label, tok=tok) for tok in range(1, tok_count)]
    total, word = local_call(
        square_kernel, "add_square", total, both, x_word, z_word, out_shape=[total_type, word_type]
    )
    word = swap(word, feat=8)
    stride = 16
    while stride < feat_count:
        total, word = local_call(middle_kernel, "add_encode", total, word, out_shape=[total_type, word_type])
        word = swap(word, feat=stride)
        stride *= 2

    toks = [0]
    stride = 2
    while stride < tok_count:
        toks = toks + [tok ^ stride for tok in toks]
        stride *= 2
    order = [(0, 1, 1), (1, 1, 0), (0, 0, 1), (0, 1, 0), (0, 0, 0), (1, 1, 1), (1, 0, 1), (1, 0, 0)]
    blocks = [(core, tok ^ flip, x) for core, flip, x in order for tok in toks]
    scale = 1.0 / math.sqrt(width * feat_count)
    label_row, *copies = local_call(
        functools.partial(last_kernel, scale, blocks),
        "sketch_rows",
        total,
        word,
        *all_labels,
        out_shape=[jax.ShapeDtypeStruct((1, len(blocks) * size), jnp.int32)] + [row_type] * 5,
    )
    stride = 2
    while stride < tok_count:
        copies = [jnp.concatenate([copies[0], swap(copies[0], tok=stride)], axis=0)] * 5
        stride *= 2
    far, crossed, beside, across, own = [
        swap(copy, tok=tok, feat=2 * x + core) if core + tok + x else copy
        for copy, (core, tok, x) in zip(copies, order)
    ]
    pieces = [far, crossed, beside, across, own] + [swap(block, feat=1) for block in (far, beside, own)]
    concepts = C // tok_count
    gram = gram_blocks(pieces, label_row, concepts, shard, C / (rows * tok_count))
    return gram.reshape(concepts, shard, kept)


def solution(mesh):
    in_specs = (P("tok", "feat"), P("feat"), P(), P("tok", None))
    out_specs = P("tok", "feat", None)
    return jax.shard_map(body, mesh=mesh, in_specs=in_specs, out_specs=out_specs, check_vma=False)
```

```python
import functools
import math

import jax
import jax.numpy as jnp
from jax import lax
from jax.experimental import pallas as pl
from jax.experimental.pallas import tpu as pltpu
from jax.sharding import PartitionSpec as P

C = 32
LOW = 256
LANES = 128
VMEM_LIMIT = 48 * 1024 * 1024


def parity_sign(number, bit_count):
    shift = 1
    while shift < bit_count:
        shift *= 2
    while shift > 1:
        shift //= 2
        number = number ^ (number >> shift)
    return (1 - 2 * (number & 1)).astype(jnp.float32)


def add_products(x_ref, sign_ref, low, high, out_ref, part, wide):
    rows, kept = out_ref.shape
    blocks = wide // LOW
    stack = []
    for block in range(part * blocks, (part + 1) * blocks):
        cols = slice(block * LOW, (block + 1) * LOW)
        stack.append(x_ref[:, cols] * sign_ref[:, cols].astype(jnp.bfloat16))
    stack = jnp.concatenate(stack, axis=0)
    for group in range(kept // LOW):
        cols = slice(group * LOW, (group + 1) * LOW)
        products = jnp.dot(stack, low[:, cols], preferred_element_type=jnp.float32)
        total = None
        for at in range(blocks):
            row = part * blocks + at
            term = products[at * rows:(at + 1) * rows] * high[row:row + 1, cols]
            total = term if total is None else total + term
        if part > 0:
            total = total + out_ref[:, cols]
        out_ref[:, cols] = total


def send_kernel(total_bits, parts, x_hbm, s_hbm, col_hbm, send_ref, x_keep, signs, low, high, x_buf, col_buf, sems):
    half, kept = send_ref.shape
    wide = x_hbm.shape[1] // parts
    me = lax.axis_index("feat")
    mine = lax.rem(me, 2)
    col_copy = pltpu.make_async_copy(col_hbm, col_buf, sems.at[parts])
    sign_copy = pltpu.make_async_copy(s_hbm, signs, sems.at[parts + 1])
    col_copy.start()
    sign_copy.start()
    copies = []
    for part in range(parts):
        cols = pl.ds(part * wide, wide)
        rows = pl.ds(pl.multiple_of((1 - mine) * half, half), half)
        copies.append(pltpu.make_async_copy(x_hbm.at[rows, cols], x_buf.at[:, cols], sems.at[part]))
    copies[0].start()
    rows = pl.ds(pl.multiple_of(mine * half, half), half)
    copies.append(pltpu.make_async_copy(x_hbm.at[rows, :], x_keep, sems.at[parts + 2]))
    col_copy.wait()
    col = col_buf[...]
    index = lax.broadcasted_iota(jnp.int32, (16, kept), 0)
    inner = parity_sign(index & col, 4)
    outer = parity_sign(index & (col >> 4), 4)
    for row in range(LOW // 16):
        low[row * 16:(row + 1) * 16] = (inner * outer[row:row + 1]).astype(jnp.bfloat16)
    high_index = lax.broadcasted_iota(jnp.int32, high.shape, 0) + me * high.shape[0]
    high[...] = parity_sign(high_index & (col >> 8), total_bits - 8)
    sign_copy.wait()
    for part in range(parts):
        copies[part].wait()
        copies[part + 1].start()
        add_products(x_buf, signs, low, high, send_ref, part, wide)
    copies[parts].wait()


def keep_kernel(parts, x_keep, signs, low, high, keep_ref):
    wide = x_keep.shape[1] // parts
    for part in range(parts):
        add_products(x_keep, signs, low, high, keep_ref, part, wide)


def partial_halves(features, signs, columns, feat_count):
    rows, width = features.shape
    kept = columns.shape[0]
    parts = max(1, width // 2048)
    half = rows // 2
    total_bits = (width * feat_count).bit_length() - 1
    params = pltpu.CompilerParams(vmem_limit_bytes=VMEM_LIMIT)
    cost = pl.CostEstimate(
        flops=2 * half * width * kept, bytes_accessed=2 * rows * width + 4 * half * kept, transcendentals=0
    )
    total_type = jax.ShapeDtypeStruct((half, kept), jnp.float32)
    send, *held = pl.pallas_call(
        functools.partial(send_kernel, total_bits, parts),
        in_specs=[pl.BlockSpec(memory_space=pltpu.HBM)] * 3,
        out_specs=[pl.BlockSpec(memory_space=pltpu.VMEM)] * 5,
        out_shape=[
            total_type,
            jax.ShapeDtypeStruct((half, width), jnp.bfloat16),
            jax.ShapeDtypeStruct((1, width), jnp.int32),
            jax.ShapeDtypeStruct((LOW, kept), jnp.bfloat16),
            jax.ShapeDtypeStruct((width // LOW, kept), jnp.float32),
        ],
        scratch_shapes=[
            pltpu.VMEM((half, width), jnp.bfloat16),
            pltpu.VMEM((1, kept), jnp.int32),
            pltpu.SemaphoreType.DMA((parts + 3,)),
        ],
        compiler_params=params,
        cost_estimate=cost,
        name="partial_sent",
    )(*(
        pltpu.with_memory_space_constraint(operand, pltpu.HBM)
        for operand in (features, signs.reshape(1, width), columns.reshape(1, kept))
    ))
    got = swap(send, feat=1)
    keep = pl.pallas_call(
        functools.partial(keep_kernel, parts),
        out_shape=total_type,
        compiler_params=params,
        cost_estimate=cost,
        name="partial_kept",
    )(*held)
    return keep, got


def gram_kernel(shard, group, factor, label_ref, *refs):
    pieces, (out_hbm, rows, blocks, sems) = refs[:-4], refs[-4:]
    steps, wide, _ = blocks.shape
    place = 0
    for piece in pieces:
        rows[place:place + piece.shape[0]] = piece[...]
        place += piece.shape[0]
    first = lax.axis_index("feat") * shard
    start = pl.multiple_of(first // LANES * LANES, LANES)
    window = rows[:, pl.ds(start, LANES)].astype(jnp.float32) * factor
    window = pltpu.roll(window, lax.rem(LANES - (first - start), LANES), 1)
    own = jnp.concatenate([window.T[:shard]] * group, axis=0)
    label = label_ref[...] - lax.broadcasted_iota(jnp.int32, own.shape, 0) // shard
    base = lax.axis_index("tok") * steps * group
    copies = []
    for step in range(steps):
        for span in ((0, shard), (shard, wide)) if step == 0 and wide > shard else ((0, wide),):
            part = slice(*span)
            chosen = jnp.where(label[part] == base + step * group, own[part], 0.0).astype(jnp.bfloat16)
            blocks[step, part] = jnp.dot(chosen, rows[...], preferred_element_type=jnp.float32)
            size = span[1] - span[0]
            copies.append(
                pltpu.make_async_copy(
                    blocks.at[step, pl.ds(span[0], size), :],
                    out_hbm.at[pl.ds(step * wide + span[0], size), :],
                    sems.at[len(copies)],
                )
            )
            copies[-1].start()
    for copy in copies:
        copy.wait()


def gram_blocks(pieces, label_row, concepts, shard, factor):
    tokens = sum(piece.shape[0] for piece in pieces)
    kept = pieces[0].shape[1]
    group = max(1, min(concepts, LOW // shard))
    wide = group * shard
    steps = concepts // group
    return pl.pallas_call(
        functools.partial(gram_kernel, shard, group, factor),
        in_specs=[pl.BlockSpec(memory_space=pltpu.VMEM)] * (1 + len(pieces)),
        out_specs=pl.BlockSpec(memory_space=pltpu.HBM),
        out_shape=jax.ShapeDtypeStruct((concepts * shard, kept), jnp.float32),
        scratch_shapes=[
            pltpu.VMEM((tokens, kept), jnp.bfloat16),
            pltpu.VMEM((steps, wide, kept), jnp.float32),
            pltpu.SemaphoreType.DMA((steps + 1,)),
        ],
        compiler_params=pltpu.CompilerParams(vmem_limit_bytes=VMEM_LIMIT),
        cost_estimate=pl.CostEstimate(
            flops=2 * tokens * concepts * shard * kept, bytes_accessed=4 * concepts * shard * kept, transcendentals=0
        ),
        name="gram",
    )(label_row, *pieces)


def encode(values, word_ref):
    size, kept = values.shape
    half = size // 2
    top = jnp.max(jnp.abs(values), axis=1, keepdims=True)
    power = jnp.ceil(jnp.log2(jnp.maximum(top, 2.0 ** -100)))
    whole = jnp.round(values * jnp.exp2(15.0 - power))
    whole = jnp.clip(whole, -32767.0, 32767.0).astype(jnp.int32)
    word = (whole[:half] & 0xFFFF) | (whole[half:] << 16)
    for column in range(kept // LANES):
        word_ref[column * half:(column + 1) * half] = word[:, column * LANES:(column + 1) * LANES]
    group = lax.broadcasted_iota(jnp.int32, (8, LANES), 1) // (LANES * 8 // size)
    tile = jnp.zeros((8, LANES), jnp.int32)
    for at in range(size // 8):
        tile = jnp.where(group == at, power[at * 8:(at + 1) * 8].astype(jnp.int32), tile)
    word_ref[kept // LANES * half:] = tile


def decode(word_ref, size):
    half = size // 2
    columns = word_ref.shape[0] // half
    word = jnp.concatenate([word_ref[at * half:(at + 1) * half] for at in range(columns)], axis=1)
    code = jnp.concatenate([(word << 16) >> 16, word >> 16], axis=0).astype(jnp.float32)
    tile = jnp.exp2(word_ref[columns * half:].astype(jnp.float32) - 15.0)
    lanes = LANES * 8 // size
    scale = jnp.concatenate([tile[:, at * lanes:at * lanes + 1] for at in range(size // 8)], axis=0)
    return code * scale


def first_kernel(stride, keep_ref, got_ref, label_ref, total_ref, there_ref, here_ref, again_ref, label_out):
    size = total_ref.shape[0]
    digit = lax.rem(lax.axis_index("feat") // stride, 2)

    def piece(at):
        span = pl.ds(pl.multiple_of(at * size, size), size)
        return keep_ref[span, :] + got_ref[span, :]

    encode(piece(1 - digit), there_ref)
    again_ref[...] = there_ref[...]
    total = piece(digit)
    total_ref[...] = total
    encode(total, here_ref)
    label_out[...] = label_ref[...]


def square_kernel(total_ref, both_ref, x_ref, z_ref, sum_ref, out_ref):
    size = total_ref.shape[0]
    total = (total_ref[...] + decode(x_ref, size)) + (decode(z_ref, size) + decode(both_ref, size))
    sum_ref[...] = total
    encode(total, out_ref)


def middle_kernel(total_ref, word_ref, sum_ref, out_ref):
    total = total_ref[...] + decode(word_ref, total_ref.shape[0])
    sum_ref[...] = total
    encode(total, out_ref)


def last_kernel(scale, blocks, total_ref, word_ref, *refs):
    label_refs, (label_out, *row_refs) = refs[:-6], refs[-6:]
    size = total_ref.shape[0]
    row = ((total_ref[...] + decode(word_ref, size)) * scale).astype(jnp.bfloat16)
    for row_ref in row_refs:
        row_ref[...] = row
    core = lax.rem(lax.axis_index("feat"), 2)
    digit = lax.rem(lax.axis_index("feat") // 2, 2)
    groups = LANES // size
    lane = lax.broadcasted_iota(jnp.int32, (8, LANES), 1)
    for place in range(0, 2 * len(blocks), groups):
        out = jnp.zeros((8, LANES), jnp.int32)
        for at in range(groups):
            half, (tok, x) = (place + at) // len(blocks), blocks[(place + at) % len(blocks)]
            source = (core ^ half) * 2 * size + (digit ^ x) * size
            moved = pltpu.roll(
                jnp.broadcast_to(label_refs[tok][...], out.shape), lax.rem(at * size - source + LANES, LANES), 1
            )
            out = jnp.where(lane // size == at, moved, out)
        label_out[:, place * size:(place + groups) * size] = out[:1]


def local_call(kernel, name, *operands, out_shape):
    return pl.pallas_call(
        kernel,
        out_shape=out_shape,
        compiler_params=pltpu.CompilerParams(vmem_limit_bytes=VMEM_LIMIT),
        name=name,
    )(*operands)


def swap(array, tok=0, feat=0):
    tok_count, feat_count = lax.axis_size("tok"), lax.axis_size("feat")
    pairs = [
        (f * tok_count + t, (f ^ feat) * tok_count + (t ^ tok))
        for f in range(feat_count)
        for t in range(tok_count)
    ]
    return lax.ppermute(array, ("feat", "tok"), pairs)


def body(features, signs, columns, labels):
    rows, width = features.shape
    feat_count = lax.axis_size("feat")
    feat_index = lax.axis_index("feat")
    tok_count = lax.axis_size("tok")
    kept = columns.shape[0]
    shard = kept // feat_count
    size = rows // 4
    total_type = jax.ShapeDtypeStruct((size, kept), jnp.float32)
    word_type = jax.ShapeDtypeStruct((kept // LANES * (size // 2) + 8, LANES), jnp.int32)
    row_type = jax.ShapeDtypeStruct((size, kept), jnp.bfloat16)
    label_type = jax.ShapeDtypeStruct((1, rows), jnp.int32)

    keep, got = partial_halves(features, signs, columns, feat_count)
    total, there, here, again, label = local_call(
        functools.partial(first_kernel, 2),
        "first_split",
        keep,
        got,
        labels.reshape(1, rows),
        out_shape=[total_type, word_type, word_type, word_type, label_type],
    )
    both = swap(again, feat=6)
    x_word = swap(there, feat=2)
    z_word = swap(here, feat=4)
    all_labels = [label] + [swap(label, tok=tok) for tok in range(1, tok_count)]
    total, word = local_call(
        square_kernel, "add_square", total, both, x_word, z_word, out_shape=[total_type, word_type]
    )
    word = swap(word, feat=8)
    stride = 16
    while stride < feat_count:
        total, word = local_call(middle_kernel, "add_encode", total, word, out_shape=[total_type, word_type])
        word = swap(word, feat=stride)
        stride *= 2

    blocks = [(0, 0)]
    stride = 2
    while stride < tok_count:
        blocks = blocks + [(tok ^ stride, x) for tok, x in blocks]
        stride *= 2
    blocks = [(tok ^ flip, x) for flip, x in ((0, 0), (1, 1), (0, 1), (1, 0)) for tok, _ in blocks]
    scale = 1.0 / math.sqrt(width * feat_count)
    label_row, *copies = local_call(
        functools.partial(last_kernel, scale, blocks),
        "sketch_rows",
        total,
        word,
        *all_labels,
        out_shape=[jax.ShapeDtypeStruct((1, 2 * len(blocks) * size), jnp.int32)] + [row_type] * 5,
    )
    stride = 2
    while stride < tok_count:
        copies = [jnp.concatenate([copies[0], swap(copies[0], tok=stride)], axis=0)] * 5
        stride *= 2
    received = [swap(copies[0], tok=1, feat=2), swap(copies[1], feat=2), swap(copies[2], tok=1)]
    last = swap(copies[3], tok=1, feat=1)
    ours = copies[4:] + received
    theirs = [swap(block, feat=1) for block in ours[:3]] + [last]
    concepts = C // tok_count
    gram = gram_blocks(ours + theirs, label_row, concepts, shard, C / (rows * tok_count))
    return gram.reshape(concepts, shard, kept)


def solution(mesh):
    in_specs = (P("tok", "feat"), P("feat"), P(), P("tok", None))
    out_specs = P("tok", "feat", None)
    return jax.shard_map(body, mesh=mesh, in_specs=in_specs, out_specs=out_specs, check_vma=False)
```

```python
import functools
import math

import jax
import jax.numpy as jnp
from jax import lax
from jax.experimental import pallas as pl
from jax.experimental.pallas import tpu as pltpu
from jax.sharding import PartitionSpec as P

C = 32
LOW = 256
LANES = 128
VMEM_LIMIT = 48 * 1024 * 1024


def parity_sign(number, bit_count):
    shift = 1
    while shift < bit_count:
        shift *= 2
    while shift > 1:
        shift //= 2
        number = number ^ (number >> shift)
    return (1 - 2 * (number & 1)).astype(jnp.float32)


def add_products(x_ref, sign_ref, low, high, out_ref, part, wide, make_tables=None):
    rows, kept = out_ref.shape
    blocks = wide // LOW
    stack = []
    for block in range(part * blocks, (part + 1) * blocks):
        cols = slice(block * LOW, (block + 1) * LOW)
        stack.append(x_ref[:, cols] * sign_ref[:, cols].astype(jnp.bfloat16))
    stack = jnp.concatenate(stack, axis=0)
    for group in range(kept // LOW):
        cols = slice(group * LOW, (group + 1) * LOW)
        if make_tables is not None:
            make_tables(cols)
        products = jnp.dot(stack, low[:, cols], preferred_element_type=jnp.float32)
        total = None
        for at in range(blocks):
            row = part * blocks + at
            term = products[at * rows:(at + 1) * rows] * high[row:row + 1, cols]
            total = term if total is None else total + term
        if part > 0:
            total = total + out_ref[:, cols]
        out_ref[:, cols] = total


def send_kernel(total_bits, parts, x_hbm, s_hbm, col_hbm, send_ref, x_keep, signs, low, high, x_buf, col_buf, sems):
    half, kept = send_ref.shape
    wide = x_hbm.shape[1] // parts
    me = lax.axis_index("feat")
    mine = lax.rem(me, 2)
    col_copy = pltpu.make_async_copy(col_hbm, col_buf, sems.at[parts])
    sign_copy = pltpu.make_async_copy(s_hbm, signs, sems.at[parts + 1])
    col_copy.start()
    sign_copy.start()
    copies = []
    for part in range(parts):
        cols = pl.ds(part * wide, wide)
        rows = pl.ds(pl.multiple_of((1 - mine) * half, half), half)
        copies.append(pltpu.make_async_copy(x_hbm.at[rows, cols], x_buf.at[:, cols], sems.at[part]))
        copies[-1].start()
    rows = pl.ds(pl.multiple_of(mine * half, half), half)
    keep_copy = pltpu.make_async_copy(x_hbm.at[rows, :], x_keep, sems.at[parts + 2])
    keep_copy.start()

    def make_tables(cols):
        col = col_buf[:, cols]
        index = lax.broadcasted_iota(jnp.int32, (16, LOW), 0)
        inner = parity_sign(index & col, 4)
        outer = parity_sign(index & (col >> 4), 4)
        for row in range(LOW // 16):
            low[row * 16:(row + 1) * 16, cols] = (inner * outer[row:row + 1]).astype(jnp.bfloat16)
        index = lax.broadcasted_iota(jnp.int32, (high.shape[0], LOW), 0) + me * high.shape[0]
        high[:, cols] = parity_sign(index & (col >> 8), total_bits - 8)

    col_copy.wait()
    sign_copy.wait()
    for part in range(parts):
        copies[part].wait()
        add_products(x_buf, signs, low, high, send_ref, part, wide, make_tables if part == 0 else None)
    keep_copy.wait()


def keep_kernel(parts, x_keep, signs, low, high, keep_ref):
    wide = x_keep.shape[1] // parts
    for part in range(parts):
        add_products(x_keep, signs, low, high, keep_ref, part, wide)


def partial_halves(features, signs, columns, feat_count):
    rows, width = features.shape
    kept = columns.shape[0]
    parts = max(1, width // 2048)
    half = rows // 2
    total_bits = (width * feat_count).bit_length() - 1
    params = pltpu.CompilerParams(vmem_limit_bytes=VMEM_LIMIT)
    cost = pl.CostEstimate(
        flops=2 * half * width * kept, bytes_accessed=2 * rows * width + 4 * half * kept, transcendentals=0
    )
    total_type = jax.ShapeDtypeStruct((half, kept), jnp.float32)
    send, *held = pl.pallas_call(
        functools.partial(send_kernel, total_bits, parts),
        in_specs=[pl.BlockSpec(memory_space=pltpu.HBM)] * 3,
        out_specs=[pl.BlockSpec(memory_space=pltpu.VMEM)] * 5,
        out_shape=[
            total_type,
            jax.ShapeDtypeStruct((half, width), jnp.bfloat16),
            jax.ShapeDtypeStruct((1, width), jnp.int32),
            jax.ShapeDtypeStruct((LOW, kept), jnp.bfloat16),
            jax.ShapeDtypeStruct((width // LOW, kept), jnp.float32),
        ],
        scratch_shapes=[
            pltpu.VMEM((half, width), jnp.bfloat16),
            pltpu.VMEM((1, kept), jnp.int32),
            pltpu.SemaphoreType.DMA((parts + 3,)),
        ],
        compiler_params=params,
        cost_estimate=cost,
        name="partial_sent",
    )(*(
        pltpu.with_memory_space_constraint(operand, pltpu.HBM)
        for operand in (features, signs.reshape(1, width), columns.reshape(1, kept))
    ))
    got = swap(send, feat=1)
    keep = pl.pallas_call(
        functools.partial(keep_kernel, parts),
        out_shape=total_type,
        compiler_params=params,
        cost_estimate=cost,
        name="partial_kept",
    )(*held)
    return keep, got


def gram_kernel(shard, group, factor, label_ref, *refs):
    pieces, (out_hbm, rows, blocks, sems) = refs[:-4], refs[-4:]
    steps, wide, kept = blocks.shape
    place = 0
    for piece in pieces:
        rows[place:place + piece.shape[0]] = piece[...]
        place += piece.shape[0]
    first = lax.axis_index("feat") * shard
    start = pl.multiple_of(first // LANES * LANES, LANES)
    window = rows[:, pl.ds(start, LANES)].astype(jnp.float32) * factor
    window = pltpu.roll(window, lax.rem(LANES - (first - start), LANES), 1)
    own = jnp.concatenate([window.T[:shard]] * group, axis=0)
    label = label_ref[...] - lax.broadcasted_iota(jnp.int32, own.shape, 0) // shard
    base = lax.axis_index("tok") * steps * group
    copies = []
    for step in range(steps):
        chosen = jnp.where(label == base + step * group, own, 0.0).astype(jnp.bfloat16)
        size = kept if step < steps - 1 else LOW
        for first in range(0, kept, size):
            cols = slice(first, first + size)
            blocks[step, :, cols] = jnp.dot(chosen, rows[:, cols], preferred_element_type=jnp.float32)
            copies.append(
                pltpu.make_async_copy(
                    blocks.at[step, :, pl.ds(first, size)],
                    out_hbm.at[pl.ds(step * wide, wide), pl.ds(first, size)],
                    sems.at[len(copies)],
                )
            )
            copies[-1].start()
    for copy in copies:
        copy.wait()


def gram_blocks(pieces, label_row, concepts, shard, factor):
    tokens = sum(piece.shape[0] for piece in pieces)
    kept = pieces[0].shape[1]
    group = max(1, min(concepts, LOW // shard))
    wide = group * shard
    steps = concepts // group
    return pl.pallas_call(
        functools.partial(gram_kernel, shard, group, factor),
        in_specs=[pl.BlockSpec(memory_space=pltpu.VMEM)] * (1 + len(pieces)),
        out_specs=pl.BlockSpec(memory_space=pltpu.HBM),
        out_shape=jax.ShapeDtypeStruct((concepts * shard, kept), jnp.float32),
        scratch_shapes=[
            pltpu.VMEM((tokens, kept), jnp.bfloat16),
            pltpu.VMEM((steps, wide, kept), jnp.float32),
            pltpu.SemaphoreType.DMA((steps - 1 + kept // LOW,)),
        ],
        compiler_params=pltpu.CompilerParams(vmem_limit_bytes=VMEM_LIMIT),
        cost_estimate=pl.CostEstimate(
            flops=2 * tokens * concepts * shard * kept, bytes_accessed=4 * concepts * shard * kept, transcendentals=0
        ),
        name="gram",
    )(label_row, *pieces)


def encode(values, word_ref):
    size, kept = values.shape
    half = size // 2
    top = jnp.max(jnp.abs(values), axis=1, keepdims=True)
    power = jnp.ceil(jnp.log2(jnp.maximum(top, 2.0 ** -100)))
    whole = jnp.round(values * jnp.exp2(15.0 - power))
    whole = jnp.clip(whole, -32767.0, 32767.0).astype(jnp.int32)
    word = (whole[:half] & 0xFFFF) | (whole[half:] << 16)
    for column in range(kept // LANES):
        word_ref[column * half:(column + 1) * half] = word[:, column * LANES:(column + 1) * LANES]
    group = lax.broadcasted_iota(jnp.int32, (8, LANES), 1) // (LANES * 8 // size)
    tile = jnp.zeros((8, LANES), jnp.int32)
    for at in range(size // 8):
        tile = jnp.where(group == at, power[at * 8:(at + 1) * 8].astype(jnp.int32), tile)
    word_ref[kept // LANES * half:] = tile


def decode(word_ref, size):
    half = size // 2
    columns = word_ref.shape[0] // half
    word = jnp.concatenate([word_ref[at * half:(at + 1) * half] for at in range(columns)], axis=1)
    code = jnp.concatenate([(word << 16) >> 16, word >> 16], axis=0).astype(jnp.float32)
    tile = jnp.exp2(word_ref[columns * half:].astype(jnp.float32) - 15.0)
    lanes = LANES * 8 // size
    scale = jnp.concatenate([tile[:, at * lanes:at * lanes + 1] for at in range(size // 8)], axis=0)
    return code * scale


def first_kernel(stride, keep_ref, got_ref, label_ref, total_ref, there_ref, here_ref, again_ref, label_out):
    size = total_ref.shape[0]
    digit = lax.rem(lax.axis_index("feat") // stride, 2)

    def piece(at):
        span = pl.ds(pl.multiple_of(at * size, size), size)
        return keep_ref[span, :] + got_ref[span, :]

    encode(piece(1 - digit), there_ref)
    again_ref[...] = there_ref[...]
    total = piece(digit)
    total_ref[...] = total
    encode(total, here_ref)
    label_out[...] = label_ref[...]


def square_kernel(total_ref, both_ref, x_ref, z_ref, sum_ref, out_ref):
    size = total_ref.shape[0]
    total = (total_ref[...] + decode(x_ref, size)) + (decode(z_ref, size) + decode(both_ref, size))
    sum_ref[...] = total
    encode(total, out_ref)


def middle_kernel(total_ref, word_ref, sum_ref, out_ref):
    total = total_ref[...] + decode(word_ref, total_ref.shape[0])
    sum_ref[...] = total
    encode(total, out_ref)


def last_kernel(scale, blocks, total_ref, word_ref, *refs):
    label_refs, (label_out, *row_refs) = refs[:-6], refs[-6:]
    size = total_ref.shape[0]
    row = ((total_ref[...] + decode(word_ref, size)) * scale).astype(jnp.bfloat16)
    for row_ref in row_refs:
        row_ref[...] = row
    core = lax.rem(lax.axis_index("feat"), 2)
    digit = lax.rem(lax.axis_index("feat") // 2, 2)
    groups = LANES // size
    lane = lax.broadcasted_iota(jnp.int32, (8, LANES), 1)
    for place in range(0, 2 * len(blocks), groups):
        out = jnp.zeros((8, LANES), jnp.int32)
        for at in range(groups):
            half, (tok, x) = (place + at) // len(blocks), blocks[(place + at) % len(blocks)]
            source = (core ^ half) * 2 * size + (digit ^ x) * size
            moved = pltpu.roll(
                jnp.broadcast_to(label_refs[tok][...], out.shape), lax.rem(at * size - source + LANES, LANES), 1
            )
            out = jnp.where(lane // size == at, moved, out)
        label_out[:, place * size:(place + groups) * size] = out[:1]


def local_call(kernel, name, *operands, out_shape):
    return pl.pallas_call(
        kernel,
        out_shape=out_shape,
        compiler_params=pltpu.CompilerParams(vmem_limit_bytes=VMEM_LIMIT),
        name=name,
    )(*operands)


def swap(array, tok=0, feat=0):
    tok_count, feat_count = lax.axis_size("tok"), lax.axis_size("feat")
    pairs = [
        (f * tok_count + t, (f ^ feat) * tok_count + (t ^ tok))
        for f in range(feat_count)
        for t in range(tok_count)
    ]
    return lax.ppermute(array, ("feat", "tok"), pairs)


def body(features, signs, columns, labels):
    rows, width = features.shape
    feat_count = lax.axis_size("feat")
    feat_index = lax.axis_index("feat")
    tok_count = lax.axis_size("tok")
    kept = columns.shape[0]
    shard = kept // feat_count
    size = rows // 4
    total_type = jax.ShapeDtypeStruct((size, kept), jnp.float32)
    word_type = jax.ShapeDtypeStruct((kept // LANES * (size // 2) + 8, LANES), jnp.int32)
    row_type = jax.ShapeDtypeStruct((size, kept), jnp.bfloat16)
    label_type = jax.ShapeDtypeStruct((1, rows), jnp.int32)

    keep, got = partial_halves(features, signs, columns, feat_count)
    total, there, here, again, label = local_call(
        functools.partial(first_kernel, 2),
        "first_split",
        keep,
        got,
        labels.reshape(1, rows),
        out_shape=[total_type, word_type, word_type, word_type, label_type],
    )
    both = swap(again, feat=6)
    x_word = swap(there, feat=2)
    z_word = swap(here, feat=4)
    all_labels = [label] + [swap(label, tok=tok) for tok in range(1, tok_count)]
    total, word = local_call(
        square_kernel, "add_square", total, both, x_word, z_word, out_shape=[total_type, word_type]
    )
    word = swap(word, feat=8)
    stride = 16
    while stride < feat_count:
        total, word = local_call(middle_kernel, "add_encode", total, word, out_shape=[total_type, word_type])
        word = swap(word, feat=stride)
        stride *= 2

    blocks = [(0, 0)]
    stride = 2
    while stride < tok_count:
        blocks = blocks + [(tok ^ stride, x) for tok, x in blocks]
        stride *= 2
    blocks = [(tok ^ flip, x) for flip, x in ((0, 0), (1, 1), (0, 1), (1, 0)) for tok, _ in blocks]
    scale = 1.0 / math.sqrt(width * feat_count)
    label_row, *copies = local_call(
        functools.partial(last_kernel, scale, blocks),
        "sketch_rows",
        total,
        word,
        *all_labels,
        out_shape=[jax.ShapeDtypeStruct((1, 2 * len(blocks) * size), jnp.int32)] + [row_type] * 5,
    )
    stride = 2
    while stride < tok_count:
        copies = [jnp.concatenate([copies[0], swap(copies[0], tok=stride)], axis=0)] * 5
        stride *= 2
    received = [swap(copies[0], tok=1, feat=2), swap(copies[1], feat=2), swap(copies[2], tok=1)]
    last = swap(copies[3], tok=1, feat=1)
    ours = copies[4:] + received
    theirs = [swap(block, feat=1) for block in ours[:3]] + [last]
    concepts = C // tok_count
    gram = gram_blocks(ours + theirs, label_row, concepts, shard, C / (rows * tok_count))
    return gram.reshape(concepts, shard, kept)


def solution(mesh):
    in_specs = (P("tok", "feat"), P("feat"), P(), P("tok", None))
    out_specs = P("tok", "feat", None)
    return jax.shard_map(body, mesh=mesh, in_specs=in_specs, out_specs=out_specs, check_vma=False)
```

```python
import functools
import math

import jax
import jax.numpy as jnp
from jax import lax
from jax.experimental import pallas as pl
from jax.experimental.pallas import tpu as pltpu
from jax.sharding import PartitionSpec as P

C = 32
LOW = 256
LANES = 128
VMEM_LIMIT = 48 * 1024 * 1024


def parity_sign(number, bit_count):
    shift = 1
    while shift < bit_count:
        shift *= 2
    while shift > 1:
        shift //= 2
        number = number ^ (number >> shift)
    return (1 - 2 * (number & 1)).astype(jnp.float32)


def add_products(x_ref, sign_ref, low, high, out_ref, part, wide):
    rows, kept = out_ref.shape
    blocks = wide // LOW
    stack = []
    for block in range(part * blocks, (part + 1) * blocks):
        cols = slice(block * LOW, (block + 1) * LOW)
        stack.append(x_ref[:, cols] * sign_ref[:, cols].astype(jnp.bfloat16))
    stack = jnp.concatenate(stack, axis=0)
    for group in range(kept // LOW):
        cols = slice(group * LOW, (group + 1) * LOW)
        products = jnp.dot(stack, low[:, cols], preferred_element_type=jnp.float32)
        total = None
        for at in range(blocks):
            row = part * blocks + at
            term = products[at * rows:(at + 1) * rows] * high[row:row + 1, cols]
            total = term if total is None else total + term
        if part > 0:
            total = total + out_ref[:, cols]
        out_ref[:, cols] = total


def send_kernel(total_bits, parts, x_hbm, s_hbm, col_hbm, send_ref, x_keep, signs, low, high, x_buf, col_buf, sems):
    half, kept = send_ref.shape
    wide = x_hbm.shape[1] // parts
    me = lax.axis_index("feat")
    mine = lax.rem(me, 2)
    col_copy = pltpu.make_async_copy(col_hbm, col_buf, sems.at[parts])
    sign_copy = pltpu.make_async_copy(s_hbm, signs, sems.at[parts + 1])
    col_copy.start()
    sign_copy.start()
    copies = []
    for part in range(parts):
        cols = pl.ds(part * wide, wide)
        rows = pl.ds(pl.multiple_of((1 - mine) * half, half), half)
        copies.append(pltpu.make_async_copy(x_hbm.at[rows, cols], x_buf.at[:, cols], sems.at[part]))
        copies[-1].start()
    rows = pl.ds(pl.multiple_of(mine * half, half), half)
    keep_copy = pltpu.make_async_copy(x_hbm.at[rows, :], x_keep, sems.at[parts + 2])
    keep_copy.start()
    col_copy.wait()
    col = col_buf[...]
    index = lax.broadcasted_iota(jnp.int32, (16, kept), 0)
    inner = parity_sign(index & col, 4)
    outer = parity_sign(index & (col >> 4), 4)
    for row in range(LOW // 16):
        low[row * 16:(row + 1) * 16] = (inner * outer[row:row + 1]).astype(jnp.bfloat16)
    high_index = lax.broadcasted_iota(jnp.int32, high.shape, 0) + me * high.shape[0]
    high[...] = parity_sign(high_index & (col >> 8), total_bits - 8)
    sign_copy.wait()
    for part in range(parts):
        copies[part].wait()
        add_products(x_buf, signs, low, high, send_ref, part, wide)
    keep_copy.wait()


def keep_kernel(parts, x_keep, signs, low, high, keep_ref):
    wide = x_keep.shape[1] // parts
    for part in range(parts):
        add_products(x_keep, signs, low, high, keep_ref, part, wide)


def partial_halves(features, signs, columns, feat_count):
    rows, width = features.shape
    kept = columns.shape[0]
    parts = max(1, width // 2048)
    half = rows // 2
    total_bits = (width * feat_count).bit_length() - 1
    params = pltpu.CompilerParams(vmem_limit_bytes=VMEM_LIMIT)
    cost = pl.CostEstimate(
        flops=2 * half * width * kept, bytes_accessed=2 * rows * width + 4 * half * kept, transcendentals=0
    )
    total_type = jax.ShapeDtypeStruct((half, kept), jnp.float32)
    send, *held = pl.pallas_call(
        functools.partial(send_kernel, total_bits, parts),
        in_specs=[pl.BlockSpec(memory_space=pltpu.HBM)] * 3,
        out_specs=[pl.BlockSpec(memory_space=pltpu.VMEM)] * 5,
        out_shape=[
            total_type,
            jax.ShapeDtypeStruct((half, width), jnp.bfloat16),
            jax.ShapeDtypeStruct((1, width), jnp.int32),
            jax.ShapeDtypeStruct((LOW, kept), jnp.bfloat16),
            jax.ShapeDtypeStruct((width // LOW, kept), jnp.float32),
        ],
        scratch_shapes=[
            pltpu.VMEM((half, width), jnp.bfloat16),
            pltpu.VMEM((1, kept), jnp.int32),
            pltpu.SemaphoreType.DMA((parts + 3,)),
        ],
        compiler_params=params,
        cost_estimate=cost,
        name="partial_sent",
    )(*(
        pltpu.with_memory_space_constraint(operand, pltpu.HBM)
        for operand in (features, signs.reshape(1, width), columns.reshape(1, kept))
    ))
    got = swap(send, feat=1)
    keep = pl.pallas_call(
        functools.partial(keep_kernel, parts),
        out_shape=total_type,
        compiler_params=params,
        cost_estimate=cost,
        name="partial_kept",
    )(*held)
    return keep, got


def gram_kernel(shard, group, factor, label_ref, *refs):
    pieces, (out_hbm, rows, blocks, sems) = refs[:-4], refs[-4:]
    steps, wide, _ = blocks.shape
    place = 0
    for piece in pieces:
        rows[place:place + piece.shape[0]] = piece[...]
        place += piece.shape[0]
    first = lax.axis_index("feat") * shard
    start = pl.multiple_of(first // LANES * LANES, LANES)
    window = rows[:, pl.ds(start, LANES)].astype(jnp.float32) * factor
    window = pltpu.roll(window, lax.rem(LANES - (first - start), LANES), 1)
    own = jnp.concatenate([window.T[:shard]] * group, axis=0)
    label = label_ref[...] - lax.broadcasted_iota(jnp.int32, own.shape, 0) // shard
    base = lax.axis_index("tok") * steps * group
    copies = []
    for step in range(steps):
        chosen = jnp.where(label == base + step * group, own, 0.0).astype(jnp.bfloat16)
        blocks[step] = jnp.dot(chosen, rows[...], preferred_element_type=jnp.float32)
        copies.append(
            pltpu.make_async_copy(blocks.at[step], out_hbm.at[pl.ds(step * wide, wide), :], sems.at[step])
        )
        copies[-1].start()
    for copy in copies:
        copy.wait()


def gram_blocks(pieces, label_row, concepts, shard, factor):
    tokens = sum(piece.shape[0] for piece in pieces)
    kept = pieces[0].shape[1]
    group = max(1, min(concepts, LOW // shard))
    wide = group * shard
    steps = concepts // group
    return pl.pallas_call(
        functools.partial(gram_kernel, shard, group, factor),
        in_specs=[pl.BlockSpec(memory_space=pltpu.VMEM)] * (1 + len(pieces)),
        out_specs=pl.BlockSpec(memory_space=pltpu.HBM),
        out_shape=jax.ShapeDtypeStruct((concepts * shard, kept), jnp.float32),
        scratch_shapes=[
            pltpu.VMEM((tokens, kept), jnp.bfloat16),
            pltpu.VMEM((steps, wide, kept), jnp.float32),
            pltpu.SemaphoreType.DMA((steps,)),
        ],
        compiler_params=pltpu.CompilerParams(vmem_limit_bytes=VMEM_LIMIT),
        cost_estimate=pl.CostEstimate(
            flops=2 * tokens * concepts * shard * kept, bytes_accessed=4 * concepts * shard * kept, transcendentals=0
        ),
        name="gram",
    )(label_row, *pieces)


def encode(values, word_ref):
    size, kept = values.shape
    half = size // 2
    top = jnp.max(jnp.abs(values), axis=1, keepdims=True)
    power = jnp.ceil(jnp.log2(jnp.maximum(top, 2.0 ** -100)))
    whole = jnp.round(values * jnp.exp2(15.0 - power))
    whole = jnp.clip(whole, -32767.0, 32767.0).astype(jnp.int32)
    word = (whole[:half] & 0xFFFF) | (whole[half:] << 16)
    for column in range(kept // LANES):
        word_ref[column * half:(column + 1) * half] = word[:, column * LANES:(column + 1) * LANES]
    group = lax.broadcasted_iota(jnp.int32, (8, LANES), 1) // (LANES * 8 // size)
    tile = jnp.zeros((8, LANES), jnp.int32)
    for at in range(size // 8):
        tile = jnp.where(group == at, power[at * 8:(at + 1) * 8].astype(jnp.int32), tile)
    word_ref[kept // LANES * half:] = tile


def decode(word_ref, size):
    half = size // 2
    columns = word_ref.shape[0] // half
    word = jnp.concatenate([word_ref[at * half:(at + 1) * half] for at in range(columns)], axis=1)
    code = jnp.concatenate([(word << 16) >> 16, word >> 16], axis=0).astype(jnp.float32)
    tile = jnp.exp2(word_ref[columns * half:].astype(jnp.float32) - 15.0)
    lanes = LANES * 8 // size
    scale = jnp.concatenate([tile[:, at * lanes:at * lanes + 1] for at in range(size // 8)], axis=0)
    return code * scale


def first_kernel(stride, keep_ref, got_ref, label_ref, total_ref, there_ref, here_ref, again_ref, label_out):
    size = total_ref.shape[0]
    digit = lax.rem(lax.axis_index("feat") // stride, 2)

    def piece(at):
        span = pl.ds(pl.multiple_of(at * size, size), size)
        return keep_ref[span, :] + got_ref[span, :]

    encode(piece(1 - digit), there_ref)
    again_ref[...] = there_ref[...]
    total = piece(digit)
    total_ref[...] = total
    encode(total, here_ref)
    label_out[...] = label_ref[...]


def square_kernel(total_ref, both_ref, z_ref, x_ref, sum_ref, out_ref):
    size = total_ref.shape[0]
    total = (total_ref[...] + decode(x_ref, size)) + (decode(z_ref, size) + decode(both_ref, size))
    sum_ref[...] = total
    encode(total, out_ref)


def middle_kernel(total_ref, word_ref, sum_ref, out_ref):
    total = total_ref[...] + decode(word_ref, total_ref.shape[0])
    sum_ref[...] = total
    encode(total, out_ref)


def last_kernel(scale, blocks, total_ref, word_ref, *refs):
    label_refs, (label_out, *row_refs) = refs[:-6], refs[-6:]
    size = total_ref.shape[0]
    row = ((total_ref[...] + decode(word_ref, size)) * scale).astype(jnp.bfloat16)
    for row_ref in row_refs:
        row_ref[...] = row
    core = lax.rem(lax.axis_index("feat"), 2)
    digit = lax.rem(lax.axis_index("feat") // 2, 2)
    groups = LANES // size
    lane = lax.broadcasted_iota(jnp.int32, (8, LANES), 1)
    for place in range(0, 2 * len(blocks), groups):
        out = jnp.zeros((8, LANES), jnp.int32)
        for at in range(groups):
            half, (tok, x) = (place + at) // len(blocks), blocks[(place + at) % len(blocks)]
            source = (core ^ half) * 2 * size + (digit ^ x) * size
            moved = pltpu.roll(
                jnp.broadcast_to(label_refs[tok][...], out.shape), lax.rem(at * size - source + LANES, LANES), 1
            )
            out = jnp.where(lane // size == at, moved, out)
        label_out[:, place * size:(place + groups) * size] = out[:1]


def local_call(kernel, name, *operands, out_shape):
    return pl.pallas_call(
        kernel,
        out_shape=out_shape,
        compiler_params=pltpu.CompilerParams(vmem_limit_bytes=VMEM_LIMIT),
        name=name,
    )(*operands)


def swap(array, tok=0, feat=0, odd=None):
    tok_count, feat_count = lax.axis_size("tok"), lax.axis_size("feat")
    bits = (feat, odd or feat)
    pairs = [
        (f * tok_count + t, (f ^ bits[f & 1]) * tok_count + (t ^ tok))
        for f in range(feat_count)
        for t in range(tok_count)
    ]
    return lax.ppermute(array, ("feat", "tok"), pairs)


def body(features, signs, columns, labels):
    rows, width = features.shape
    feat_count = lax.axis_size("feat")
    feat_index = lax.axis_index("feat")
    tok_count = lax.axis_size("tok")
    kept = columns.shape[0]
    shard = kept // feat_count
    size = rows // 4
    total_type = jax.ShapeDtypeStruct((size, kept), jnp.float32)
    word_type = jax.ShapeDtypeStruct((kept // LANES * (size // 2) + 8, LANES), jnp.int32)
    row_type = jax.ShapeDtypeStruct((size, kept), jnp.bfloat16)
    label_type = jax.ShapeDtypeStruct((1, rows), jnp.int32)

    keep, got = partial_halves(features, signs, columns, feat_count)
    total, there, here, again, label = local_call(
        functools.partial(first_kernel, 2),
        "first_split",
        keep,
        got,
        labels.reshape(1, rows),
        out_shape=[total_type, word_type, word_type, word_type, label_type],
    )
    both = swap(again, feat=10, odd=6)
    z_word = swap(here, feat=8, odd=4)
    x_word = swap(there, feat=2)
    all_labels = [label] + [swap(label, tok=tok) for tok in range(1, tok_count)]
    total, word = local_call(
        square_kernel, "add_square", total, both, z_word, x_word, out_shape=[total_type, word_type]
    )
    word = swap(word, feat=4, odd=8)
    stride = 16
    while stride < feat_count:
        total, word = local_call(middle_kernel, "add_encode", total, word, out_shape=[total_type, word_type])
        word = swap(word, feat=stride)
        stride *= 2

    blocks = [(0, 0)]
    stride = 2
    while stride < tok_count:
        blocks = blocks + [(tok ^ stride, x) for tok, x in blocks]
        stride *= 2
    blocks = [(tok ^ flip, x) for flip, x in ((0, 0), (1, 1), (0, 1), (1, 0)) for tok, _ in blocks]
    scale = 1.0 / math.sqrt(width * feat_count)
    label_row, *copies = local_call(
        functools.partial(last_kernel, scale, blocks),
        "sketch_rows",
        total,
        word,
        *all_labels,
        out_shape=[jax.ShapeDtypeStruct((1, 2 * len(blocks) * size), jnp.int32)] + [row_type] * 5,
    )
    stride = 2
    while stride < tok_count:
        copies = [jnp.concatenate([copies[0], swap(copies[0], tok=stride)], axis=0)] * 5
        stride *= 2
    received = [swap(copies[0], tok=1, feat=2), swap(copies[1], feat=2), swap(copies[2], tok=1)]
    last = swap(copies[3], tok=1, feat=1)
    ours = copies[4:] + received
    theirs = [swap(block, feat=1) for block in ours[:3]] + [last]
    concepts = C // tok_count
    gram = gram_blocks(ours + theirs, label_row, concepts, shard, C / (rows * tok_count))
    return gram.reshape(concepts, shard, kept)


def solution(mesh):
    in_specs = (P("tok", "feat"), P("feat"), P(), P("tok", None))
    out_specs = P("tok", "feat", None)
    return jax.shard_map(body, mesh=mesh, in_specs=in_specs, out_specs=out_specs, check_vma=False)
```

```python
import functools
import math

import jax
import jax.numpy as jnp
from jax import lax
from jax.experimental import pallas as pl
from jax.experimental.pallas import tpu as pltpu
from jax.sharding import PartitionSpec as P

C = 32
LOW = 256
LANES = 128
VMEM_LIMIT = 48 * 1024 * 1024


def parity_sign(number, bit_count):
    shift = 1
    while shift < bit_count:
        shift *= 2
    while shift > 1:
        shift //= 2
        number = number ^ (number >> shift)
    return (1 - 2 * (number & 1)).astype(jnp.float32)


def add_products(x_ref, sign_ref, low, high, out_ref, part, wide):
    rows, kept = out_ref.shape
    blocks = wide // LOW
    stack = []
    for block in range(part * blocks, (part + 1) * blocks):
        cols = slice(block * LOW, (block + 1) * LOW)
        stack.append(x_ref[:, cols] * sign_ref[:, cols].astype(jnp.bfloat16))
    stack = jnp.concatenate(stack, axis=0)
    for group in range(kept // LOW):
        cols = slice(group * LOW, (group + 1) * LOW)
        products = jnp.dot(stack, low[:, cols], preferred_element_type=jnp.float32)
        total = None
        for at in range(blocks):
            row = part * blocks + at
            term = products[at * rows:(at + 1) * rows] * high[row:row + 1, cols]
            total = term if total is None else total + term
        if part > 0:
            total = total + out_ref[:, cols]
        out_ref[:, cols] = total


def send_kernel(total_bits, parts, x_hbm, s_hbm, col_hbm, send_ref, x_keep, signs, low, high, x_buf, col_buf, sems):
    half, kept = send_ref.shape
    wide = x_hbm.shape[1] // parts
    me = lax.axis_index("feat")
    mine = lax.rem(me, 2)
    col_copy = pltpu.make_async_copy(col_hbm, col_buf, sems.at[parts])
    sign_copy = pltpu.make_async_copy(s_hbm, signs, sems.at[parts + 1])
    col_copy.start()
    sign_copy.start()
    copies = []
    for part in range(parts):
        cols = pl.ds(part * wide, wide)
        rows = pl.ds(pl.multiple_of((1 - mine) * half, half), half)
        copies.append(pltpu.make_async_copy(x_hbm.at[rows, cols], x_buf.at[:, cols], sems.at[part]))
        copies[-1].start()
    rows = pl.ds(pl.multiple_of(mine * half, half), half)
    keep_copy = pltpu.make_async_copy(x_hbm.at[rows, :], x_keep, sems.at[parts + 2])
    keep_copy.start()
    col_copy.wait()
    col = col_buf[...]
    index = lax.broadcasted_iota(jnp.int32, (16, kept), 0)
    inner = parity_sign(index & col, 4)
    outer = parity_sign(index & (col >> 4), 4)
    for row in range(LOW // 16):
        low[row * 16:(row + 1) * 16] = (inner * outer[row:row + 1]).astype(jnp.bfloat16)
    high_index = lax.broadcasted_iota(jnp.int32, high.shape, 0) + me * high.shape[0]
    high[...] = parity_sign(high_index & (col >> 8), total_bits - 8)
    sign_copy.wait()
    for part in range(parts):
        copies[part].wait()
        add_products(x_buf, signs, low, high, send_ref, part, wide)
    keep_copy.wait()


def keep_kernel(parts, x_keep, signs, low, high, keep_ref):
    wide = x_keep.shape[1] // parts
    for part in range(parts):
        add_products(x_keep, signs, low, high, keep_ref, part, wide)


def partial_halves(features, signs, columns, feat_count):
    rows, width = features.shape
    kept = columns.shape[0]
    parts = max(1, width // 2048)
    half = rows // 2
    total_bits = (width * feat_count).bit_length() - 1
    params = pltpu.CompilerParams(vmem_limit_bytes=VMEM_LIMIT)
    cost = pl.CostEstimate(
        flops=2 * half * width * kept, bytes_accessed=2 * rows * width + 4 * half * kept, transcendentals=0
    )
    total_type = jax.ShapeDtypeStruct((half, kept), jnp.float32)
    send, *held = pl.pallas_call(
        functools.partial(send_kernel, total_bits, parts),
        in_specs=[pl.BlockSpec(memory_space=pltpu.HBM)] * 3,
        out_specs=[pl.BlockSpec(memory_space=pltpu.VMEM)] * 5,
        out_shape=[
            total_type,
            jax.ShapeDtypeStruct((half, width), jnp.bfloat16),
            jax.ShapeDtypeStruct((1, width), jnp.int32),
            jax.ShapeDtypeStruct((LOW, kept), jnp.bfloat16),
            jax.ShapeDtypeStruct((width // LOW, kept), jnp.float32),
        ],
        scratch_shapes=[
            pltpu.VMEM((half, width), jnp.bfloat16),
            pltpu.VMEM((1, kept), jnp.int32),
            pltpu.SemaphoreType.DMA((parts + 3,)),
        ],
        compiler_params=params,
        cost_estimate=cost,
        name="partial_sent",
    )(*(
        pltpu.with_memory_space_constraint(operand, pltpu.HBM)
        for operand in (features, signs.reshape(1, width), columns.reshape(1, kept))
    ))
    got = swap(send, feat=1)
    keep = pl.pallas_call(
        functools.partial(keep_kernel, parts),
        out_shape=total_type,
        compiler_params=params,
        cost_estimate=cost,
        name="partial_kept",
    )(*held)
    return keep, got


def gram_kernel(shard, group, factor, *refs):
    pieces, (out_hbm, rows, blocks, sems) = refs[:-4], refs[-4:]
    steps, wide, kept = blocks.shape
    place = 0
    for piece in pieces:
        rows[place:place + piece.shape[0]] = piece[:, :kept]
        place += piece.shape[0]
    first = lax.axis_index("feat") * shard
    start = pl.multiple_of(first // LANES * LANES, LANES)
    window = rows[:, pl.ds(start, LANES)].astype(jnp.float32) * factor
    window = pltpu.roll(window, lax.rem(LANES - (first - start), LANES), 1)
    own = jnp.concatenate([window.T[:shard]] * group, axis=0)
    named = jnp.concatenate([piece[:, kept:].astype(jnp.float32) for piece in pieces], axis=0).T[:1]
    label = named.astype(jnp.int32) - lax.broadcasted_iota(jnp.int32, own.shape, 0) // shard
    base = lax.axis_index("tok") * steps * group
    copies = []
    for step in range(steps):
        chosen = jnp.where(label == base + step * group, own, 0.0).astype(jnp.bfloat16)
        blocks[step] = jnp.dot(chosen, rows[...], preferred_element_type=jnp.float32)
        copies.append(
            pltpu.make_async_copy(blocks.at[step], out_hbm.at[pl.ds(step * wide, wide), :], sems.at[step])
        )
        copies[-1].start()
    for copy in copies:
        copy.wait()


def gram_blocks(pieces, concepts, shard, factor):
    tokens = sum(piece.shape[0] for piece in pieces)
    kept = pieces[0].shape[1] - LANES
    group = max(1, min(concepts, LOW // shard))
    wide = group * shard
    steps = concepts // group
    return pl.pallas_call(
        functools.partial(gram_kernel, shard, group, factor),
        in_specs=[pl.BlockSpec(memory_space=pltpu.VMEM)] * len(pieces),
        out_specs=pl.BlockSpec(memory_space=pltpu.HBM),
        out_shape=jax.ShapeDtypeStruct((concepts * shard, kept), jnp.float32),
        scratch_shapes=[
            pltpu.VMEM((tokens, kept), jnp.bfloat16),
            pltpu.VMEM((steps, wide, kept), jnp.float32),
            pltpu.SemaphoreType.DMA((steps,)),
        ],
        compiler_params=pltpu.CompilerParams(vmem_limit_bytes=VMEM_LIMIT),
        cost_estimate=pl.CostEstimate(
            flops=2 * tokens * concepts * shard * kept, bytes_accessed=4 * concepts * shard * kept, transcendentals=0
        ),
        name="gram",
    )(*pieces)


def encode(values, word_ref):
    size, kept = values.shape
    half = size // 2
    top = jnp.max(jnp.abs(values), axis=1, keepdims=True)
    power = jnp.ceil(jnp.log2(jnp.maximum(top, 2.0 ** -100)))
    whole = jnp.round(values * jnp.exp2(15.0 - power))
    whole = jnp.clip(whole, -32767.0, 32767.0).astype(jnp.int32)
    word = (whole[:half] & 0xFFFF) | (whole[half:] << 16)
    for column in range(kept // LANES):
        word_ref[column * half:(column + 1) * half] = word[:, column * LANES:(column + 1) * LANES]
    group = lax.broadcasted_iota(jnp.int32, (8, LANES), 1) // (LANES * 8 // size)
    tile = jnp.zeros((8, LANES), jnp.int32)
    for at in range(size // 8):
        tile = jnp.where(group == at, power[at * 8:(at + 1) * 8].astype(jnp.int32), tile)
    word_ref[kept // LANES * half:] = tile


def decode(word_ref, size):
    half = size // 2
    columns = word_ref.shape[0] // half
    word = jnp.concatenate([word_ref[at * half:(at + 1) * half] for at in range(columns)], axis=1)
    code = jnp.concatenate([(word << 16) >> 16, word >> 16], axis=0).astype(jnp.float32)
    tile = jnp.exp2(word_ref[columns * half:].astype(jnp.float32) - 15.0)
    lanes = LANES * 8 // size
    scale = jnp.concatenate([tile[:, at * lanes:at * lanes + 1] for at in range(size // 8)], axis=0)
    return code * scale


def first_kernel(stride, keep_ref, got_ref, total_ref, there_ref, here_ref, again_ref):
    size = total_ref.shape[0]
    digit = lax.rem(lax.axis_index("feat") // stride, 2)

    def piece(at):
        span = pl.ds(pl.multiple_of(at * size, size), size)
        return keep_ref[span, :] + got_ref[span, :]

    encode(piece(1 - digit), there_ref)
    again_ref[...] = there_ref[...]
    total = piece(digit)
    total_ref[...] = total
    encode(total, here_ref)


def square_kernel(total_ref, both_ref, z_ref, x_ref, sum_ref, out_ref):
    size = total_ref.shape[0]
    total = (total_ref[...] + decode(x_ref, size)) + (decode(z_ref, size) + decode(both_ref, size))
    sum_ref[...] = total
    encode(total, out_ref)


def middle_kernel(total_ref, word_ref, sum_ref, out_ref):
    total = total_ref[...] + decode(word_ref, total_ref.shape[0])
    sum_ref[...] = total
    encode(total, out_ref)


def last_kernel(scale, total_ref, word_ref, label_ref, *row_refs):
    size, kept = total_ref.shape
    row = ((total_ref[...] + decode(word_ref, size)) * scale).astype(jnp.bfloat16)
    me = lax.axis_index("feat")
    first = lax.rem(me, 2) * 2 * size + lax.rem(me // 2, 2) * size
    label = jnp.broadcast_to(label_ref[...].astype(jnp.float32), (8, LANES))
    label = pltpu.roll(label, lax.rem(LANES - first, LANES), 1)
    label = jnp.broadcast_to(label[:1], (LANES, LANES)).T[:size].astype(jnp.bfloat16)
    for row_ref in row_refs:
        row_ref[:, :kept] = row
        row_ref[:, kept:] = label


def local_call(kernel, name, *operands, out_shape):
    return pl.pallas_call(
        kernel,
        out_shape=out_shape,
        compiler_params=pltpu.CompilerParams(vmem_limit_bytes=VMEM_LIMIT),
        name=name,
    )(*operands)


def swap(array, tok=0, feat=0, odd=None):
    tok_count, feat_count = lax.axis_size("tok"), lax.axis_size("feat")
    bits = (feat, odd or feat)
    pairs = [
        (f * tok_count + t, (f ^ bits[f & 1]) * tok_count + (t ^ tok))
        for f in range(feat_count)
        for t in range(tok_count)
    ]
    return lax.ppermute(array, ("feat", "tok"), pairs)


def body(features, signs, columns, labels):
    rows, width = features.shape
    feat_count = lax.axis_size("feat")
    tok_count = lax.axis_size("tok")
    kept = columns.shape[0]
    shard = kept // feat_count
    size = rows // 4
    total_type = jax.ShapeDtypeStruct((size, kept), jnp.float32)
    word_type = jax.ShapeDtypeStruct((kept // LANES * (size // 2) + 8, LANES), jnp.int32)
    row_type = jax.ShapeDtypeStruct((size, kept + LANES), jnp.bfloat16)

    keep, got = partial_halves(features, signs, columns, feat_count)
    total, there, here, again = local_call(
        functools.partial(first_kernel, 2),
        "first_split",
        keep,
        got,
        out_shape=[total_type, word_type, word_type, word_type],
    )
    both = swap(again, feat=10, odd=6)
    z_word = swap(here, feat=8, odd=4)
    x_word = swap(there, feat=2)
    total, word = local_call(
        square_kernel, "add_square", total, both, z_word, x_word, out_shape=[total_type, word_type]
    )
    word = swap(word, feat=4, odd=8)
    stride = 16
    while stride < feat_count:
        total, word = local_call(middle_kernel, "add_encode", total, word, out_shape=[total_type, word_type])
        word = swap(word, feat=stride)
        stride *= 2

    scale = 1.0 / math.sqrt(width * feat_count)
    own, *copies = local_call(
        functools.partial(last_kernel, scale),
        "sketch_rows",
        total,
        word,
        labels.reshape(1, rows),
        out_shape=[row_type] * 5,
    )
    stride = 2
    while stride < tok_count:
        copies = [jnp.concatenate([copies[0], swap(copies[0], tok=stride)], axis=0)] * 4
        own = copies[0]
        stride *= 2
    received = [swap(copies[0], tok=1, feat=2), swap(copies[1], feat=2), swap(copies[2], tok=1)]
    last = swap(copies[3], tok=1, feat=1)
    ours = [own] + received
    theirs = [swap(block, feat=1) for block in ours[:3]] + [last]
    concepts = C // tok_count
    gram = gram_blocks(ours + theirs, concepts, shard, C / (rows * tok_count))
    return gram.reshape(concepts, shard, kept)


def solution(mesh):
    in_specs = (P("tok", "feat"), P("feat"), P(), P("tok", None))
    out_specs = P("tok", "feat", None)
    return jax.shard_map(body, mesh=mesh, in_specs=in_specs, out_specs=out_specs, check_vma=False)
```

```python
import functools
import math

import jax
import jax.numpy as jnp
from jax import lax
from jax.experimental import pallas as pl
from jax.experimental.pallas import tpu as pltpu
from jax.sharding import PartitionSpec as P

C = 32
LOW = 256
LANES = 128
VMEM_LIMIT = 48 * 1024 * 1024


def parity_sign(number, bit_count):
    shift = 1
    while shift < bit_count:
        shift *= 2
    while shift > 1:
        shift //= 2
        number = number ^ (number >> shift)
    return (1 - 2 * (number & 1)).astype(jnp.float32)


def add_products(x_ref, sign_ref, low, high, out_ref, part, wide):
    rows, kept = out_ref.shape
    blocks = wide // LOW
    stack = []
    for block in range(part * blocks, (part + 1) * blocks):
        cols = slice(block * LOW, (block + 1) * LOW)
        stack.append(x_ref[:, cols] * sign_ref[:, cols].astype(jnp.bfloat16))
    stack = jnp.concatenate(stack, axis=0)
    for group in range(kept // LOW):
        cols = slice(group * LOW, (group + 1) * LOW)
        products = jnp.dot(stack, low[:, cols], preferred_element_type=jnp.float32)
        total = None
        for at in range(blocks):
            row = part * blocks + at
            term = products[at * rows:(at + 1) * rows] * high[row:row + 1, cols]
            total = term if total is None else total + term
        if part > 0:
            total = total + out_ref[:, cols]
        out_ref[:, cols] = total


def send_kernel(total_bits, parts, x_hbm, s_hbm, col_hbm, send_ref, x_keep, signs, low, high, x_buf, col_buf, sems):
    half, kept = send_ref.shape
    wide = x_hbm.shape[1] // parts
    me = lax.axis_index("feat")
    mine = lax.rem(me, 2)
    col_copy = pltpu.make_async_copy(col_hbm, col_buf, sems.at[parts])
    sign_copy = pltpu.make_async_copy(s_hbm, signs, sems.at[parts + 1])
    col_copy.start()
    sign_copy.start()
    copies = []
    for part in range(parts):
        cols = pl.ds(part * wide, wide)
        rows = pl.ds(pl.multiple_of((1 - mine) * half, half), half)
        copies.append(pltpu.make_async_copy(x_hbm.at[rows, cols], x_buf.at[:, cols], sems.at[part]))
        copies[-1].start()
    rows = pl.ds(pl.multiple_of(mine * half, half), half)
    keep_copy = pltpu.make_async_copy(x_hbm.at[rows, :], x_keep, sems.at[parts + 2])
    keep_copy.start()
    col_copy.wait()
    col = col_buf[...]
    index = lax.broadcasted_iota(jnp.int32, (16, kept), 0)
    inner = parity_sign(index & col, 4)
    outer = parity_sign(index & (col >> 4), 4)
    for row in range(LOW // 16):
        low[row * 16:(row + 1) * 16] = (inner * outer[row:row + 1]).astype(jnp.bfloat16)
    high_index = lax.broadcasted_iota(jnp.int32, high.shape, 0) + me * high.shape[0]
    high[...] = parity_sign(high_index & (col >> 8), total_bits - 8)
    sign_copy.wait()
    for part in range(parts):
        copies[part].wait()
        add_products(x_buf, signs, low, high, send_ref, part, wide)
    keep_copy.wait()


def keep_kernel(parts, x_keep, signs, low, high, keep_ref):
    wide = x_keep.shape[1] // parts
    for part in range(parts):
        add_products(x_keep, signs, low, high, keep_ref, part, wide)


def partial_halves(features, signs, columns, feat_count):
    rows, width = features.shape
    kept = columns.shape[0]
    parts = max(1, width // 2048)
    half = rows // 2
    total_bits = (width * feat_count).bit_length() - 1
    params = pltpu.CompilerParams(vmem_limit_bytes=VMEM_LIMIT)
    cost = pl.CostEstimate(
        flops=2 * half * width * kept, bytes_accessed=2 * rows * width + 4 * half * kept, transcendentals=0
    )
    total_type = jax.ShapeDtypeStruct((half, kept), jnp.float32)
    send, *held = pl.pallas_call(
        functools.partial(send_kernel, total_bits, parts),
        in_specs=[pl.BlockSpec(memory_space=pltpu.HBM)] * 3,
        out_specs=[pl.BlockSpec(memory_space=pltpu.VMEM)] * 5,
        out_shape=[
            total_type,
            jax.ShapeDtypeStruct((half, width), jnp.bfloat16),
            jax.ShapeDtypeStruct((1, width), jnp.int32),
            jax.ShapeDtypeStruct((LOW, kept), jnp.bfloat16),
            jax.ShapeDtypeStruct((width // LOW, kept), jnp.float32),
        ],
        scratch_shapes=[
            pltpu.VMEM((half, width), jnp.bfloat16),
            pltpu.VMEM((1, kept), jnp.int32),
            pltpu.SemaphoreType.DMA((parts + 3,)),
        ],
        compiler_params=params,
        cost_estimate=cost,
        name="partial_sent",
    )(*(
        pltpu.with_memory_space_constraint(operand, pltpu.HBM)
        for operand in (features, signs.reshape(1, width), columns.reshape(1, kept))
    ))
    got = swap(send, (0, 1))
    keep = pl.pallas_call(
        functools.partial(keep_kernel, parts),
        out_shape=total_type,
        compiler_params=params,
        cost_estimate=cost,
        name="partial_kept",
    )(*held)
    return keep, got


def gram_kernel(shard, group, factor, *refs):
    pieces, (out_hbm, rows, blocks, sems) = refs[:-4], refs[-4:]
    steps, wide, kept = blocks.shape
    place = 0
    for piece in pieces:
        rows[place:place + piece.shape[0]] = piece[:, :kept]
        place += piece.shape[0]
    first = lax.axis_index("feat") * shard
    start = pl.multiple_of(first // LANES * LANES, LANES)
    window = rows[:, pl.ds(start, LANES)].astype(jnp.float32) * factor
    window = pltpu.roll(window, lax.rem(LANES - (first - start), LANES), 1)
    own = jnp.concatenate([window.T[:shard]] * group, axis=0)
    named = jnp.concatenate([piece[:, kept:].astype(jnp.float32) for piece in pieces], axis=0).T[:1]
    label = named.astype(jnp.int32) - lax.broadcasted_iota(jnp.int32, own.shape, 0) // shard
    base = lax.axis_index("tok") * steps * group
    copies = []
    for step in range(steps):
        chosen = jnp.where(label == base + step * group, own, 0.0).astype(jnp.bfloat16)
        blocks[step] = jnp.dot(chosen, rows[...], preferred_element_type=jnp.float32)
        copies.append(
            pltpu.make_async_copy(blocks.at[step], out_hbm.at[pl.ds(step * wide, wide), :], sems.at[step])
        )
        copies[-1].start()
    for copy in copies:
        copy.wait()


def gram_blocks(pieces, concepts, shard, factor):
    tokens = sum(piece.shape[0] for piece in pieces)
    kept = pieces[0].shape[1] - LANES
    group = max(1, min(concepts, LOW // shard))
    wide = group * shard
    steps = concepts // group
    return pl.pallas_call(
        functools.partial(gram_kernel, shard, group, factor),
        in_specs=[pl.BlockSpec(memory_space=pltpu.VMEM)] * len(pieces),
        out_specs=pl.BlockSpec(memory_space=pltpu.HBM),
        out_shape=jax.ShapeDtypeStruct((concepts * shard, kept), jnp.float32),
        scratch_shapes=[
            pltpu.VMEM((tokens, kept), jnp.bfloat16),
            pltpu.VMEM((steps, wide, kept), jnp.float32),
            pltpu.SemaphoreType.DMA((steps,)),
        ],
        compiler_params=pltpu.CompilerParams(vmem_limit_bytes=VMEM_LIMIT),
        cost_estimate=pl.CostEstimate(
            flops=2 * tokens * concepts * shard * kept, bytes_accessed=4 * concepts * shard * kept, transcendentals=0
        ),
        name="gram",
    )(*pieces)


def encode(values, word_ref):
    size, kept = values.shape
    half = size // 2
    top = jnp.max(jnp.abs(values), axis=1, keepdims=True)
    power = jnp.ceil(jnp.log2(jnp.maximum(top, 2.0 ** -100)))
    whole = jnp.round(values * jnp.exp2(15.0 - power))
    whole = jnp.clip(whole, -32767.0, 32767.0).astype(jnp.int32)
    word = (whole[:half] & 0xFFFF) | (whole[half:] << 16)
    for column in range(kept // LANES):
        word_ref[column * half:(column + 1) * half] = word[:, column * LANES:(column + 1) * LANES]
    group = lax.broadcasted_iota(jnp.int32, (8, LANES), 1) // (LANES * 8 // size)
    tile = jnp.zeros((8, LANES), jnp.int32)
    for at in range(size // 8):
        tile = jnp.where(group == at, power[at * 8:(at + 1) * 8].astype(jnp.int32), tile)
    word_ref[kept // LANES * half:] = tile


def decode(word_ref, size):
    half = size // 2
    columns = word_ref.shape[0] // half
    word = jnp.concatenate([word_ref[at * half:(at + 1) * half] for at in range(columns)], axis=1)
    code = jnp.concatenate([(word << 16) >> 16, word >> 16], axis=0).astype(jnp.float32)
    tile = jnp.exp2(word_ref[columns * half:].astype(jnp.float32) - 15.0)
    lanes = LANES * 8 // size
    scale = jnp.concatenate([tile[:, at * lanes:at * lanes + 1] for at in range(size // 8)], axis=0)
    return code * scale


def first_kernel(stride, keep_ref, got_ref, total_ref, there_ref, here_ref, again_ref):
    size = total_ref.shape[0]
    digit = lax.rem(lax.axis_index("feat") // stride, 2)

    def piece(at):
        span = pl.ds(pl.multiple_of(at * size, size), size)
        return keep_ref[span, :] + got_ref[span, :]

    encode(piece(1 - digit), there_ref)
    again_ref[...] = there_ref[...]
    total = piece(digit)
    total_ref[...] = total
    encode(total, here_ref)


def square_kernel(total_ref, both_ref, z_ref, x_ref, sum_ref, out_ref):
    size = total_ref.shape[0]
    total = (total_ref[...] + decode(x_ref, size)) + (decode(z_ref, size) + decode(both_ref, size))
    sum_ref[...] = total
    encode(total, out_ref)


def middle_kernel(total_ref, word_ref, sum_ref, out_ref):
    total = total_ref[...] + decode(word_ref, total_ref.shape[0])
    sum_ref[...] = total
    encode(total, out_ref)


def last_kernel(scale, total_ref, word_ref, label_ref, *row_refs):
    size, kept = total_ref.shape
    row = ((total_ref[...] + decode(word_ref, size)) * scale).astype(jnp.bfloat16)
    me = lax.axis_index("feat")
    first = lax.rem(me, 2) * 2 * size + lax.rem(me // 2, 2) * size
    label = jnp.broadcast_to(label_ref[...].astype(jnp.float32), (8, LANES))
    label = pltpu.roll(label, lax.rem(LANES - first, LANES), 1)
    label = jnp.broadcast_to(label[:1], (LANES, LANES)).T[:size].astype(jnp.bfloat16)
    for row_ref in row_refs:
        row_ref[:, :kept] = row
        row_ref[:, kept:] = label


def local_call(kernel, name, *operands, out_shape):
    return pl.pallas_call(
        kernel,
        out_shape=out_shape,
        compiler_params=pltpu.CompilerParams(vmem_limit_bytes=VMEM_LIMIT),
        name=name,
    )(*operands)


def swap(array, even, odd=None):
    tok_count, feat_count = lax.axis_size("tok"), lax.axis_size("feat")
    bits = (even, odd or even)
    pairs = [
        (f * tok_count + t, (f ^ bits[f & 1][1]) * tok_count + (t ^ bits[f & 1][0]))
        for f in range(feat_count)
        for t in range(tok_count)
    ]
    return lax.ppermute(array, ("feat", "tok"), pairs)


def body(features, signs, columns, labels):
    rows, width = features.shape
    feat_count = lax.axis_size("feat")
    tok_count = lax.axis_size("tok")
    kept = columns.shape[0]
    shard = kept // feat_count
    size = rows // 4
    total_type = jax.ShapeDtypeStruct((size, kept), jnp.float32)
    word_type = jax.ShapeDtypeStruct((kept // LANES * (size // 2) + 8, LANES), jnp.int32)
    row_type = jax.ShapeDtypeStruct((size, kept + LANES), jnp.bfloat16)

    keep, got = partial_halves(features, signs, columns, feat_count)
    total, there, here, again = local_call(
        functools.partial(first_kernel, 2),
        "first_split",
        keep,
        got,
        out_shape=[total_type, word_type, word_type, word_type],
    )
    both = swap(again, (0, 10), (0, 6))
    z_word = swap(here, (0, 8), (0, 4))
    x_word = swap(there, (0, 2))
    total, word = local_call(
        square_kernel, "add_square", total, both, z_word, x_word, out_shape=[total_type, word_type]
    )
    word = swap(word, (0, 4), (0, 8))
    stride = 16
    while stride < feat_count:
        total, word = local_call(middle_kernel, "add_encode", total, word, out_shape=[total_type, word_type])
        word = swap(word, (0, stride))
        stride *= 2

    scale = 1.0 / math.sqrt(width * feat_count)
    own, *copies = local_call(
        functools.partial(last_kernel, scale),
        "sketch_rows",
        total,
        word,
        labels.reshape(1, rows),
        out_shape=[row_type] * 5,
    )
    stride = 2
    while stride < tok_count:
        copies = [jnp.concatenate([copies[0], swap(copies[0], (stride, 0))], axis=0)] * 4
        own = copies[0]
        stride *= 2
    far = swap(copies[0], (1, 2))
    second = swap(copies[1], (0, 2), (1, 0))
    third = swap(copies[2], (1, 0), (0, 2))
    crossed = swap(copies[3], (1, 1), (0, 3))
    pieces = [own, far, second, third] + [swap(block, (0, 1)) for block in (own, far, second)] + [crossed]
    concepts = C // tok_count
    gram = gram_blocks(pieces, concepts, shard, C / (rows * tok_count))
    return gram.reshape(concepts, shard, kept)


def solution(mesh):
    in_specs = (P("tok", "feat"), P("feat"), P(), P("tok", None))
    out_specs = P("tok", "feat", None)
    return jax.shard_map(body, mesh=mesh, in_specs=in_specs, out_specs=out_specs, check_vma=False)
```

```python
import functools
import math

import jax
import jax.numpy as jnp
from jax import lax
from jax.experimental import pallas as pl
from jax.experimental.pallas import tpu as pltpu
from jax.sharding import PartitionSpec as P

C = 32
LOW = 256
LANES = 128
VMEM_LIMIT = 48 * 1024 * 1024


def parity_sign(number, bit_count):
    shift = 1
    while shift < bit_count:
        shift *= 2
    while shift > 1:
        shift //= 2
        number = number ^ (number >> shift)
    return (1 - 2 * (number & 1)).astype(jnp.float32)


def spans_of(width):
    return [(0, 1024), (1024, 2048)] + [(first, first + 2048) for first in range(2048, width, 2048)]


def add_products(x_ref, sign_ref, low, high, out_ref, span):
    rows, kept = out_ref.shape
    first, blocks = span[0] // LOW, (span[1] - span[0]) // LOW
    stack = []
    for block in range(first, first + blocks):
        cols = slice(block * LOW, (block + 1) * LOW)
        stack.append(x_ref[:, cols] * sign_ref[:, cols].astype(jnp.bfloat16))
    stack = jnp.concatenate(stack, axis=0)
    for group in range(kept // LOW):
        cols = slice(group * LOW, (group + 1) * LOW)
        products = jnp.dot(stack, low[:, cols], preferred_element_type=jnp.float32)
        total = None
        for at in range(blocks):
            row = first + at
            term = products[at * rows:(at + 1) * rows] * high[row:row + 1, cols]
            total = term if total is None else total + term
        if first > 0:
            total = total + out_ref[:, cols]
        out_ref[:, cols] = total


def send_kernel(total_bits, x_hbm, s_hbm, col_hbm, send_ref, x_keep, signs, low, high, x_buf, col_buf, sems):
    half, kept = send_ref.shape
    spans = spans_of(x_hbm.shape[1])
    parts = len(spans)
    me = lax.axis_index("feat")
    mine = lax.rem(me, 2)
    col_copy = pltpu.make_async_copy(col_hbm, col_buf, sems.at[parts])
    sign_copy = pltpu.make_async_copy(s_hbm, signs, sems.at[parts + 1])
    copies = []
    for part, (first, last) in enumerate(spans):
        cols = pl.ds(first, last - first)
        rows = pl.ds(pl.multiple_of((1 - mine) * half, half), half)
        copies.append(pltpu.make_async_copy(x_hbm.at[rows, cols], x_buf.at[:, cols], sems.at[part]))
    for copy in (col_copy, copies[0], sign_copy, *copies[1:]):
        copy.start()
    rows = pl.ds(pl.multiple_of(mine * half, half), half)
    keep_copy = pltpu.make_async_copy(x_hbm.at[rows, :], x_keep, sems.at[parts + 2])
    keep_copy.start()
    col_copy.wait()
    col = col_buf[...]
    index = lax.broadcasted_iota(jnp.int32, (16, kept), 0)
    inner = parity_sign(index & col, 4)
    outer = parity_sign(index & (col >> 4), 4)
    for row in range(LOW // 16):
        low[row * 16:(row + 1) * 16] = (inner * outer[row:row + 1]).astype(jnp.bfloat16)
    high_index = lax.broadcasted_iota(jnp.int32, high.shape, 0) + me * high.shape[0]
    high[...] = parity_sign(high_index & (col >> 8), total_bits - 8)
    sign_copy.wait()
    for span, copy in zip(spans, copies):
        copy.wait()
        add_products(x_buf, signs, low, high, send_ref, span)
    keep_copy.wait()


def keep_kernel(x_keep, signs, low, high, keep_ref):
    for first in range(0, x_keep.shape[1], 2048):
        add_products(x_keep, signs, low, high, keep_ref, (first, first + 2048))


def partial_halves(features, signs, columns, feat_count):
    rows, width = features.shape
    kept = columns.shape[0]
    parts = len(spans_of(width))
    half = rows // 2
    total_bits = (width * feat_count).bit_length() - 1
    params = pltpu.CompilerParams(vmem_limit_bytes=VMEM_LIMIT)
    cost = pl.CostEstimate(
        flops=2 * half * width * kept, bytes_accessed=2 * rows * width + 4 * half * kept, transcendentals=0
    )
    total_type = jax.ShapeDtypeStruct((half, kept), jnp.float32)
    send, *held = pl.pallas_call(
        functools.partial(send_kernel, total_bits),
        in_specs=[pl.BlockSpec(memory_space=pltpu.HBM)] * 3,
        out_specs=[pl.BlockSpec(memory_space=pltpu.VMEM)] * 5,
        out_shape=[
            total_type,
            jax.ShapeDtypeStruct((half, width), jnp.bfloat16),
            jax.ShapeDtypeStruct((1, width), jnp.int32),
            jax.ShapeDtypeStruct((LOW, kept), jnp.bfloat16),
            jax.ShapeDtypeStruct((width // LOW, kept), jnp.float32),
        ],
        scratch_shapes=[
            pltpu.VMEM((half, width), jnp.bfloat16),
            pltpu.VMEM((1, kept), jnp.int32),
            pltpu.SemaphoreType.DMA((parts + 3,)),
        ],
        compiler_params=params,
        cost_estimate=cost,
        name="partial_sent",
    )(*(
        pltpu.with_memory_space_constraint(operand, pltpu.HBM)
        for operand in (features, signs.reshape(1, width), columns.reshape(1, kept))
    ))
    got = swap(send, (0, 1))
    keep = pl.pallas_call(
        keep_kernel,
        out_shape=total_type,
        compiler_params=params,
        cost_estimate=cost,
        name="partial_kept",
    )(*held)
    return keep, got


def gram_kernel(shard, group, factor, *refs):
    pieces, (out_hbm, rows, blocks, sems) = refs[:-4], refs[-4:]
    steps, wide, kept = blocks.shape
    place = 0
    for piece in pieces:
        rows[place:place + piece.shape[0]] = piece[:, :kept]
        place += piece.shape[0]
    first = lax.axis_index("feat") * shard
    start = pl.multiple_of(first // LANES * LANES, LANES)
    window = rows[:, pl.ds(start, LANES)].astype(jnp.float32) * factor
    window = pltpu.roll(window, lax.rem(LANES - (first - start), LANES), 1)
    own = jnp.concatenate([window.T[:shard]] * group, axis=0)
    named = jnp.concatenate([piece[:, kept:].astype(jnp.float32) for piece in pieces], axis=0).T[:1]
    label = named.astype(jnp.int32) - lax.broadcasted_iota(jnp.int32, own.shape, 0) // shard
    base = lax.axis_index("tok") * steps * group
    copies = []
    for step in range(steps):
        chosen = jnp.where(label == base + step * group, own, 0.0).astype(jnp.bfloat16)
        blocks[step] = jnp.dot(chosen, rows[...], preferred_element_type=jnp.float32)
        copies.append(
            pltpu.make_async_copy(blocks.at[step], out_hbm.at[pl.ds(step * wide, wide), :], sems.at[step])
        )
        copies[-1].start()
    for copy in copies:
        copy.wait()


def gram_blocks(pieces, concepts, shard, factor):
    tokens = sum(piece.shape[0] for piece in pieces)
    kept = pieces[0].shape[1] - LANES
    group = max(1, min(concepts, LOW // shard))
    wide = group * shard
    steps = concepts // group
    return pl.pallas_call(
        functools.partial(gram_kernel, shard, group, factor),
        in_specs=[pl.BlockSpec(memory_space=pltpu.VMEM)] * len(pieces),
        out_specs=pl.BlockSpec(memory_space=pltpu.HBM),
        out_shape=jax.ShapeDtypeStruct((concepts * shard, kept), jnp.float32),
        scratch_shapes=[
            pltpu.VMEM((tokens, kept), jnp.bfloat16),
            pltpu.VMEM((steps, wide, kept), jnp.float32),
            pltpu.SemaphoreType.DMA((steps,)),
        ],
        compiler_params=pltpu.CompilerParams(vmem_limit_bytes=VMEM_LIMIT),
        cost_estimate=pl.CostEstimate(
            flops=2 * tokens * concepts * shard * kept, bytes_accessed=4 * concepts * shard * kept, transcendentals=0
        ),
        name="gram",
    )(*pieces)


def encode(values, word_ref):
    size, kept = values.shape
    half = size // 2
    top = jnp.max(jnp.abs(values), axis=1, keepdims=True)
    power = jnp.ceil(jnp.log2(jnp.maximum(top, 2.0 ** -100)))
    whole = jnp.round(values * jnp.exp2(15.0 - power))
    whole = jnp.clip(whole, -32767.0, 32767.0).astype(jnp.int32)
    word = (whole[:half] & 0xFFFF) | (whole[half:] << 16)
    for column in range(kept // LANES):
        word_ref[column * half:(column + 1) * half] = word[:, column * LANES:(column + 1) * LANES]
    group = lax.broadcasted_iota(jnp.int32, (8, LANES), 1) // (LANES * 8 // size)
    tile = jnp.zeros((8, LANES), jnp.int32)
    for at in range(size // 8):
        tile = jnp.where(group == at, power[at * 8:(at + 1) * 8].astype(jnp.int32), tile)
    word_ref[kept // LANES * half:] = tile


def decode(word_ref, size):
    half = size // 2
    columns = word_ref.shape[0] // half
    word = jnp.concatenate([word_ref[at * half:(at + 1) * half] for at in range(columns)], axis=1)
    code = jnp.concatenate([(word << 16) >> 16, word >> 16], axis=0).astype(jnp.float32)
    tile = jnp.exp2(word_ref[columns * half:].astype(jnp.float32) - 15.0)
    lanes = LANES * 8 // size
    scale = jnp.concatenate([tile[:, at * lanes:at * lanes + 1] for at in range(size // 8)], axis=0)
    return code * scale


def first_kernel(stride, keep_ref, got_ref, total_ref, far_ref, second_ref, third_ref, there_ref, here_ref):
    size = total_ref.shape[0]
    digit = lax.rem(lax.axis_index("feat") // stride, 2)

    def piece(at):
        span = pl.ds(pl.multiple_of(at * size, size), size)
        return keep_ref[span, :] + got_ref[span, :]

    encode(piece(1 - digit), there_ref)
    total = piece(digit)
    total_ref[...] = total
    encode(total, here_ref)
    even = lax.rem(lax.axis_index("feat"), 2) == 0
    far_ref[...] = there_ref[...]
    second_ref[...] = jnp.where(even, here_ref[...], there_ref[...])
    third_ref[...] = jnp.where(even, there_ref[...], here_ref[...])


def square_kernel(total_ref, far_ref, second_ref, third_ref, sum_ref, out_ref):
    size = total_ref.shape[0]
    total = (total_ref[...] + decode(far_ref, size)) + (decode(second_ref, size) + decode(third_ref, size))
    sum_ref[...] = total
    encode(total, out_ref)


def middle_kernel(total_ref, word_ref, sum_ref, out_ref):
    total = total_ref[...] + decode(word_ref, total_ref.shape[0])
    sum_ref[...] = total
    encode(total, out_ref)


def last_kernel(scale, total_ref, word_ref, label_ref, *row_refs):
    size, kept = total_ref.shape
    row = ((total_ref[...] + decode(word_ref, size)) * scale).astype(jnp.bfloat16)
    me = lax.axis_index("feat")
    first = lax.rem(me, 2) * 2 * size + lax.rem(me // 2, 2) * size
    label = jnp.broadcast_to(label_ref[...].astype(jnp.float32), (8, LANES))
    label = pltpu.roll(label, lax.rem(LANES - first, LANES), 1)
    label = jnp.broadcast_to(label[:1], (LANES, LANES)).T[:size].astype(jnp.bfloat16)
    for row_ref in row_refs:
        row_ref[:, :kept] = row
        row_ref[:, kept:] = label


def local_call(kernel, name, *operands, out_shape, scratch=()):
    return pl.pallas_call(
        kernel,
        out_shape=out_shape,
        scratch_shapes=scratch,
        compiler_params=pltpu.CompilerParams(vmem_limit_bytes=VMEM_LIMIT),
        name=name,
    )(*operands)


def swap(array, even, odd=None):
    tok_count, feat_count = lax.axis_size("tok"), lax.axis_size("feat")
    bits = (even, odd or even)
    pairs = [
        (f * tok_count + t, (f ^ bits[f & 1][1]) * tok_count + (t ^ bits[f & 1][0]))
        for f in range(feat_count)
        for t in range(tok_count)
    ]
    return lax.ppermute(array, ("feat", "tok"), pairs)


def body(features, signs, columns, labels):
    rows, width = features.shape
    feat_count = lax.axis_size("feat")
    tok_count = lax.axis_size("tok")
    kept = columns.shape[0]
    shard = kept // feat_count
    size = rows // 4
    total_type = jax.ShapeDtypeStruct((size, kept), jnp.float32)
    word_type = jax.ShapeDtypeStruct((kept // LANES * (size // 2) + 8, LANES), jnp.int32)
    row_type = jax.ShapeDtypeStruct((size, kept + LANES), jnp.bfloat16)

    keep, got = partial_halves(features, signs, columns, feat_count)
    total, far, second, third = local_call(
        functools.partial(first_kernel, 2),
        "first_split",
        keep,
        got,
        out_shape=[total_type, word_type, word_type, word_type],
        scratch=[pltpu.VMEM(word_type.shape, word_type.dtype)] * 2,
    )
    far = swap(far, (0, 10), (0, 6))
    second = swap(second, (0, 8), (0, 2))
    third = swap(third, (0, 2), (0, 4))
    total, word = local_call(
        square_kernel, "add_square", total, far, second, third, out_shape=[total_type, word_type]
    )
    word = swap(word, (0, 4), (0, 8))
    stride = 16
    while stride < feat_count:
        total, word = local_call(middle_kernel, "add_encode", total, word, out_shape=[total_type, word_type])
        word = swap(word, (0, stride))
        stride *= 2

    scale = 1.0 / math.sqrt(width * feat_count)
    own, *copies = local_call(
        functools.partial(last_kernel, scale),
        "sketch_rows",
        total,
        word,
        labels.reshape(1, rows),
        out_shape=[row_type] * 5,
    )
    stride = 2
    while stride < tok_count:
        copies = [jnp.concatenate([copies[0], swap(copies[0], (stride, 0))], axis=0)] * 4
        own = copies[0]
        stride *= 2
    far = swap(copies[0], (1, 2))
    second = swap(copies[1], (0, 2), (1, 0))
    third = swap(copies[2], (1, 0), (0, 2))
    crossed = swap(copies[3], (1, 1), (0, 3))
    pieces = [own, far, second, third] + [swap(block, (0, 1)) for block in (own, far, second)] + [crossed]
    concepts = C // tok_count
    gram = gram_blocks(pieces, concepts, shard, C / (rows * tok_count))
    return gram.reshape(concepts, shard, kept)


def solution(mesh):
    in_specs = (P("tok", "feat"), P("feat"), P(), P("tok", None))
    out_specs = P("tok", "feat", None)
    return jax.shard_map(body, mesh=mesh, in_specs=in_specs, out_specs=out_specs, check_vma=False)
```

```python
import functools
import math

import jax
import jax.numpy as jnp
from jax import lax
from jax.experimental import pallas as pl
from jax.experimental.pallas import tpu as pltpu
from jax.sharding import PartitionSpec as P

C = 32
LOW = 256
LANES = 128
VMEM_LIMIT = 48 * 1024 * 1024


def parity_sign(number, bit_count):
    shift = 1
    while shift < bit_count:
        shift *= 2
    while shift > 1:
        shift //= 2
        number = number ^ (number >> shift)
    return (1 - 2 * (number & 1)).astype(jnp.float32)


def add_products(x_ref, sign_ref, low, high, out_ref, part, wide):
    rows, kept = out_ref.shape
    blocks = wide // LOW
    stack = []
    for block in range(part * blocks, (part + 1) * blocks):
        cols = slice(block * LOW, (block + 1) * LOW)
        stack.append(x_ref[:, cols] * sign_ref[:, cols].astype(jnp.bfloat16))
    stack = jnp.concatenate(stack, axis=0)
    for group in range(kept // LOW):
        cols = slice(group * LOW, (group + 1) * LOW)
        products = jnp.dot(stack, low[:, cols], preferred_element_type=jnp.float32)
        total = None
        for at in range(blocks):
            row = part * blocks + at
            term = products[at * rows:(at + 1) * rows] * high[row:row + 1, cols]
            total = term if total is None else total + term
        if part > 0:
            total = total + out_ref[:, cols]
        out_ref[:, cols] = total


def send_kernel(total_bits, parts, x_hbm, s_hbm, col_hbm, send_ref, x_keep, signs, low, high, x_buf, col_buf, sems):
    half, kept = send_ref.shape
    wide = x_hbm.shape[1] // parts
    me = lax.axis_index("feat")
    mine = lax.rem(me, 2)
    col_copy = pltpu.make_async_copy(col_hbm, col_buf, sems.at[parts])
    sign_copy = pltpu.make_async_copy(s_hbm, signs, sems.at[parts + 1])
    col_copy.start()
    sign_copy.start()
    copies = []
    for part in range(parts):
        cols = pl.ds(part * wide, wide)
        rows = pl.ds(pl.multiple_of((1 - mine) * half, half), half)
        copies.append(pltpu.make_async_copy(x_hbm.at[rows, cols], x_buf.at[:, cols], sems.at[part]))
        copies[-1].start()
    rows = pl.ds(pl.multiple_of(mine * half, half), half)
    keep_copy = pltpu.make_async_copy(x_hbm.at[rows, :], x_keep, sems.at[parts + 2])
    keep_copy.start()
    col_copy.wait()
    col = col_buf[...]
    index = lax.broadcasted_iota(jnp.int32, (16, kept), 0)
    inner = parity_sign(index & col, 4)
    outer = parity_sign(index & (col >> 4), 4)
    for row in range(LOW // 16):
        low[row * 16:(row + 1) * 16] = (inner * outer[row:row + 1]).astype(jnp.bfloat16)
    high_index = lax.broadcasted_iota(jnp.int32, high.shape, 0) + me * high.shape[0]
    high[...] = parity_sign(high_index & (col >> 8), total_bits - 8)
    sign_copy.wait()
    for part in range(parts):
        copies[part].wait()
        add_products(x_buf, signs, low, high, send_ref, part, wide)
    keep_copy.wait()


def keep_kernel(parts, x_keep, signs, low, high, keep_ref):
    wide = x_keep.shape[1] // parts
    for part in range(parts):
        add_products(x_keep, signs, low, high, keep_ref, part, wide)


def partial_halves(features, signs, columns, feat_count):
    rows, width = features.shape
    kept = columns.shape[0]
    parts = max(1, width // 4096)
    half = rows // 2
    total_bits = (width * feat_count).bit_length() - 1
    params = pltpu.CompilerParams(vmem_limit_bytes=VMEM_LIMIT)
    cost = pl.CostEstimate(
        flops=2 * half * width * kept, bytes_accessed=2 * rows * width + 4 * half * kept, transcendentals=0
    )
    total_type = jax.ShapeDtypeStruct((half, kept), jnp.float32)
    send, *held = pl.pallas_call(
        functools.partial(send_kernel, total_bits, parts),
        in_specs=[pl.BlockSpec(memory_space=pltpu.HBM)] * 3,
        out_specs=[pl.BlockSpec(memory_space=pltpu.VMEM)] * 5,
        out_shape=[
            total_type,
            jax.ShapeDtypeStruct((half, width), jnp.bfloat16),
            jax.ShapeDtypeStruct((1, width), jnp.int32),
            jax.ShapeDtypeStruct((LOW, kept), jnp.bfloat16),
            jax.ShapeDtypeStruct((width // LOW, kept), jnp.float32),
        ],
        scratch_shapes=[
            pltpu.VMEM((half, width), jnp.bfloat16),
            pltpu.VMEM((1, kept), jnp.int32),
            pltpu.SemaphoreType.DMA((parts + 3,)),
        ],
        compiler_params=params,
        cost_estimate=cost,
        name="partial_sent",
    )(*(
        pltpu.with_memory_space_constraint(operand, pltpu.HBM)
        for operand in (features, signs.reshape(1, width), columns.reshape(1, kept))
    ))
    got = swap(send, (0, 1))
    keep = pl.pallas_call(
        functools.partial(keep_kernel, parts),
        out_shape=total_type,
        compiler_params=params,
        cost_estimate=cost,
        name="partial_kept",
    )(*held)
    return keep, got


def gram_kernel(shard, group, factor, *refs):
    pieces, (out_hbm, rows, blocks, sems) = refs[:-4], refs[-4:]
    steps, wide, kept = blocks.shape
    place = 0
    for piece in pieces:
        rows[place:place + piece.shape[0]] = piece[:, :kept]
        place += piece.shape[0]
    first = lax.axis_index("feat") * shard
    start = pl.multiple_of(first // LANES * LANES, LANES)
    window = rows[:, pl.ds(start, LANES)].astype(jnp.float32) * factor
    window = pltpu.roll(window, lax.rem(LANES - (first - start), LANES), 1)
    own = jnp.concatenate([window.T[:shard]] * group, axis=0)
    named = jnp.concatenate([piece[:, kept:].astype(jnp.float32) for piece in pieces], axis=0).T[:1]
    label = named.astype(jnp.int32) - lax.broadcasted_iota(jnp.int32, own.shape, 0) // shard
    base = lax.axis_index("tok") * steps * group
    copies = []
    for step in range(steps):
        chosen = jnp.where(label == base + step * group, own, 0.0).astype(jnp.bfloat16)
        blocks[step] = jnp.dot(chosen, rows[...], preferred_element_type=jnp.float32)
        copies.append(
            pltpu.make_async_copy(blocks.at[step], out_hbm.at[pl.ds(step * wide, wide), :], sems.at[step])
        )
        copies[-1].start()
    for copy in copies:
        copy.wait()


def gram_blocks(pieces, concepts, shard, factor):
    tokens = sum(piece.shape[0] for piece in pieces)
    kept = pieces[0].shape[1] - LANES
    group = max(1, min(concepts, LOW // shard))
    wide = group * shard
    steps = concepts // group
    return pl.pallas_call(
        functools.partial(gram_kernel, shard, group, factor),
        in_specs=[pl.BlockSpec(memory_space=pltpu.VMEM)] * len(pieces),
        out_specs=pl.BlockSpec(memory_space=pltpu.HBM),
        out_shape=jax.ShapeDtypeStruct((concepts * shard, kept), jnp.float32),
        scratch_shapes=[
            pltpu.VMEM((tokens, kept), jnp.bfloat16),
            pltpu.VMEM((steps, wide, kept), jnp.float32),
            pltpu.SemaphoreType.DMA((steps,)),
        ],
        compiler_params=pltpu.CompilerParams(vmem_limit_bytes=VMEM_LIMIT),
        cost_estimate=pl.CostEstimate(
            flops=2 * tokens * concepts * shard * kept, bytes_accessed=4 * concepts * shard * kept, transcendentals=0
        ),
        name="gram",
    )(*pieces)


def encode(values, word_ref):
    size, kept = values.shape
    half = size // 2
    top = jnp.max(jnp.abs(values), axis=1, keepdims=True)
    power = jnp.ceil(jnp.log2(jnp.maximum(top, 2.0 ** -100)))
    whole = jnp.round(values * jnp.exp2(15.0 - power))
    whole = jnp.clip(whole, -32767.0, 32767.0).astype(jnp.int32)
    word = (whole[:half] & 0xFFFF) | (whole[half:] << 16)
    for column in range(kept // LANES):
        word_ref[column * half:(column + 1) * half] = word[:, column * LANES:(column + 1) * LANES]
    group = lax.broadcasted_iota(jnp.int32, (8, LANES), 1) // (LANES * 8 // size)
    tile = jnp.zeros((8, LANES), jnp.int32)
    for at in range(size // 8):
        tile = jnp.where(group == at, power[at * 8:(at + 1) * 8].astype(jnp.int32), tile)
    word_ref[kept // LANES * half:] = tile


def decode(word_ref, size):
    half = size // 2
    columns = word_ref.shape[0] // half
    word = jnp.concatenate([word_ref[at * half:(at + 1) * half] for at in range(columns)], axis=1)
    code = jnp.concatenate([(word << 16) >> 16, word >> 16], axis=0).astype(jnp.float32)
    tile = jnp.exp2(word_ref[columns * half:].astype(jnp.float32) - 15.0)
    lanes = LANES * 8 // size
    scale = jnp.concatenate([tile[:, at * lanes:at * lanes + 1] for at in range(size // 8)], axis=0)
    return code * scale


def first_kernel(stride, keep_ref, got_ref, total_ref, there_ref, here_ref, again_ref):
    size = total_ref.shape[0]
    digit = lax.rem(lax.axis_index("feat") // stride, 2)

    def piece(at):
        span = pl.ds(pl.multiple_of(at * size, size), size)
        return keep_ref[span, :] + got_ref[span, :]

    encode(piece(1 - digit), there_ref)
    again_ref[...] = there_ref[...]
    total = piece(digit)
    total_ref[...] = total
    encode(total, here_ref)


def square_kernel(total_ref, both_ref, z_ref, x_ref, sum_ref, out_ref):
    size = total_ref.shape[0]
    total = (total_ref[...] + decode(x_ref, size)) + (decode(z_ref, size) + decode(both_ref, size))
    sum_ref[...] = total
    encode(total, out_ref)


def middle_kernel(total_ref, word_ref, sum_ref, out_ref):
    total = total_ref[...] + decode(word_ref, total_ref.shape[0])
    sum_ref[...] = total
    encode(total, out_ref)


def last_kernel(scale, total_ref, word_ref, label_ref, *row_refs):
    size, kept = total_ref.shape
    row = ((total_ref[...] + decode(word_ref, size)) * scale).astype(jnp.bfloat16)
    me = lax.axis_index("feat")
    first = lax.rem(me, 2) * 2 * size + lax.rem(me // 2, 2) * size
    label = jnp.broadcast_to(label_ref[...].astype(jnp.float32), (8, LANES))
    label = pltpu.roll(label, lax.rem(LANES - first, LANES), 1)
    label = jnp.broadcast_to(label[:1], (LANES, LANES)).T[:size].astype(jnp.bfloat16)
    for row_ref in row_refs:
        row_ref[:, :kept] = row
        row_ref[:, kept:] = label


def local_call(kernel, name, *operands, out_shape):
    return pl.pallas_call(
        kernel,
        out_shape=out_shape,
        compiler_params=pltpu.CompilerParams(vmem_limit_bytes=VMEM_LIMIT),
        name=name,
    )(*operands)


def swap(array, even, odd=None):
    tok_count, feat_count = lax.axis_size("tok"), lax.axis_size("feat")
    bits = (even, odd or even)
    pairs = [
        (f * tok_count + t, (f ^ bits[f & 1][1]) * tok_count + (t ^ bits[f & 1][0]))
        for f in range(feat_count)
        for t in range(tok_count)
    ]
    return lax.ppermute(array, ("feat", "tok"), pairs)


def body(features, signs, columns, labels):
    rows, width = features.shape
    feat_count = lax.axis_size("feat")
    tok_count = lax.axis_size("tok")
    kept = columns.shape[0]
    shard = kept // feat_count
    size = rows // 4
    total_type = jax.ShapeDtypeStruct((size, kept), jnp.float32)
    word_type = jax.ShapeDtypeStruct((kept // LANES * (size // 2) + 8, LANES), jnp.int32)
    row_type = jax.ShapeDtypeStruct((size, kept + LANES), jnp.bfloat16)

    keep, got = partial_halves(features, signs, columns, feat_count)
    total, there, here, again = local_call(
        functools.partial(first_kernel, 2),
        "first_split",
        keep,
        got,
        out_shape=[total_type, word_type, word_type, word_type],
    )
    both = swap(again, (0, 10), (0, 6))
    z_word = swap(here, (0, 8), (0, 4))
    x_word = swap(there, (0, 2))
    total, word = local_call(
        square_kernel, "add_square", total, both, z_word, x_word, out_shape=[total_type, word_type]
    )
    word = swap(word, (0, 4), (0, 8))
    stride = 16
    while stride < feat_count:
        total, word = local_call(middle_kernel, "add_encode", total, word, out_shape=[total_type, word_type])
        word = swap(word, (0, stride))
        stride *= 2

    scale = 1.0 / math.sqrt(width * feat_count)
    own, *copies = local_call(
        functools.partial(last_kernel, scale),
        "sketch_rows",
        total,
        word,
        labels.reshape(1, rows),
        out_shape=[row_type] * 5,
    )
    stride = 2
    while stride < tok_count:
        copies = [jnp.concatenate([copies[0], swap(copies[0], (stride, 0))], axis=0)] * 4
        own = copies[0]
        stride *= 2
    far = swap(copies[0], (1, 3))
    second = swap(copies[1], (0, 2), (1, 0))
    third = swap(copies[2], (1, 0), (0, 2))
    crossed = swap(copies[3], (1, 1), (0, 3))
    pieces = [own, far, second, third] + [swap(block, (0, 1)) for block in (own, far, second)] + [crossed]
    concepts = C // tok_count
    gram = gram_blocks(pieces, concepts, shard, C / (rows * tok_count))
    return gram.reshape(concepts, shard, kept)


def solution(mesh):
    in_specs = (P("tok", "feat"), P("feat"), P(), P("tok", None))
    out_specs = P("tok", "feat", None)
    return jax.shard_map(body, mesh=mesh, in_specs=in_specs, out_specs=out_specs, check_vma=False)
```

```python
import functools
import math

import jax
import jax.numpy as jnp
from jax import lax
from jax.experimental import pallas as pl
from jax.experimental.pallas import tpu as pltpu
from jax.sharding import PartitionSpec as P

C = 32
LOW = 256
LANES = 128
VMEM_LIMIT = 48 * 1024 * 1024


def parity_sign(number, bit_count):
    shift = 1
    while shift < bit_count:
        shift *= 2
    while shift > 1:
        shift //= 2
        number = number ^ (number >> shift)
    return (1 - 2 * (number & 1)).astype(jnp.float32)


def add_products(x_ref, sign_ref, low, high, out_ref, part, wide):
    rows, kept = out_ref.shape
    blocks = wide // LOW
    stack = []
    for block in range(part * blocks, (part + 1) * blocks):
        cols = slice(block * LOW, (block + 1) * LOW)
        stack.append(x_ref[:, cols] * sign_ref[:, cols].astype(jnp.bfloat16))
    stack = jnp.concatenate(stack, axis=0)
    for group in range(kept // LOW):
        cols = slice(group * LOW, (group + 1) * LOW)
        products = jnp.dot(stack, low[:, cols], preferred_element_type=jnp.float32)
        total = None
        for at in range(blocks):
            row = part * blocks + at
            term = products[at * rows:(at + 1) * rows] * high[row:row + 1, cols]
            total = term if total is None else total + term
        if part > 0:
            total = total + out_ref[:, cols]
        out_ref[:, cols] = total


def send_kernel(total_bits, parts, x_hbm, s_hbm, col_hbm, send_ref, x_keep, signs, low, high, x_buf, col_buf, sems):
    half, kept = send_ref.shape
    wide = x_hbm.shape[1] // parts
    me = lax.axis_index("feat")
    mine = lax.rem(me, 2)
    col_copy = pltpu.make_async_copy(col_hbm, col_buf, sems.at[parts])
    sign_copy = pltpu.make_async_copy(s_hbm, signs, sems.at[parts + 1])
    col_copy.start()
    sign_copy.start()
    copies = []
    for part in range(parts):
        cols = pl.ds(part * wide, wide)
        rows = pl.ds(pl.multiple_of((1 - mine) * half, half), half)
        copies.append(pltpu.make_async_copy(x_hbm.at[rows, cols], x_buf.at[:, cols], sems.at[part]))
        copies[-1].start()
    rows = pl.ds(pl.multiple_of(mine * half, half), half)
    keep_copy = pltpu.make_async_copy(x_hbm.at[rows, :], x_keep, sems.at[parts + 2])
    keep_copy.start()
    col_copy.wait()
    col = col_buf[...]
    index = lax.broadcasted_iota(jnp.int32, (16, kept), 0)
    inner = parity_sign(index & col, 4)
    outer = parity_sign(index & (col >> 4), 4)
    for row in range(LOW // 16):
        low[row * 16:(row + 1) * 16] = (inner * outer[row:row + 1]).astype(jnp.bfloat16)
    high_index = lax.broadcasted_iota(jnp.int32, high.shape, 0) + me * high.shape[0]
    high[...] = parity_sign(high_index & (col >> 8), total_bits - 8)
    sign_copy.wait()
    for part in range(parts):
        copies[part].wait()
        add_products(x_buf, signs, low, high, send_ref, part, wide)
    keep_copy.wait()


def keep_kernel(parts, x_keep, signs, low, high, keep_ref):
    wide = x_keep.shape[1] // parts
    for part in range(parts):
        add_products(x_keep, signs, low, high, keep_ref, part, wide)


def partial_halves(features, signs, columns, feat_count):
    rows, width = features.shape
    kept = columns.shape[0]
    parts = 1
    half = rows // 2
    total_bits = (width * feat_count).bit_length() - 1
    params = pltpu.CompilerParams(vmem_limit_bytes=VMEM_LIMIT)
    cost = pl.CostEstimate(
        flops=2 * half * width * kept, bytes_accessed=2 * rows * width + 4 * half * kept, transcendentals=0
    )
    total_type = jax.ShapeDtypeStruct((half, kept), jnp.float32)
    send, *held = pl.pallas_call(
        functools.partial(send_kernel, total_bits, parts),
        in_specs=[pl.BlockSpec(memory_space=pltpu.HBM)] * 3,
        out_specs=[pl.BlockSpec(memory_space=pltpu.VMEM)] * 5,
        out_shape=[
            total_type,
            jax.ShapeDtypeStruct((half, width), jnp.bfloat16),
            jax.ShapeDtypeStruct((1, width), jnp.int32),
            jax.ShapeDtypeStruct((LOW, kept), jnp.bfloat16),
            jax.ShapeDtypeStruct((width // LOW, kept), jnp.float32),
        ],
        scratch_shapes=[
            pltpu.VMEM((half, width), jnp.bfloat16),
            pltpu.VMEM((1, kept), jnp.int32),
            pltpu.SemaphoreType.DMA((parts + 3,)),
        ],
        compiler_params=params,
        cost_estimate=cost,
        name="partial_sent",
    )(*(
        pltpu.with_memory_space_constraint(operand, pltpu.HBM)
        for operand in (features, signs.reshape(1, width), columns.reshape(1, kept))
    ))
    got = swap(send, (0, 1))
    keep = pl.pallas_call(
        functools.partial(keep_kernel, parts),
        out_shape=total_type,
        compiler_params=params,
        cost_estimate=cost,
        name="partial_kept",
    )(*held)
    return keep, got


def gram_kernel(shard, group, factor, *refs):
    pieces, (out_hbm, rows, blocks, sems) = refs[:-4], refs[-4:]
    steps, wide, kept = blocks.shape
    place = 0
    for piece in pieces:
        rows[place:place + piece.shape[0]] = piece[:, :kept]
        place += piece.shape[0]
    first = lax.axis_index("feat") * shard
    start = pl.multiple_of(first // LANES * LANES, LANES)
    window = rows[:, pl.ds(start, LANES)].astype(jnp.float32) * factor
    window = pltpu.roll(window, lax.rem(LANES - (first - start), LANES), 1)
    own = jnp.concatenate([window.T[:shard]] * group, axis=0)
    named = jnp.concatenate([piece[:, kept:].astype(jnp.float32) for piece in pieces], axis=0).T[:1]
    label = named.astype(jnp.int32) - lax.broadcasted_iota(jnp.int32, own.shape, 0) // shard
    base = lax.axis_index("tok") * steps * group
    copies = []
    for step in range(steps):
        chosen = jnp.where(label == base + step * group, own, 0.0).astype(jnp.bfloat16)
        blocks[step] = jnp.dot(chosen, rows[...], preferred_element_type=jnp.float32)
        copies.append(
            pltpu.make_async_copy(blocks.at[step], out_hbm.at[pl.ds(step * wide, wide), :], sems.at[step])
        )
        copies[-1].start()
    for copy in copies:
        copy.wait()


def gram_blocks(pieces, concepts, shard, factor):
    tokens = sum(piece.shape[0] for piece in pieces)
    kept = pieces[0].shape[1] - LANES
    group = max(1, min(concepts, LOW // shard))
    wide = group * shard
    steps = concepts // group
    return pl.pallas_call(
        functools.partial(gram_kernel, shard, group, factor),
        in_specs=[pl.BlockSpec(memory_space=pltpu.VMEM)] * len(pieces),
        out_specs=pl.BlockSpec(memory_space=pltpu.HBM),
        out_shape=jax.ShapeDtypeStruct((concepts * shard, kept), jnp.float32),
        scratch_shapes=[
            pltpu.VMEM((tokens, kept), jnp.bfloat16),
            pltpu.VMEM((steps, wide, kept), jnp.float32),
            pltpu.SemaphoreType.DMA((steps,)),
        ],
        compiler_params=pltpu.CompilerParams(vmem_limit_bytes=VMEM_LIMIT),
        cost_estimate=pl.CostEstimate(
            flops=2 * tokens * concepts * shard * kept, bytes_accessed=4 * concepts * shard * kept, transcendentals=0
        ),
        name="gram",
    )(*pieces)


def encode(values, word_ref):
    size, kept = values.shape
    half = size // 2
    top = jnp.max(jnp.abs(values), axis=1, keepdims=True)
    power = jnp.ceil(jnp.log2(jnp.maximum(top, 2.0 ** -100)))
    whole = jnp.round(values * jnp.exp2(15.0 - power))
    whole = jnp.clip(whole, -32767.0, 32767.0).astype(jnp.int32)
    word = (whole[:half] & 0xFFFF) | (whole[half:] << 16)
    for column in range(kept // LANES):
        word_ref[column * half:(column + 1) * half] = word[:, column * LANES:(column + 1) * LANES]
    group = lax.broadcasted_iota(jnp.int32, (8, LANES), 1) // (LANES * 8 // size)
    tile = jnp.zeros((8, LANES), jnp.int32)
    for at in range(size // 8):
        tile = jnp.where(group == at, power[at * 8:(at + 1) * 8].astype(jnp.int32), tile)
    word_ref[kept // LANES * half:] = tile


def decode(word_ref, size):
    half = size // 2
    columns = word_ref.shape[0] // half
    word = jnp.concatenate([word_ref[at * half:(at + 1) * half] for at in range(columns)], axis=1)
    code = jnp.concatenate([(word << 16) >> 16, word >> 16], axis=0).astype(jnp.float32)
    tile = jnp.exp2(word_ref[columns * half:].astype(jnp.float32) - 15.0)
    lanes = LANES * 8 // size
    scale = jnp.concatenate([tile[:, at * lanes:at * lanes + 1] for at in range(size // 8)], axis=0)
    return code * scale


def first_kernel(stride, keep_ref, got_ref, total_ref, there_ref, here_ref, again_ref):
    size = total_ref.shape[0]
    digit = lax.rem(lax.axis_index("feat") // stride, 2)

    def piece(at):
        span = pl.ds(pl.multiple_of(at * size, size), size)
        return keep_ref[span, :] + got_ref[span, :]

    encode(piece(1 - digit), there_ref)
    again_ref[...] = there_ref[...]
    total = piece(digit)
    total_ref[...] = total
    encode(total, here_ref)


def square_kernel(total_ref, both_ref, z_ref, x_ref, sum_ref, out_ref):
    size = total_ref.shape[0]
    total = (total_ref[...] + decode(x_ref, size)) + (decode(z_ref, size) + decode(both_ref, size))
    sum_ref[...] = total
    encode(total, out_ref)


def middle_kernel(total_ref, word_ref, sum_ref, out_ref):
    total = total_ref[...] + decode(word_ref, total_ref.shape[0])
    sum_ref[...] = total
    encode(total, out_ref)


def last_kernel(scale, total_ref, word_ref, label_ref, *row_refs):
    size, kept = total_ref.shape
    row = ((total_ref[...] + decode(word_ref, size)) * scale).astype(jnp.bfloat16)
    me = lax.axis_index("feat")
    first = lax.rem(me, 2) * 2 * size + lax.rem(me // 2, 2) * size
    label = jnp.broadcast_to(label_ref[...].astype(jnp.float32), (8, LANES))
    label = pltpu.roll(label, lax.rem(LANES - first, LANES), 1)
    label = jnp.broadcast_to(label[:1], (LANES, LANES)).T[:size].astype(jnp.bfloat16)
    for row_ref in row_refs:
        row_ref[:, :kept] = row
        row_ref[:, kept:] = label


def local_call(kernel, name, *operands, out_shape):
    return pl.pallas_call(
        kernel,
        out_shape=out_shape,
        compiler_params=pltpu.CompilerParams(vmem_limit_bytes=VMEM_LIMIT),
        name=name,
    )(*operands)


def swap(array, even, odd=None):
    tok_count, feat_count = lax.axis_size("tok"), lax.axis_size("feat")
    bits = (even, odd or even)
    pairs = [
        (f * tok_count + t, (f ^ bits[f & 1][1]) * tok_count + (t ^ bits[f & 1][0]))
        for f in range(feat_count)
        for t in range(tok_count)
    ]
    return lax.ppermute(array, ("feat", "tok"), pairs)


def body(features, signs, columns, labels):
    rows, width = features.shape
    feat_count = lax.axis_size("feat")
    tok_count = lax.axis_size("tok")
    kept = columns.shape[0]
    shard = kept // feat_count
    size = rows // 4
    total_type = jax.ShapeDtypeStruct((size, kept), jnp.float32)
    word_type = jax.ShapeDtypeStruct((kept // LANES * (size // 2) + 8, LANES), jnp.int32)
    row_type = jax.ShapeDtypeStruct((size, kept + LANES), jnp.bfloat16)

    keep, got = partial_halves(features, signs, columns, feat_count)
    total, there, here, again = local_call(
        functools.partial(first_kernel, 2),
        "first_split",
        keep,
        got,
        out_shape=[total_type, word_type, word_type, word_type],
    )
    both = swap(again, (0, 10), (0, 6))
    z_word = swap(here, (0, 8), (0, 4))
    x_word = swap(there, (0, 2))
    total, word = local_call(
        square_kernel, "add_square", total, both, z_word, x_word, out_shape=[total_type, word_type]
    )
    word = swap(word, (0, 4), (0, 8))
    stride = 16
    while stride < feat_count:
        total, word = local_call(middle_kernel, "add_encode", total, word, out_shape=[total_type, word_type])
        word = swap(word, (0, stride))
        stride *= 2

    scale = 1.0 / math.sqrt(width * feat_count)
    own, *copies = local_call(
        functools.partial(last_kernel, scale),
        "sketch_rows",
        total,
        word,
        labels.reshape(1, rows),
        out_shape=[row_type] * 5,
    )
    stride = 2
    while stride < tok_count:
        copies = [jnp.concatenate([copies[0], swap(copies[0], (stride, 0))], axis=0)] * 4
        own = copies[0]
        stride *= 2
    far = swap(copies[0], (1, 3))
    second = swap(copies[1], (0, 2), (1, 0))
    third = swap(copies[2], (1, 0), (0, 2))
    crossed = swap(copies[3], (1, 1), (0, 3))
    pieces = [own, far, second, third] + [swap(block, (0, 1)) for block in (own, far, second)] + [crossed]
    concepts = C // tok_count
    gram = gram_blocks(pieces, concepts, shard, C / (rows * tok_count))
    return gram.reshape(concepts, shard, kept)


def solution(mesh):
    in_specs = (P("tok", "feat"), P("feat"), P(), P("tok", None))
    out_specs = P("tok", "feat", None)
    return jax.shard_map(body, mesh=mesh, in_specs=in_specs, out_specs=out_specs, check_vma=False)
```

```python
import functools
import math

import jax
import jax.numpy as jnp
from jax import lax
from jax.experimental import pallas as pl
from jax.experimental.pallas import tpu as pltpu
from jax.sharding import PartitionSpec as P

C = 32
LOW = 256
LANES = 128
VMEM_LIMIT = 48 * 1024 * 1024


def parity_sign(number, bit_count):
    shift = 1
    while shift < bit_count:
        shift *= 2
    while shift > 1:
        shift //= 2
        number = number ^ (number >> shift)
    return (1 - 2 * (number & 1)).astype(jnp.float32)


def add_products(x_ref, sign_ref, low, high, out_ref, part, wide):
    rows, kept = out_ref.shape
    blocks = wide // LOW
    stack = []
    for block in range(part * blocks, (part + 1) * blocks):
        cols = slice(block * LOW, (block + 1) * LOW)
        stack.append(x_ref[:, cols] * sign_ref[:, cols].astype(jnp.bfloat16))
    stack = jnp.concatenate(stack, axis=0)
    for group in range(kept // LOW):
        cols = slice(group * LOW, (group + 1) * LOW)
        products = jnp.dot(stack, low[:, cols], preferred_element_type=jnp.float32)
        total = None
        for at in range(blocks):
            row = part * blocks + at
            term = products[at * rows:(at + 1) * rows] * high[row:row + 1, cols]
            total = term if total is None else total + term
        if part > 0:
            total = total + out_ref[:, cols]
        out_ref[:, cols] = total


def send_kernel(total_bits, parts, x_hbm, s_hbm, col_hbm, send_ref, x_keep, signs, low, high, x_buf, col_buf, sems):
    half, kept = send_ref.shape
    wide = x_hbm.shape[1] // parts
    me = lax.axis_index("feat")
    mine = lax.rem(me, 2)
    col_copy = pltpu.make_async_copy(col_hbm, col_buf, sems.at[parts])
    sign_copy = pltpu.make_async_copy(s_hbm, signs, sems.at[parts + 1])
    col_copy.start()
    sign_copy.start()
    copies = []
    for part in range(parts):
        cols = pl.ds(part * wide, wide)
        rows = pl.ds(pl.multiple_of((1 - mine) * half, half), half)
        copies.append(pltpu.make_async_copy(x_hbm.at[rows, cols], x_buf.at[:, cols], sems.at[part]))
        copies[-1].start()
    rows = pl.ds(pl.multiple_of(mine * half, half), half)
    keep_copy = pltpu.make_async_copy(x_hbm.at[rows, :], x_keep, sems.at[parts + 2])
    keep_copy.start()
    col_copy.wait()
    col = col_buf[...]
    index = lax.broadcasted_iota(jnp.int32, (16, kept), 0)
    inner = parity_sign(index & col, 4)
    outer = parity_sign(index & (col >> 4), 4)
    for row in range(LOW // 16):
        low[row * 16:(row + 1) * 16] = (inner * outer[row:row + 1]).astype(jnp.bfloat16)
    high_index = lax.broadcasted_iota(jnp.int32, high.shape, 0) + me * high.shape[0]
    high[...] = parity_sign(high_index & (col >> 8), total_bits - 8)
    sign_copy.wait()
    for part in range(parts):
        copies[part].wait()
        add_products(x_buf, signs, low, high, send_ref, part, wide)
    keep_copy.wait()


def keep_kernel(parts, x_keep, signs, low, high, keep_ref):
    wide = x_keep.shape[1] // parts
    for part in range(parts):
        add_products(x_keep, signs, low, high, keep_ref, part, wide)


def partial_halves(features, signs, columns, feat_count):
    rows, width = features.shape
    kept = columns.shape[0]
    parts = max(1, width // 4096)
    half = rows // 2
    total_bits = (width * feat_count).bit_length() - 1
    params = pltpu.CompilerParams(vmem_limit_bytes=VMEM_LIMIT)
    cost = pl.CostEstimate(
        flops=2 * half * width * kept, bytes_accessed=2 * rows * width + 4 * half * kept, transcendentals=0
    )
    total_type = jax.ShapeDtypeStruct((half, kept), jnp.float32)
    send, *held = pl.pallas_call(
        functools.partial(send_kernel, total_bits, parts),
        in_specs=[pl.BlockSpec(memory_space=pltpu.HBM)] * 3,
        out_specs=[pl.BlockSpec(memory_space=pltpu.VMEM)] * 5,
        out_shape=[
            total_type,
            jax.ShapeDtypeStruct((half, width), jnp.bfloat16),
            jax.ShapeDtypeStruct((1, width), jnp.int32),
            jax.ShapeDtypeStruct((LOW, kept), jnp.bfloat16),
            jax.ShapeDtypeStruct((width // LOW, kept), jnp.float32),
        ],
        scratch_shapes=[
            pltpu.VMEM((half, width), jnp.bfloat16),
            pltpu.VMEM((1, kept), jnp.int32),
            pltpu.SemaphoreType.DMA((parts + 3,)),
        ],
        compiler_params=params,
        cost_estimate=cost,
        name="partial_sent",
    )(*(
        pltpu.with_memory_space_constraint(operand, pltpu.HBM)
        for operand in (features, signs.reshape(1, width), columns.reshape(1, kept))
    ))
    got = swap(send, (0, 1))
    keep = pl.pallas_call(
        functools.partial(keep_kernel, parts),
        out_shape=total_type,
        compiler_params=params,
        cost_estimate=cost,
        name="partial_kept",
    )(*held)
    return keep, got


def gram_kernel(shard, group, factor, *refs):
    pieces, (out_hbm, rows, blocks, sems) = refs[:-4], refs[-4:]
    steps, wide, kept = blocks.shape
    place = 0
    for piece in pieces:
        rows[place:place + piece.shape[0]] = piece[:, :kept]
        place += piece.shape[0]
    first = lax.axis_index("feat") * shard
    start = pl.multiple_of(first // LANES * LANES, LANES)
    window = rows[:, pl.ds(start, LANES)].astype(jnp.float32) * factor
    window = pltpu.roll(window, lax.rem(LANES - (first - start), LANES), 1)
    own = jnp.concatenate([window.T[:shard]] * group, axis=0)
    named = jnp.concatenate([piece[:, kept:].astype(jnp.float32) for piece in pieces], axis=0).T[:1]
    label = named.astype(jnp.int32) - lax.broadcasted_iota(jnp.int32, own.shape, 0) // shard
    base = lax.axis_index("tok") * steps * group
    copies = []
    for step in range(steps):
        chosen = jnp.where(label == base + step * group, own, 0.0).astype(jnp.bfloat16)
        blocks[step] = jnp.dot(chosen, rows[...], preferred_element_type=jnp.float32)
        copies.append(
            pltpu.make_async_copy(blocks.at[step], out_hbm.at[pl.ds(step * wide, wide), :], sems.at[step])
        )
        copies[-1].start()
    for copy in copies:
        copy.wait()


def gram_blocks(pieces, concepts, shard, factor):
    tokens = sum(piece.shape[0] for piece in pieces)
    kept = pieces[0].shape[1] - LANES
    group = max(1, min(concepts, LOW // shard))
    wide = group * shard
    steps = concepts // group
    return pl.pallas_call(
        functools.partial(gram_kernel, shard, group, factor),
        in_specs=[pl.BlockSpec(memory_space=pltpu.VMEM)] * len(pieces),
        out_specs=pl.BlockSpec(memory_space=pltpu.HBM),
        out_shape=jax.ShapeDtypeStruct((concepts * shard, kept), jnp.float32),
        scratch_shapes=[
            pltpu.VMEM((tokens, kept), jnp.bfloat16),
            pltpu.VMEM((steps, wide, kept), jnp.float32),
            pltpu.SemaphoreType.DMA((steps,)),
        ],
        compiler_params=pltpu.CompilerParams(vmem_limit_bytes=VMEM_LIMIT),
        cost_estimate=pl.CostEstimate(
            flops=2 * tokens * concepts * shard * kept, bytes_accessed=4 * concepts * shard * kept, transcendentals=0
        ),
        name="gram",
    )(*pieces)


def encode(values, word_ref):
    size, kept = values.shape
    half = size // 2
    top = jnp.max(jnp.abs(values), axis=1, keepdims=True)
    power = jnp.ceil(jnp.log2(jnp.maximum(top, 2.0 ** -100)))
    whole = jnp.round(values * jnp.exp2(15.0 - power))
    whole = jnp.clip(whole, -32767.0, 32767.0).astype(jnp.int32)
    word = (whole[:half] & 0xFFFF) | (whole[half:] << 16)
    for column in range(kept // LANES):
        word_ref[column * half:(column + 1) * half] = word[:, column * LANES:(column + 1) * LANES]
    group = lax.broadcasted_iota(jnp.int32, (8, LANES), 1) // (LANES * 8 // size)
    tile = jnp.zeros((8, LANES), jnp.int32)
    for at in range(size // 8):
        tile = jnp.where(group == at, power[at * 8:(at + 1) * 8].astype(jnp.int32), tile)
    word_ref[kept // LANES * half:] = tile


def decode(word_ref, size):
    half = size // 2
    columns = word_ref.shape[0] // half
    word = jnp.concatenate([word_ref[at * half:(at + 1) * half] for at in range(columns)], axis=1)
    code = jnp.concatenate([(word << 16) >> 16, word >> 16], axis=0).astype(jnp.float32)
    tile = jnp.exp2(word_ref[columns * half:].astype(jnp.float32) - 15.0)
    lanes = LANES * 8 // size
    scale = jnp.concatenate([tile[:, at * lanes:at * lanes + 1] for at in range(size // 8)], axis=0)
    return code * scale


def first_kernel(stride, keep_ref, got_ref, total_ref, there_ref, here_ref, again_ref):
    size = total_ref.shape[0]
    digit = lax.rem(lax.axis_index("feat") // stride, 2)

    def piece(at):
        span = pl.ds(pl.multiple_of(at * size, size), size)
        return keep_ref[span, :] + got_ref[span, :]

    encode(piece(1 - digit), there_ref)
    again_ref[...] = there_ref[...]
    total = piece(digit)
    total_ref[...] = total
    encode(total, here_ref)


def square_kernel(total_ref, both_ref, z_ref, x_ref, sum_ref, out_ref):
    size = total_ref.shape[0]
    total = (total_ref[...] + decode(x_ref, size)) + (decode(z_ref, size) + decode(both_ref, size))
    sum_ref[...] = total
    encode(total, out_ref)


def middle_kernel(total_ref, word_ref, sum_ref, out_ref):
    total = total_ref[...] + decode(word_ref, total_ref.shape[0])
    sum_ref[...] = total
    encode(total, out_ref)


def last_kernel(scale, total_ref, word_ref, label_ref, *row_refs):
    size, kept = total_ref.shape
    row = ((total_ref[...] + decode(word_ref, size)) * scale).astype(jnp.bfloat16)
    me = lax.axis_index("feat")
    first = lax.rem(me, 2) * 2 * size + lax.rem(me // 2, 2) * size
    label = jnp.broadcast_to(label_ref[...].astype(jnp.float32), (8, LANES))
    label = pltpu.roll(label, lax.rem(LANES - first, LANES), 1)
    label = jnp.broadcast_to(label[:1], (LANES, LANES)).T[:size].astype(jnp.bfloat16)
    for row_ref in row_refs:
        row_ref[:, :kept] = row
        row_ref[:, kept:] = label


def local_call(kernel, name, *operands, out_shape):
    return pl.pallas_call(
        kernel,
        out_shape=out_shape,
        compiler_params=pltpu.CompilerParams(vmem_limit_bytes=VMEM_LIMIT),
        name=name,
    )(*operands)


def swap(array, even, odd=None):
    tok_count, feat_count = lax.axis_size("tok"), lax.axis_size("feat")
    bits = (even, odd or even)
    pairs = [
        (f * tok_count + t, (f ^ bits[f & 1][1]) * tok_count + (t ^ bits[f & 1][0]))
        for f in range(feat_count)
        for t in range(tok_count)
    ]
    return lax.ppermute(array, ("feat", "tok"), pairs)


def body(features, signs, columns, labels):
    rows, width = features.shape
    feat_count = lax.axis_size("feat")
    tok_count = lax.axis_size("tok")
    kept = columns.shape[0]
    shard = kept // feat_count
    size = rows // 4
    total_type = jax.ShapeDtypeStruct((size, kept), jnp.float32)
    word_type = jax.ShapeDtypeStruct((kept // LANES * (size // 2) + 8, LANES), jnp.int32)
    row_type = jax.ShapeDtypeStruct((size, kept + LANES), jnp.bfloat16)

    keep, got = partial_halves(features, signs, columns, feat_count)
    total, there, here, again = local_call(
        functools.partial(first_kernel, 2),
        "first_split",
        keep,
        got,
        out_shape=[total_type, word_type, word_type, word_type],
    )
    both = swap(again, (0, 6), (0, 10))
    z_word = swap(here, (0, 4), (0, 8))
    x_word = swap(there, (0, 2))
    total, word = local_call(
        square_kernel, "add_square", total, both, z_word, x_word, out_shape=[total_type, word_type]
    )
    word = swap(word, (0, 8), (0, 4))
    stride = 16
    while stride < feat_count:
        total, word = local_call(middle_kernel, "add_encode", total, word, out_shape=[total_type, word_type])
        word = swap(word, (0, stride))
        stride *= 2

    scale = 1.0 / math.sqrt(width * feat_count)
    own, *copies = local_call(
        functools.partial(last_kernel, scale),
        "sketch_rows",
        total,
        word,
        labels.reshape(1, rows),
        out_shape=[row_type] * 5,
    )
    stride = 2
    while stride < tok_count:
        copies = [jnp.concatenate([copies[0], swap(copies[0], (stride, 0))], axis=0)] * 4
        own = copies[0]
        stride *= 2
    far = swap(copies[0], (1, 3))
    second = swap(copies[1], (0, 2), (1, 0))
    third = swap(copies[2], (1, 0), (0, 2))
    crossed = swap(copies[3], (1, 1), (0, 3))
    pieces = [own, far, second, third] + [swap(block, (0, 1)) for block in (own, far, second)] + [crossed]
    concepts = C // tok_count
    gram = gram_blocks(pieces, concepts, shard, C / (rows * tok_count))
    return gram.reshape(concepts, shard, kept)


def solution(mesh):
    in_specs = (P("tok", "feat"), P("feat"), P(), P("tok", None))
    out_specs = P("tok", "feat", None)
    return jax.shard_map(body, mesh=mesh, in_specs=in_specs, out_specs=out_specs, check_vma=False)
```

```python
import functools
import math

import jax
import jax.numpy as jnp
from jax import lax
from jax.experimental import pallas as pl
from jax.experimental.pallas import tpu as pltpu
from jax.sharding import PartitionSpec as P

C = 32
LOW = 256
LANES = 128
TILE = 16
VMEM_LIMIT = 48 * 1024 * 1024


def parity_sign(number, bit_count):
    shift = 1
    while shift < bit_count:
        shift *= 2
    while shift > 1:
        shift //= 2
        number = number ^ (number >> shift)
    return (1 - 2 * (number & 1)).astype(jnp.float32)


def add_products(x_ref, sign_ref, low, high, out_ref, part, wide):
    rows, kept = out_ref.shape
    blocks = wide // LOW
    stack = []
    for block in range(part * blocks, (part + 1) * blocks):
        cols = slice(block * LOW, (block + 1) * LOW)
        stack.append(x_ref[:, cols] * sign_ref[:, cols].astype(jnp.bfloat16))
    stack = jnp.concatenate(stack, axis=0)
    for group in range(kept // LOW):
        cols = slice(group * LOW, (group + 1) * LOW)
        products = jnp.dot(stack, low[:, cols], preferred_element_type=jnp.float32)
        total = None
        for at in range(blocks):
            row = part * blocks + at
            term = products[at * rows:(at + 1) * rows] * high[row:row + 1, cols]
            total = term if total is None else total + term
        if part > 0:
            total = total + out_ref[:, cols]
        out_ref[:, cols] = total


def send_kernel(total_bits, parts, x_hbm, s_hbm, col_hbm, send_ref, x_keep, signs, low, high, x_buf, col_buf, sems):
    half, kept = send_ref.shape
    wide = x_hbm.shape[1] // parts
    me = lax.axis_index("feat")
    mine = lax.rem(me, 2)
    col_copy = pltpu.make_async_copy(col_hbm, col_buf, sems.at[parts])
    sign_copy = pltpu.make_async_copy(s_hbm, signs, sems.at[parts + 1])
    col_copy.start()
    sign_copy.start()
    copies = []
    for part in range(parts):
        cols = pl.ds(part * wide, wide)
        rows = pl.ds(pl.multiple_of((1 - mine) * half, half), half)
        copies.append(pltpu.make_async_copy(x_hbm.at[rows, cols], x_buf.at[:, cols], sems.at[part]))
        copies[-1].start()
    rows = pl.ds(pl.multiple_of(mine * half, half), half)
    keep_copy = pltpu.make_async_copy(x_hbm.at[rows, :], x_keep, sems.at[parts + 2])
    keep_copy.start()
    col_copy.wait()
    col = col_buf[...]
    index = lax.broadcasted_iota(jnp.int32, (16, kept), 0)
    inner = parity_sign(index & col, 4)
    outer = parity_sign(index & (col >> 4), 4)
    for row in range(LOW // 16):
        low[row * 16:(row + 1) * 16] = (inner * outer[row:row + 1]).astype(jnp.bfloat16)
    high_index = lax.broadcasted_iota(jnp.int32, high.shape, 0) + me * high.shape[0]
    high[...] = parity_sign(high_index & (col >> 8), total_bits - 8)
    sign_copy.wait()
    for part in range(parts):
        copies[part].wait()
        add_products(x_buf, signs, low, high, send_ref, part, wide)
    keep_copy.wait()


def keep_kernel(parts, x_keep, signs, low, high, keep_ref):
    wide = x_keep.shape[1] // parts
    for part in range(parts):
        add_products(x_keep, signs, low, high, keep_ref, part, wide)


def partial_halves(features, signs, columns, feat_count):
    rows, width = features.shape
    kept = columns.shape[0]
    parts = max(1, width // 4096)
    half = rows // 2
    total_bits = (width * feat_count).bit_length() - 1
    params = pltpu.CompilerParams(vmem_limit_bytes=VMEM_LIMIT)
    cost = pl.CostEstimate(
        flops=2 * half * width * kept, bytes_accessed=2 * rows * width + 4 * half * kept, transcendentals=0
    )
    total_type = jax.ShapeDtypeStruct((half, kept), jnp.float32)
    send, *held = pl.pallas_call(
        functools.partial(send_kernel, total_bits, parts),
        in_specs=[pl.BlockSpec(memory_space=pltpu.HBM)] * 3,
        out_specs=[pl.BlockSpec(memory_space=pltpu.VMEM)] * 5,
        out_shape=[
            total_type,
            jax.ShapeDtypeStruct((half, width), jnp.bfloat16),
            jax.ShapeDtypeStruct((1, width), jnp.int32),
            jax.ShapeDtypeStruct((LOW, kept), jnp.bfloat16),
            jax.ShapeDtypeStruct((width // LOW, kept), jnp.float32),
        ],
        scratch_shapes=[
            pltpu.VMEM((half, width), jnp.bfloat16),
            pltpu.VMEM((1, kept), jnp.int32),
            pltpu.SemaphoreType.DMA((parts + 3,)),
        ],
        compiler_params=params,
        cost_estimate=cost,
        name="partial_sent",
    )(*(
        pltpu.with_memory_space_constraint(operand, pltpu.HBM)
        for operand in (features, signs.reshape(1, width), columns.reshape(1, kept))
    ))
    got = swap(send, (0, 1))
    keep = pl.pallas_call(
        functools.partial(keep_kernel, parts),
        out_shape=total_type,
        compiler_params=params,
        cost_estimate=cost,
        name="partial_kept",
    )(*held)
    return keep, got


def gram_kernel(shard, group, factor, size, *refs):
    pieces, (out_hbm, rows, blocks, sems) = refs[:-4], refs[-4:]
    steps, wide, kept = blocks.shape
    stride = kept // LANES * size + TILE
    lane = lax.broadcasted_iota(jnp.int32, (8, LANES), 1)
    place = 0
    names = []
    for piece in pieces:
        for start in range(0, piece.shape[0], stride):
            for column in range(kept // LANES):
                at = start + column * size
                rows[place:place + size, column * LANES:(column + 1) * LANES] = piece[at:at + size]
            named = piece[start + stride - TILE:start + stride].astype(jnp.float32)[:8]
            shift = place % LANES
            if shift == 0:
                names.append(named)
            else:
                names[-1] = jnp.where(lane // size == shift // size, pltpu.roll(named, shift, 1), names[-1])
            place += size
    named = jnp.concatenate(names, axis=1)[:1, :place]
    first = lax.axis_index("feat") * shard
    start = pl.multiple_of(first // LANES * LANES, LANES)
    window = rows[:, pl.ds(start, LANES)].astype(jnp.float32) * factor
    window = pltpu.roll(window, lax.rem(LANES - (first - start), LANES), 1)
    own = jnp.concatenate([window.T[:shard]] * group, axis=0)
    label = named.astype(jnp.int32) - lax.broadcasted_iota(jnp.int32, own.shape, 0) // shard
    base = lax.axis_index("tok") * steps * group
    copies = []
    for step in range(steps):
        chosen = jnp.where(label == base + step * group, own, 0.0).astype(jnp.bfloat16)
        blocks[step] = jnp.dot(chosen, rows[...], preferred_element_type=jnp.float32)
        copies.append(
            pltpu.make_async_copy(blocks.at[step], out_hbm.at[pl.ds(step * wide, wide), :], sems.at[step])
        )
        copies[-1].start()
    for copy in copies:
        copy.wait()


def gram_blocks(pieces, size, kept, concepts, shard, factor):
    tokens = sum(piece.shape[0] for piece in pieces) // (kept // LANES * size + TILE) * size
    group = max(1, min(concepts, LOW // shard))
    wide = group * shard
    steps = concepts // group
    return pl.pallas_call(
        functools.partial(gram_kernel, shard, group, factor, size),
        in_specs=[pl.BlockSpec(memory_space=pltpu.VMEM)] * len(pieces),
        out_specs=pl.BlockSpec(memory_space=pltpu.HBM),
        out_shape=jax.ShapeDtypeStruct((concepts * shard, kept), jnp.float32),
        scratch_shapes=[
            pltpu.VMEM((tokens, kept), jnp.bfloat16),
            pltpu.VMEM((steps, wide, kept), jnp.float32),
            pltpu.SemaphoreType.DMA((steps,)),
        ],
        compiler_params=pltpu.CompilerParams(vmem_limit_bytes=VMEM_LIMIT),
        cost_estimate=pl.CostEstimate(
            flops=2 * tokens * concepts * shard * kept, bytes_accessed=4 * concepts * shard * kept, transcendentals=0
        ),
        name="gram",
    )(*pieces)


def encode(values, word_ref):
    size, kept = values.shape
    half = size // 2
    top = jnp.max(jnp.abs(values), axis=1, keepdims=True)
    power = jnp.ceil(jnp.log2(jnp.maximum(top, 2.0 ** -100)))
    whole = jnp.round(values * jnp.exp2(15.0 - power))
    whole = jnp.clip(whole, -32767.0, 32767.0).astype(jnp.int32)
    word = (whole[:half] & 0xFFFF) | (whole[half:] << 16)
    for column in range(kept // LANES):
        word_ref[column * half:(column + 1) * half] = word[:, column * LANES:(column + 1) * LANES]
    group = lax.broadcasted_iota(jnp.int32, (8, LANES), 1) // (LANES * 8 // size)
    tile = jnp.zeros((8, LANES), jnp.int32)
    for at in range(size // 8):
        tile = jnp.where(group == at, power[at * 8:(at + 1) * 8].astype(jnp.int32), tile)
    word_ref[kept // LANES * half:] = tile


def decode(word_ref, size):
    half = size // 2
    columns = word_ref.shape[0] // half
    word = jnp.concatenate([word_ref[at * half:(at + 1) * half] for at in range(columns)], axis=1)
    code = jnp.concatenate([(word << 16) >> 16, word >> 16], axis=0).astype(jnp.float32)
    tile = jnp.exp2(word_ref[columns * half:].astype(jnp.float32) - 15.0)
    lanes = LANES * 8 // size
    scale = jnp.concatenate([tile[:, at * lanes:at * lanes + 1] for at in range(size // 8)], axis=0)
    return code * scale


def first_kernel(stride, keep_ref, got_ref, total_ref, there_ref, here_ref, again_ref):
    size = total_ref.shape[0]
    digit = lax.rem(lax.axis_index("feat") // stride, 2)

    def piece(at):
        span = pl.ds(pl.multiple_of(at * size, size), size)
        return keep_ref[span, :] + got_ref[span, :]

    encode(piece(1 - digit), there_ref)
    again_ref[...] = there_ref[...]
    total = piece(digit)
    total_ref[...] = total
    encode(total, here_ref)


def square_kernel(total_ref, both_ref, z_ref, x_ref, sum_ref, out_ref):
    size = total_ref.shape[0]
    total = (total_ref[...] + decode(x_ref, size)) + (decode(z_ref, size) + decode(both_ref, size))
    sum_ref[...] = total
    encode(total, out_ref)


def middle_kernel(total_ref, word_ref, sum_ref, out_ref):
    total = total_ref[...] + decode(word_ref, total_ref.shape[0])
    sum_ref[...] = total
    encode(total, out_ref)


def last_kernel(scale, total_ref, word_ref, label_ref, *row_refs):
    size, kept = total_ref.shape
    row = ((total_ref[...] + decode(word_ref, size)) * scale).astype(jnp.bfloat16)
    me = lax.axis_index("feat")
    first = lax.rem(me, 2) * 2 * size + lax.rem(me // 2, 2) * size
    label = jnp.broadcast_to(label_ref[...].astype(jnp.float32), (8, LANES))
    label = pltpu.roll(label, lax.rem(LANES - first, LANES), 1)
    label = jnp.broadcast_to(label[:1], (TILE, LANES)).astype(jnp.bfloat16)
    for row_ref in row_refs:
        for column in range(kept // LANES):
            row_ref[column * size:(column + 1) * size] = row[:, column * LANES:(column + 1) * LANES]
        row_ref[kept // LANES * size:] = label


def local_call(kernel, name, *operands, out_shape):
    return pl.pallas_call(
        kernel,
        out_shape=out_shape,
        compiler_params=pltpu.CompilerParams(vmem_limit_bytes=VMEM_LIMIT),
        name=name,
    )(*operands)


def swap(array, even, odd=None):
    tok_count, feat_count = lax.axis_size("tok"), lax.axis_size("feat")
    bits = (even, odd or even)
    pairs = [
        (f * tok_count + t, (f ^ bits[f & 1][1]) * tok_count + (t ^ bits[f & 1][0]))
        for f in range(feat_count)
        for t in range(tok_count)
    ]
    return lax.ppermute(array, ("feat", "tok"), pairs)


def body(features, signs, columns, labels):
    rows, width = features.shape
    feat_count = lax.axis_size("feat")
    tok_count = lax.axis_size("tok")
    kept = columns.shape[0]
    shard = kept // feat_count
    size = rows // 4
    total_type = jax.ShapeDtypeStruct((size, kept), jnp.float32)
    word_type = jax.ShapeDtypeStruct((kept // LANES * (size // 2) + 8, LANES), jnp.int32)
    row_type = jax.ShapeDtypeStruct((kept // LANES * size + TILE, LANES), jnp.bfloat16)

    keep, got = partial_halves(features, signs, columns, feat_count)
    total, there, here, again = local_call(
        functools.partial(first_kernel, 2),
        "first_split",
        keep,
        got,
        out_shape=[total_type, word_type, word_type, word_type],
    )
    both = swap(again, (0, 10), (0, 6))
    z_word = swap(here, (0, 8), (0, 4))
    x_word = swap(there, (0, 2))
    total, word = local_call(
        square_kernel, "add_square", total, both, z_word, x_word, out_shape=[total_type, word_type]
    )
    word = swap(word, (0, 4), (0, 8))
    stride = 16
    while stride < feat_count:
        total, word = local_call(middle_kernel, "add_encode", total, word, out_shape=[total_type, word_type])
        word = swap(word, (0, stride))
        stride *= 2

    scale = 1.0 / math.sqrt(width * feat_count)
    own, *copies = local_call(
        functools.partial(last_kernel, scale),
        "sketch_rows",
        total,
        word,
        labels.reshape(1, rows),
        out_shape=[row_type] * 5,
    )
    stride = 2
    while stride < tok_count:
        copies = [jnp.concatenate([copies[0], swap(copies[0], (stride, 0))], axis=0)] * 4
        own = copies[0]
        stride *= 2
    far = swap(copies[0], (1, 3))
    second = swap(copies[1], (0, 2), (1, 0))
    third = swap(copies[2], (1, 0), (0, 2))
    crossed = swap(copies[3], (1, 1), (0, 3))
    pieces = [own, far, second, third] + [swap(block, (0, 1)) for block in (own, far, second)] + [crossed]
    concepts = C // tok_count
    gram = gram_blocks(pieces, size, kept, concepts, shard, C / (rows * tok_count))
    return gram.reshape(concepts, shard, kept)


def solution(mesh):
    in_specs = (P("tok", "feat"), P("feat"), P(), P("tok", None))
    out_specs = P("tok", "feat", None)
    return jax.shard_map(body, mesh=mesh, in_specs=in_specs, out_specs=out_specs, check_vma=False)
```

```python
import functools
import math

import jax
import jax.numpy as jnp
from jax import lax
from jax.experimental import pallas as pl
from jax.experimental.pallas import tpu as pltpu
from jax.sharding import PartitionSpec as P

C = 32
LOW = 256
LANES = 128
TILE = 16
VMEM_LIMIT = 48 * 1024 * 1024


def parity_sign(number, bit_count):
    shift = 1
    while shift < bit_count:
        shift *= 2
    while shift > 1:
        shift //= 2
        number = number ^ (number >> shift)
    return (1 - 2 * (number & 1)).astype(jnp.float32)


def add_products(x_ref, sign_ref, low, high, out_ref, part, wide):
    rows, kept = out_ref.shape
    blocks = wide // LOW
    stack = []
    for block in range(part * blocks, (part + 1) * blocks):
        cols = slice(block * LOW, (block + 1) * LOW)
        stack.append(x_ref[:, cols] * sign_ref[:, cols].astype(jnp.bfloat16))
    stack = jnp.concatenate(stack, axis=0)
    for group in range(kept // LOW):
        cols = slice(group * LOW, (group + 1) * LOW)
        products = jnp.dot(stack, low[:, cols], preferred_element_type=jnp.float32)
        total = None
        for at in range(blocks):
            row = part * blocks + at
            term = products[at * rows:(at + 1) * rows] * high[row:row + 1, cols]
            total = term if total is None else total + term
        if part > 0:
            total = total + out_ref[:, cols]
        out_ref[:, cols] = total


def send_kernel(total_bits, parts, x_hbm, s_hbm, col_hbm, send_ref, x_keep, signs, low, high, x_buf, col_buf, sems):
    half, kept = send_ref.shape
    wide = x_hbm.shape[1] // parts
    me = lax.axis_index("feat")
    mine = lax.rem(me, 2)
    col_copy = pltpu.make_async_copy(col_hbm, col_buf, sems.at[parts])
    sign_copy = pltpu.make_async_copy(s_hbm, signs, sems.at[parts + 1])
    copies = []
    for part in range(parts):
        cols = pl.ds(part * wide, wide)
        rows = pl.ds(pl.multiple_of((1 - mine) * half, half), half)
        copies.append(pltpu.make_async_copy(x_hbm.at[rows, cols], x_buf.at[:, cols], sems.at[part]))
    for copy in (copies[0], col_copy, sign_copy, *copies[1:]):
        copy.start()
    rows = pl.ds(pl.multiple_of(mine * half, half), half)
    keep_copy = pltpu.make_async_copy(x_hbm.at[rows, :], x_keep, sems.at[parts + 2])
    keep_copy.start()
    col_copy.wait()
    col = col_buf[...]
    index = lax.broadcasted_iota(jnp.int32, (16, kept), 0)
    inner = parity_sign(index & col, 4)
    outer = parity_sign(index & (col >> 4), 4)
    for row in range(LOW // 16):
        low[row * 16:(row + 1) * 16] = (inner * outer[row:row + 1]).astype(jnp.bfloat16)
    high_index = lax.broadcasted_iota(jnp.int32, high.shape, 0) + me * high.shape[0]
    high[...] = parity_sign(high_index & (col >> 8), total_bits - 8)
    sign_copy.wait()
    for part in range(parts):
        copies[part].wait()
        add_products(x_buf, signs, low, high, send_ref, part, wide)
    keep_copy.wait()


def keep_kernel(parts, x_keep, signs, low, high, keep_ref):
    wide = x_keep.shape[1] // parts
    for part in range(parts):
        add_products(x_keep, signs, low, high, keep_ref, part, wide)


def partial_halves(features, signs, columns, feat_count):
    rows, width = features.shape
    kept = columns.shape[0]
    parts = max(1, width // 4096)
    half = rows // 2
    total_bits = (width * feat_count).bit_length() - 1
    params = pltpu.CompilerParams(vmem_limit_bytes=VMEM_LIMIT)
    cost = pl.CostEstimate(
        flops=2 * half * width * kept, bytes_accessed=2 * rows * width + 4 * half * kept, transcendentals=0
    )
    total_type = jax.ShapeDtypeStruct((half, kept), jnp.float32)
    send, *held = pl.pallas_call(
        functools.partial(send_kernel, total_bits, parts),
        in_specs=[pl.BlockSpec(memory_space=pltpu.HBM)] * 3,
        out_specs=[pl.BlockSpec(memory_space=pltpu.VMEM)] * 5,
        out_shape=[
            total_type,
            jax.ShapeDtypeStruct((half, width), jnp.bfloat16),
            jax.ShapeDtypeStruct((1, width), jnp.int32),
            jax.ShapeDtypeStruct((LOW, kept), jnp.bfloat16),
            jax.ShapeDtypeStruct((width // LOW, kept), jnp.float32),
        ],
        scratch_shapes=[
            pltpu.VMEM((half, width), jnp.bfloat16),
            pltpu.VMEM((1, kept), jnp.int32),
            pltpu.SemaphoreType.DMA((parts + 3,)),
        ],
        compiler_params=params,
        cost_estimate=cost,
        name="partial_sent",
    )(*(
        pltpu.with_memory_space_constraint(operand, pltpu.HBM)
        for operand in (features, signs.reshape(1, width), columns.reshape(1, kept))
    ))
    got = swap(send, (0, 1))
    keep = pl.pallas_call(
        functools.partial(keep_kernel, parts),
        out_shape=total_type,
        compiler_params=params,
        cost_estimate=cost,
        name="partial_kept",
    )(*held)
    return keep, got


def gram_kernel(shard, group, factor, size, *refs):
    pieces, (out_hbm, rows, blocks, sems) = refs[:-4], refs[-4:]
    steps, wide, kept = blocks.shape
    stride = kept // LANES * size + TILE
    lane = lax.broadcasted_iota(jnp.int32, (8, LANES), 1)
    place = 0
    names = []
    for piece in pieces:
        for start in range(0, piece.shape[0], stride):
            for column in range(kept // LANES):
                at = start + column * size
                rows[place:place + size, column * LANES:(column + 1) * LANES] = piece[at:at + size]
            named = piece[start + stride - TILE:start + stride].astype(jnp.float32)[:8]
            shift = place % LANES
            if shift == 0:
                names.append(named)
            else:
                names[-1] = jnp.where(lane // size == shift // size, pltpu.roll(named, shift, 1), names[-1])
            place += size
    named = jnp.concatenate(names, axis=1)[:1, :place]
    first = lax.axis_index("feat") * shard
    start = pl.multiple_of(first // LANES * LANES, LANES)
    window = rows[:, pl.ds(start, LANES)].astype(jnp.float32) * factor
    window = pltpu.roll(window, lax.rem(LANES - (first - start), LANES), 1)
    own = jnp.concatenate([window.T[:shard]] * group, axis=0)
    label = named.astype(jnp.int32) - lax.broadcasted_iota(jnp.int32, own.shape, 0) // shard
    base = lax.axis_index("tok") * steps * group
    copies = []
    for step in range(steps):
        chosen = jnp.where(label == base + step * group, own, 0.0).astype(jnp.bfloat16)
        blocks[step] = jnp.dot(chosen, rows[...], preferred_element_type=jnp.float32)
        copies.append(
            pltpu.make_async_copy(blocks.at[step], out_hbm.at[pl.ds(step * wide, wide), :], sems.at[step])
        )
        copies[-1].start()
    for copy in copies:
        copy.wait()


def gram_blocks(pieces, size, kept, concepts, shard, factor):
    tokens = sum(piece.shape[0] for piece in pieces) // (kept // LANES * size + TILE) * size
    group = max(1, min(concepts, LOW // shard))
    wide = group * shard
    steps = concepts // group
    return pl.pallas_call(
        functools.partial(gram_kernel, shard, group, factor, size),
        in_specs=[pl.BlockSpec(memory_space=pltpu.VMEM)] * len(pieces),
        out_specs=pl.BlockSpec(memory_space=pltpu.HBM),
        out_shape=jax.ShapeDtypeStruct((concepts * shard, kept), jnp.float32),
        scratch_shapes=[
            pltpu.VMEM((tokens, kept), jnp.bfloat16),
            pltpu.VMEM((steps, wide, kept), jnp.float32),
            pltpu.SemaphoreType.DMA((steps,)),
        ],
        compiler_params=pltpu.CompilerParams(vmem_limit_bytes=VMEM_LIMIT),
        cost_estimate=pl.CostEstimate(
            flops=2 * tokens * concepts * shard * kept, bytes_accessed=4 * concepts * shard * kept, transcendentals=0
        ),
        name="gram",
    )(*pieces)


def encode(values, word_ref):
    size, kept = values.shape
    half = size // 2
    top = jnp.max(jnp.abs(values), axis=1, keepdims=True)
    power = jnp.ceil(jnp.log2(jnp.maximum(top, 2.0 ** -100)))
    whole = jnp.round(values * jnp.exp2(15.0 - power))
    whole = jnp.clip(whole, -32767.0, 32767.0).astype(jnp.int32)
    word = (whole[:half] & 0xFFFF) | (whole[half:] << 16)
    for column in range(kept // LANES):
        word_ref[column * half:(column + 1) * half] = word[:, column * LANES:(column + 1) * LANES]
    group = lax.broadcasted_iota(jnp.int32, (8, LANES), 1) // (LANES * 8 // size)
    tile = jnp.zeros((8, LANES), jnp.int32)
    for at in range(size // 8):
        tile = jnp.where(group == at, power[at * 8:(at + 1) * 8].astype(jnp.int32), tile)
    word_ref[kept // LANES * half:] = tile


def decode(word_ref, size):
    half = size // 2
    columns = word_ref.shape[0] // half
    word = jnp.concatenate([word_ref[at * half:(at + 1) * half] for at in range(columns)], axis=1)
    code = jnp.concatenate([(word << 16) >> 16, word >> 16], axis=0).astype(jnp.float32)
    tile = jnp.exp2(word_ref[columns * half:].astype(jnp.float32) - 15.0)
    lanes = LANES * 8 // size
    scale = jnp.concatenate([tile[:, at * lanes:at * lanes + 1] for at in range(size // 8)], axis=0)
    return code * scale


def first_kernel(stride, keep_ref, got_ref, total_ref, there_ref, here_ref, again_ref):
    size = total_ref.shape[0]
    digit = lax.rem(lax.axis_index("feat") // stride, 2)

    def piece(at):
        span = pl.ds(pl.multiple_of(at * size, size), size)
        return keep_ref[span, :] + got_ref[span, :]

    encode(piece(1 - digit), there_ref)
    again_ref[...] = there_ref[...]
    total = piece(digit)
    total_ref[...] = total
    encode(total, here_ref)


def far_kernel(total_ref, far_ref, sum_ref):
    sum_ref[...] = total_ref[...] + decode(far_ref, total_ref.shape[0])


def square_kernel(total_ref, z_ref, x_ref, sum_ref, out_ref):
    size = total_ref.shape[0]
    total = total_ref[...] + (decode(z_ref, size) + decode(x_ref, size))
    sum_ref[...] = total
    encode(total, out_ref)


def middle_kernel(total_ref, word_ref, sum_ref, out_ref):
    total = total_ref[...] + decode(word_ref, total_ref.shape[0])
    sum_ref[...] = total
    encode(total, out_ref)


def last_kernel(scale, total_ref, word_ref, label_ref, *row_refs):
    size, kept = total_ref.shape
    row = ((total_ref[...] + decode(word_ref, size)) * scale).astype(jnp.bfloat16)
    me = lax.axis_index("feat")
    first = lax.rem(me, 2) * 2 * size + lax.rem(me // 2, 2) * size
    label = jnp.broadcast_to(label_ref[...].astype(jnp.float32), (8, LANES))
    label = pltpu.roll(label, lax.rem(LANES - first, LANES), 1)
    label = jnp.broadcast_to(label[:1], (TILE, LANES)).astype(jnp.bfloat16)
    for row_ref in row_refs:
        for column in range(kept // LANES):
            row_ref[column * size:(column + 1) * size] = row[:, column * LANES:(column + 1) * LANES]
        row_ref[kept // LANES * size:] = label


def local_call(kernel, name, *operands, out_shape):
    return pl.pallas_call(
        kernel,
        out_shape=out_shape,
        compiler_params=pltpu.CompilerParams(vmem_limit_bytes=VMEM_LIMIT),
        name=name,
    )(*operands)


def swap(array, even, odd=None):
    tok_count, feat_count = lax.axis_size("tok"), lax.axis_size("feat")
    bits = (even, odd or even)
    pairs = [
        (f * tok_count + t, (f ^ bits[f & 1][1]) * tok_count + (t ^ bits[f & 1][0]))
        for f in range(feat_count)
        for t in range(tok_count)
    ]
    return lax.ppermute(array, ("feat", "tok"), pairs)


def body(features, signs, columns, labels):
    rows, width = features.shape
    feat_count = lax.axis_size("feat")
    tok_count = lax.axis_size("tok")
    kept = columns.shape[0]
    shard = kept // feat_count
    size = rows // 4
    total_type = jax.ShapeDtypeStruct((size, kept), jnp.float32)
    word_type = jax.ShapeDtypeStruct((kept // LANES * (size // 2) + 8, LANES), jnp.int32)
    row_type = jax.ShapeDtypeStruct((kept // LANES * size + TILE, LANES), jnp.bfloat16)

    keep, got = partial_halves(features, signs, columns, feat_count)
    total, there, here, again = local_call(
        functools.partial(first_kernel, 2),
        "first_split",
        keep,
        got,
        out_shape=[total_type, word_type, word_type, word_type],
    )
    both = swap(again, (0, 10), (0, 6))
    z_word = swap(here, (0, 8), (0, 4))
    x_word = swap(there, (0, 2))
    total = local_call(far_kernel, "add_far", total, both, out_shape=total_type)
    total, word = local_call(
        square_kernel, "add_square", total, z_word, x_word, out_shape=[total_type, word_type]
    )
    word = swap(word, (0, 4), (0, 8))
    stride = 16
    while stride < feat_count:
        total, word = local_call(middle_kernel, "add_encode", total, word, out_shape=[total_type, word_type])
        word = swap(word, (0, stride))
        stride *= 2

    scale = 1.0 / math.sqrt(width * feat_count)
    own, *copies = local_call(
        functools.partial(last_kernel, scale),
        "sketch_rows",
        total,
        word,
        labels.reshape(1, rows),
        out_shape=[row_type] * 5,
    )
    stride = 2
    while stride < tok_count:
        copies = [jnp.concatenate([copies[0], swap(copies[0], (stride, 0))], axis=0)] * 4
        own = copies[0]
        stride *= 2
    far = swap(copies[0], (1, 3))
    second = swap(copies[1], (0, 2), (1, 0))
    third = swap(copies[2], (1, 0), (0, 2))
    crossed = swap(copies[3], (1, 1), (0, 3))
    pieces = [own, far, second, third] + [swap(block, (0, 1)) for block in (own, far, second)] + [crossed]
    concepts = C // tok_count
    gram = gram_blocks(pieces, size, kept, concepts, shard, C / (rows * tok_count))
    return gram.reshape(concepts, shard, kept)


def solution(mesh):
    in_specs = (P("tok", "feat"), P("feat"), P(), P("tok", None))
    out_specs = P("tok", "feat", None)
    return jax.shard_map(body, mesh=mesh, in_specs=in_specs, out_specs=out_specs, check_vma=False)
```

```python
import functools
import math

import jax
import jax.numpy as jnp
from jax import lax
from jax.experimental import pallas as pl
from jax.experimental.pallas import tpu as pltpu
from jax.sharding import PartitionSpec as P

C = 32
LOW = 256
LANES = 128
TILE = 16
VMEM_LIMIT = 48 * 1024 * 1024


def parity_sign(number, bit_count):
    shift = 1
    while shift < bit_count:
        shift *= 2
    while shift > 1:
        shift //= 2
        number = number ^ (number >> shift)
    return (1 - 2 * (number & 1)).astype(jnp.float32)


def add_products(x_ref, sign_ref, low, high, out_ref, part, wide):
    rows, kept = out_ref.shape
    blocks = wide // LOW
    stack = []
    for block in range(part * blocks, (part + 1) * blocks):
        cols = slice(block * LOW, (block + 1) * LOW)
        stack.append(x_ref[:, cols] * sign_ref[:, cols].astype(jnp.bfloat16))
    stack = jnp.concatenate(stack, axis=0)
    for group in range(kept // LOW):
        cols = slice(group * LOW, (group + 1) * LOW)
        products = jnp.dot(stack, low[:, cols], preferred_element_type=jnp.float32)
        total = None
        for at in range(blocks):
            row = part * blocks + at
            term = products[at * rows:(at + 1) * rows] * high[row:row + 1, cols]
            total = term if total is None else total + term
        if part > 0:
            total = total + out_ref[:, cols]
        out_ref[:, cols] = total


def send_kernel(total_bits, parts, x_hbm, s_hbm, col_hbm, send_ref, x_keep, signs, low, high, x_buf, col_buf, sems):
    half, kept = send_ref.shape
    wide = x_hbm.shape[1] // parts
    me = lax.axis_index("feat")
    mine = lax.rem(me, 2)
    col_copy = pltpu.make_async_copy(col_hbm, col_buf, sems.at[parts])
    sign_copy = pltpu.make_async_copy(s_hbm, signs, sems.at[parts + 1])
    copies = []
    for part in range(parts):
        cols = pl.ds(part * wide, wide)
        rows = pl.ds(pl.multiple_of((1 - mine) * half, half), half)
        copies.append(pltpu.make_async_copy(x_hbm.at[rows, cols], x_buf.at[:, cols], sems.at[part]))
    for copy in (copies[0], col_copy, sign_copy, *copies[1:]):
        copy.start()
    rows = pl.ds(pl.multiple_of(mine * half, half), half)
    keep_copy = pltpu.make_async_copy(x_hbm.at[rows, :], x_keep, sems.at[parts + 2])
    keep_copy.start()
    col_copy.wait()
    col = col_buf[...]
    index = lax.broadcasted_iota(jnp.int32, (16, kept), 0)
    inner = parity_sign(index & col, 4)
    outer = parity_sign(index & (col >> 4), 4)
    for row in range(LOW // 16):
        low[row * 16:(row + 1) * 16] = (inner * outer[row:row + 1]).astype(jnp.bfloat16)
    high_index = lax.broadcasted_iota(jnp.int32, high.shape, 0) + me * high.shape[0]
    high[...] = parity_sign(high_index & (col >> 8), total_bits - 8)
    sign_copy.wait()
    for part in range(parts):
        copies[part].wait()
        add_products(x_buf, signs, low, high, send_ref, part, wide)
    keep_copy.wait()


def keep_kernel(parts, x_keep, signs, low, high, keep_ref):
    wide = x_keep.shape[1] // parts
    for part in range(parts):
        add_products(x_keep, signs, low, high, keep_ref, part, wide)


def partial_halves(features, signs, columns, feat_count):
    rows, width = features.shape
    kept = columns.shape[0]
    parts = max(1, width // 4096)
    half = rows // 2
    total_bits = (width * feat_count).bit_length() - 1
    params = pltpu.CompilerParams(vmem_limit_bytes=VMEM_LIMIT)
    cost = pl.CostEstimate(
        flops=2 * half * width * kept, bytes_accessed=2 * rows * width + 4 * half * kept, transcendentals=0
    )
    total_type = jax.ShapeDtypeStruct((half, kept), jnp.float32)
    send, *held = pl.pallas_call(
        functools.partial(send_kernel, total_bits, parts),
        in_specs=[pl.BlockSpec(memory_space=pltpu.HBM)] * 3,
        out_specs=[pl.BlockSpec(memory_space=pltpu.VMEM)] * 5,
        out_shape=[
            total_type,
            jax.ShapeDtypeStruct((half, width), jnp.bfloat16),
            jax.ShapeDtypeStruct((1, width), jnp.int32),
            jax.ShapeDtypeStruct((LOW, kept), jnp.bfloat16),
            jax.ShapeDtypeStruct((width // LOW, kept), jnp.float32),
        ],
        scratch_shapes=[
            pltpu.VMEM((half, width), jnp.bfloat16),
            pltpu.VMEM((1, kept), jnp.int32),
            pltpu.SemaphoreType.DMA((parts + 3,)),
        ],
        compiler_params=params,
        cost_estimate=cost,
        name="partial_sent",
    )(*(
        pltpu.with_memory_space_constraint(operand, pltpu.HBM)
        for operand in (features, signs.reshape(1, width), columns.reshape(1, kept))
    ))
    got = swap(send, (0, 1))
    keep = pl.pallas_call(
        functools.partial(keep_kernel, parts),
        out_shape=total_type,
        compiler_params=params,
        cost_estimate=cost,
        name="partial_kept",
    )(*held)
    return keep, got


def gram_kernel(shard, group, factor, size, *refs):
    pieces, (out_hbm, rows, blocks, sems) = refs[:-4], refs[-4:]
    steps, wide, kept = blocks.shape
    stride = kept // LANES * size + TILE
    lane = lax.broadcasted_iota(jnp.int32, (8, LANES), 1)
    place = 0
    names = []
    for piece in pieces:
        for start in range(0, piece.shape[0], stride):
            for column in range(kept // LANES):
                at = start + column * size
                rows[place:place + size, column * LANES:(column + 1) * LANES] = piece[at:at + size]
            named = piece[start + stride - TILE:start + stride].astype(jnp.float32)[:8]
            shift = place % LANES
            if shift == 0:
                names.append(named)
            else:
                names[-1] = jnp.where(lane // size == shift // size, pltpu.roll(named, shift, 1), names[-1])
            place += size
    named = jnp.concatenate(names, axis=1)[:1, :place]
    first = lax.axis_index("feat") * shard
    start = pl.multiple_of(first // LANES * LANES, LANES)
    window = rows[:, pl.ds(start, LANES)].astype(jnp.float32) * factor
    window = pltpu.roll(window, lax.rem(LANES - (first - start), LANES), 1)
    own = jnp.concatenate([window.T[:shard]] * group, axis=0)
    label = named.astype(jnp.int32) - lax.broadcasted_iota(jnp.int32, own.shape, 0) // shard
    base = lax.axis_index("tok") * steps * group
    copies = []
    for step in range(steps):
        chosen = jnp.where(label == base + step * group, own, 0.0).astype(jnp.bfloat16)
        blocks[step] = jnp.dot(chosen, rows[...], preferred_element_type=jnp.float32)
        copies.append(
            pltpu.make_async_copy(blocks.at[step], out_hbm.at[pl.ds(step * wide, wide), :], sems.at[step])
        )
        copies[-1].start()
    for copy in copies:
        copy.wait()


def gram_blocks(pieces, size, kept, concepts, shard, factor):
    tokens = sum(piece.shape[0] for piece in pieces) // (kept // LANES * size + TILE) * size
    group = max(1, min(concepts, LOW // shard))
    wide = group * shard
    steps = concepts // group
    return pl.pallas_call(
        functools.partial(gram_kernel, shard, group, factor, size),
        in_specs=[pl.BlockSpec(memory_space=pltpu.VMEM)] * len(pieces),
        out_specs=pl.BlockSpec(memory_space=pltpu.HBM),
        out_shape=jax.ShapeDtypeStruct((concepts * shard, kept), jnp.float32),
        scratch_shapes=[
            pltpu.VMEM((tokens, kept), jnp.bfloat16),
            pltpu.VMEM((steps, wide, kept), jnp.float32),
            pltpu.SemaphoreType.DMA((steps,)),
        ],
        compiler_params=pltpu.CompilerParams(vmem_limit_bytes=VMEM_LIMIT),
        cost_estimate=pl.CostEstimate(
            flops=2 * tokens * concepts * shard * kept, bytes_accessed=4 * concepts * shard * kept, transcendentals=0
        ),
        name="gram",
    )(*pieces)


def encode(values, word_ref):
    size, kept = values.shape
    half = size // 2
    top = jnp.max(jnp.abs(values), axis=1, keepdims=True)
    power = jnp.ceil(jnp.log2(jnp.maximum(top, 2.0 ** -100)))
    whole = jnp.round(values * jnp.exp2(15.0 - power))
    whole = jnp.clip(whole, -32767.0, 32767.0).astype(jnp.int32)
    word = (whole[:half] & 0xFFFF) | (whole[half:] << 16)
    for column in range(kept // LANES):
        word_ref[column * half:(column + 1) * half] = word[:, column * LANES:(column + 1) * LANES]
    group = lax.broadcasted_iota(jnp.int32, (8, LANES), 1) // (LANES * 8 // size)
    tile = jnp.zeros((8, LANES), jnp.int32)
    for at in range(size // 8):
        tile = jnp.where(group == at, power[at * 8:(at + 1) * 8].astype(jnp.int32), tile)
    word_ref[kept // LANES * half:] = tile


def decode(word_ref, size):
    half = size // 2
    columns = word_ref.shape[0] // half
    word = jnp.concatenate([word_ref[at * half:(at + 1) * half] for at in range(columns)], axis=1)
    code = jnp.concatenate([(word << 16) >> 16, word >> 16], axis=0).astype(jnp.float32)
    tile = jnp.exp2(word_ref[columns * half:].astype(jnp.float32) - 15.0)
    lanes = LANES * 8 // size
    scale = jnp.concatenate([tile[:, at * lanes:at * lanes + 1] for at in range(size // 8)], axis=0)
    return code * scale


def first_kernel(stride, keep_ref, got_ref, total_ref, there_ref, here_ref, again_ref):
    size = total_ref.shape[0]
    digit = lax.rem(lax.axis_index("feat") // stride, 2)

    def piece(at):
        span = pl.ds(pl.multiple_of(at * size, size), size)
        return keep_ref[span, :] + got_ref[span, :]

    encode(piece(1 - digit), there_ref)
    again_ref[...] = there_ref[...]
    total = piece(digit)
    total_ref[...] = total
    encode(total, here_ref)


def far_kernel(total_ref, far_ref, sum_ref):
    sum_ref[...] = total_ref[...] + decode(far_ref, total_ref.shape[0])


def square_kernel(total_ref, z_ref, x_ref, sum_ref, out_ref):
    size = total_ref.shape[0]
    total = total_ref[...] + (decode(z_ref, size) + decode(x_ref, size))
    sum_ref[...] = total
    encode(total, out_ref)


def middle_kernel(total_ref, word_ref, sum_ref, out_ref):
    total = total_ref[...] + decode(word_ref, total_ref.shape[0])
    sum_ref[...] = total
    encode(total, out_ref)


def last_kernel(scale, total_ref, word_ref, label_ref, *row_refs):
    size, kept = total_ref.shape
    row = ((total_ref[...] + decode(word_ref, size)) * scale).astype(jnp.bfloat16)
    me = lax.axis_index("feat")
    first = lax.rem(me, 2) * 2 * size + lax.rem(me // 2, 2) * size
    label = jnp.broadcast_to(label_ref[...].astype(jnp.float32), (8, LANES))
    label = pltpu.roll(label, lax.rem(LANES - first, LANES), 1)
    label = jnp.broadcast_to(label[:1], (TILE, LANES)).astype(jnp.bfloat16)
    for row_ref in row_refs:
        for column in range(kept // LANES):
            row_ref[column * size:(column + 1) * size] = row[:, column * LANES:(column + 1) * LANES]
        row_ref[kept // LANES * size:] = label


def local_call(kernel, name, *operands, out_shape):
    return pl.pallas_call(
        kernel,
        out_shape=out_shape,
        compiler_params=pltpu.CompilerParams(vmem_limit_bytes=VMEM_LIMIT),
        name=name,
    )(*operands)


def swap(array, even, odd=None):
    tok_count, feat_count = lax.axis_size("tok"), lax.axis_size("feat")
    bits = (even, odd or even)
    pairs = [
        (f * tok_count + t, (f ^ bits[f & 1][1]) * tok_count + (t ^ bits[f & 1][0]))
        for f in range(feat_count)
        for t in range(tok_count)
    ]
    return lax.ppermute(array, ("feat", "tok"), pairs)


def body(features, signs, columns, labels):
    rows, width = features.shape
    feat_count = lax.axis_size("feat")
    tok_count = lax.axis_size("tok")
    kept = columns.shape[0]
    shard = kept // feat_count
    size = rows // 4
    total_type = jax.ShapeDtypeStruct((size, kept), jnp.float32)
    word_type = jax.ShapeDtypeStruct((kept // LANES * (size // 2) + 8, LANES), jnp.int32)
    row_type = jax.ShapeDtypeStruct((kept // LANES * size + TILE, LANES), jnp.bfloat16)

    keep, got = partial_halves(features, signs, columns, feat_count)
    total, there, here, again = local_call(
        functools.partial(first_kernel, 2),
        "first_split",
        keep,
        got,
        out_shape=[total_type, word_type, word_type, word_type],
    )
    both = swap(again, (0, 10), (0, 6))
    z_word = swap(here, (0, 8), (0, 4))
    x_word = swap(there, (0, 2))
    total = local_call(far_kernel, "add_far", total, both, out_shape=total_type)
    total, word = local_call(
        square_kernel, "add_square", total, z_word, x_word, out_shape=[total_type, word_type]
    )
    word = swap(word, (0, 4), (0, 8))
    stride = 16
    while stride < feat_count:
        total, word = local_call(middle_kernel, "add_encode", total, word, out_shape=[total_type, word_type])
        word = swap(word, (0, stride))
        stride *= 2

    scale = 1.0 / math.sqrt(width * feat_count)
    own, *copies = local_call(
        functools.partial(last_kernel, scale),
        "sketch_rows",
        total,
        word,
        labels.reshape(1, rows),
        out_shape=[row_type] * 4,
    )
    stride = 2
    while stride < tok_count:
        copies = [jnp.concatenate([copies[0], swap(copies[0], (stride, 0))], axis=0)] * 3
        own = copies[0]
        stride *= 2
    crossed = swap(copies[0], (1, 1), (0, 3))
    far = swap(copies[1], (1, 2))
    second = swap(copies[2], (0, 2), (1, 0))
    pieces = [own, crossed, far, second]
    pieces += [swap(block, (0, 1)) for block in pieces]
    concepts = C // tok_count
    gram = gram_blocks(pieces, size, kept, concepts, shard, C / (rows * tok_count))
    return gram.reshape(concepts, shard, kept)


def solution(mesh):
    in_specs = (P("tok", "feat"), P("feat"), P(), P("tok", None))
    out_specs = P("tok", "feat", None)
    return jax.shard_map(body, mesh=mesh, in_specs=in_specs, out_specs=out_specs, check_vma=False)
```

```python
import functools
import math

import jax
import jax.numpy as jnp
from jax import lax
from jax.experimental import pallas as pl
from jax.experimental.pallas import tpu as pltpu
from jax.sharding import PartitionSpec as P

C = 32
LOW = 256
LANES = 128
TILE = 16
VMEM_LIMIT = 48 * 1024 * 1024


def parity_sign(number, bit_count):
    shift = 1
    while shift < bit_count:
        shift *= 2
    while shift > 1:
        shift //= 2
        number = number ^ (number >> shift)
    return (1 - 2 * (number & 1)).astype(jnp.float32)


def add_products(x_ref, sign_ref, low, high, out_ref, part, wide):
    rows, kept = out_ref.shape
    blocks = wide // LOW
    stack = []
    for block in range(part * blocks, (part + 1) * blocks):
        cols = slice(block * LOW, (block + 1) * LOW)
        stack.append(x_ref[:, cols] * sign_ref[:, cols].astype(jnp.bfloat16))
    stack = jnp.concatenate(stack, axis=0)
    for group in range(kept // LOW):
        cols = slice(group * LOW, (group + 1) * LOW)
        products = jnp.dot(stack, low[:, cols], preferred_element_type=jnp.float32)
        total = None
        for at in range(blocks):
            row = part * blocks + at
            term = products[at * rows:(at + 1) * rows] * high[row:row + 1, cols]
            total = term if total is None else total + term
        if part > 0:
            total = total + out_ref[:, cols]
        out_ref[:, cols] = total


def send_kernel(total_bits, parts, x_hbm, s_hbm, col_hbm, send_ref, x_keep, signs, low, high, x_buf, col_buf, sems):
    half, kept = send_ref.shape
    wide = x_hbm.shape[1] // parts
    me = lax.axis_index("feat")
    mine = lax.rem(me, 2)
    col_copy = pltpu.make_async_copy(col_hbm, col_buf, sems.at[parts])
    sign_copy = pltpu.make_async_copy(s_hbm, signs, sems.at[parts + 1])
    col_copy.start()
    sign_copy.start()
    copies = []
    for part in range(parts):
        cols = pl.ds(part * wide, wide)
        rows = pl.ds(pl.multiple_of((1 - mine) * half, half), half)
        copies.append(pltpu.make_async_copy(x_hbm.at[rows, cols], x_buf.at[:, cols], sems.at[part]))
        copies[-1].start()
    rows = pl.ds(pl.multiple_of(mine * half, half), half)
    keep_copy = pltpu.make_async_copy(x_hbm.at[rows, :], x_keep, sems.at[parts + 2])
    keep_copy.start()
    col_copy.wait()
    col = col_buf[...]
    index = lax.broadcasted_iota(jnp.int32, (16, kept), 0)
    inner = parity_sign(index & col, 4)
    outer = parity_sign(index & (col >> 4), 4)
    for row in range(LOW // 16):
        low[row * 16:(row + 1) * 16] = (inner * outer[row:row + 1]).astype(jnp.bfloat16)
    high_index = lax.broadcasted_iota(jnp.int32, high.shape, 0) + me * high.shape[0]
    high[...] = parity_sign(high_index & (col >> 8), total_bits - 8)
    sign_copy.wait()
    for part in range(parts):
        copies[part].wait()
        add_products(x_buf, signs, low, high, send_ref, part, wide)
    keep_copy.wait()


def keep_kernel(parts, x_keep, signs, low, high, keep_ref):
    wide = x_keep.shape[1] // parts
    for part in range(parts):
        add_products(x_keep, signs, low, high, keep_ref, part, wide)


def partial_halves(features, signs, columns, feat_count):
    rows, width = features.shape
    kept = columns.shape[0]
    parts = max(1, width // 4096)
    half = rows // 2
    total_bits = (width * feat_count).bit_length() - 1
    params = pltpu.CompilerParams(vmem_limit_bytes=VMEM_LIMIT)
    cost = pl.CostEstimate(
        flops=2 * half * width * kept, bytes_accessed=2 * rows * width + 4 * half * kept, transcendentals=0
    )
    total_type = jax.ShapeDtypeStruct((half, kept), jnp.float32)
    send, *held = pl.pallas_call(
        functools.partial(send_kernel, total_bits, parts),
        in_specs=[pl.BlockSpec(memory_space=pltpu.HBM)] * 3,
        out_specs=[pl.BlockSpec(memory_space=pltpu.VMEM)] * 5,
        out_shape=[
            total_type,
            jax.ShapeDtypeStruct((half, width), jnp.bfloat16),
            jax.ShapeDtypeStruct((1, width), jnp.int32),
            jax.ShapeDtypeStruct((LOW, kept), jnp.bfloat16),
            jax.ShapeDtypeStruct((width // LOW, kept), jnp.float32),
        ],
        scratch_shapes=[
            pltpu.VMEM((half, width), jnp.bfloat16),
            pltpu.VMEM((1, kept), jnp.int32),
            pltpu.SemaphoreType.DMA((parts + 3,)),
        ],
        compiler_params=params,
        cost_estimate=cost,
        name="partial_sent",
    )(*(
        pltpu.with_memory_space_constraint(operand, pltpu.HBM)
        for operand in (features, signs.reshape(1, width), columns.reshape(1, kept))
    ))
    got = swap(send, (0, 1))
    keep = pl.pallas_call(
        functools.partial(keep_kernel, parts),
        out_shape=total_type,
        compiler_params=params,
        cost_estimate=cost,
        name="partial_kept",
    )(*held)
    return keep, got


def gram_kernel(shard, group, factor, size, *refs):
    pieces, (out_hbm, rows, blocks, sems) = refs[:-4], refs[-4:]
    steps, wide, kept = blocks.shape
    stride = kept // LANES * size + TILE
    lane = lax.broadcasted_iota(jnp.int32, (8, LANES), 1)
    place = 0
    names = []
    for piece in pieces:
        for start in range(0, piece.shape[0], stride):
            for column in range(kept // LANES):
                at = start + column * size
                rows[place:place + size, column * LANES:(column + 1) * LANES] = piece[at:at + size]
            named = piece[start + stride - TILE:start + stride].astype(jnp.float32)[:8]
            shift = place % LANES
            if shift == 0:
                names.append(named)
            else:
                names[-1] = jnp.where(lane // size == shift // size, pltpu.roll(named, shift, 1), names[-1])
            place += size
    named = jnp.concatenate(names, axis=1)[:1, :place]
    first = lax.axis_index("feat") * shard
    start = pl.multiple_of(first // LANES * LANES, LANES)
    window = rows[:, pl.ds(start, LANES)].astype(jnp.float32) * factor
    window = pltpu.roll(window, lax.rem(LANES - (first - start), LANES), 1)
    own = jnp.concatenate([window.T[:shard]] * group, axis=0)
    label = named.astype(jnp.int32) - lax.broadcasted_iota(jnp.int32, own.shape, 0) // shard
    base = lax.axis_index("tok") * steps * group
    copies = []
    for step in range(steps):
        chosen = jnp.where(label == base + step * group, own, 0.0).astype(jnp.bfloat16)
        blocks[step] = jnp.dot(chosen, rows[...], preferred_element_type=jnp.float32)
        copies.append(
            pltpu.make_async_copy(blocks.at[step], out_hbm.at[pl.ds(step * wide, wide), :], sems.at[step])
        )
        copies[-1].start()
    for copy in copies:
        copy.wait()


def gram_blocks(pieces, size, kept, concepts, shard, factor):
    tokens = sum(piece.shape[0] for piece in pieces) // (kept // LANES * size + TILE) * size
    group = max(1, min(concepts, LOW // shard))
    wide = group * shard
    steps = concepts // group
    return pl.pallas_call(
        functools.partial(gram_kernel, shard, group, factor, size),
        in_specs=[pl.BlockSpec(memory_space=pltpu.VMEM)] * len(pieces),
        out_specs=pl.BlockSpec(memory_space=pltpu.HBM),
        out_shape=jax.ShapeDtypeStruct((concepts * shard, kept), jnp.float32),
        scratch_shapes=[
            pltpu.VMEM((tokens, kept), jnp.bfloat16),
            pltpu.VMEM((steps, wide, kept), jnp.float32),
            pltpu.SemaphoreType.DMA((steps,)),
        ],
        compiler_params=pltpu.CompilerParams(vmem_limit_bytes=VMEM_LIMIT),
        cost_estimate=pl.CostEstimate(
            flops=2 * tokens * concepts * shard * kept, bytes_accessed=4 * concepts * shard * kept, transcendentals=0
        ),
        name="gram",
    )(*pieces)


def encode(values, word_ref):
    size, kept = values.shape
    half = size // 2
    top = jnp.max(jnp.abs(values), axis=1, keepdims=True)
    power = jnp.ceil(jnp.log2(jnp.maximum(top, 2.0 ** -100)))
    whole = jnp.round(values * jnp.exp2(15.0 - power))
    whole = jnp.clip(whole, -32767.0, 32767.0).astype(jnp.int32)
    word = (whole[:half] & 0xFFFF) | (whole[half:] << 16)
    for column in range(kept // LANES):
        word_ref[column * half:(column + 1) * half] = word[:, column * LANES:(column + 1) * LANES]
    group = lax.broadcasted_iota(jnp.int32, (8, LANES), 1) // (LANES * 8 // size)
    tile = jnp.zeros((8, LANES), jnp.int32)
    for at in range(size // 8):
        tile = jnp.where(group == at, power[at * 8:(at + 1) * 8].astype(jnp.int32), tile)
    word_ref[kept // LANES * half:] = tile


def decode(word_ref, size):
    half = size // 2
    columns = word_ref.shape[0] // half
    word = jnp.concatenate([word_ref[at * half:(at + 1) * half] for at in range(columns)], axis=1)
    code = jnp.concatenate([(word << 16) >> 16, word >> 16], axis=0).astype(jnp.float32)
    tile = jnp.exp2(word_ref[columns * half:].astype(jnp.float32) - 15.0)
    lanes = LANES * 8 // size
    scale = jnp.concatenate([tile[:, at * lanes:at * lanes + 1] for at in range(size // 8)], axis=0)
    return code * scale


def first_kernel(stride, keep_ref, got_ref, total_ref, there_ref, here_ref, again_ref):
    size = total_ref.shape[0]
    digit = lax.rem(lax.axis_index("feat") // stride, 2)

    def piece(at):
        span = pl.ds(pl.multiple_of(at * size, size), size)
        return keep_ref[span, :] + got_ref[span, :]

    encode(piece(1 - digit), there_ref)
    again_ref[...] = there_ref[...]
    total = piece(digit)
    total_ref[...] = total
    encode(total, here_ref)


def square_kernel(total_ref, both_ref, z_ref, x_ref, sum_ref, out_ref):
    size = total_ref.shape[0]
    total = (total_ref[...] + decode(x_ref, size)) + (decode(z_ref, size) + decode(both_ref, size))
    sum_ref[...] = total
    encode(total, out_ref)


def middle_kernel(total_ref, word_ref, sum_ref, out_ref):
    total = total_ref[...] + decode(word_ref, total_ref.shape[0])
    sum_ref[...] = total
    encode(total, out_ref)


def last_kernel(scale, total_ref, word_ref, label_ref, *row_refs):
    size, kept = total_ref.shape
    row = ((total_ref[...] + decode(word_ref, size)) * scale).astype(jnp.bfloat16)
    me = lax.axis_index("feat")
    first = lax.rem(me, 2) * 2 * size + lax.rem(me // 2, 2) * size
    label = jnp.broadcast_to(label_ref[...].astype(jnp.float32), (8, LANES))
    label = pltpu.roll(label, lax.rem(LANES - first, LANES), 1)
    label = jnp.broadcast_to(label[:1], (TILE, LANES)).astype(jnp.bfloat16)
    for row_ref in row_refs:
        for column in range(kept // LANES):
            row_ref[column * size:(column + 1) * size] = row[:, column * LANES:(column + 1) * LANES]
        row_ref[kept // LANES * size:] = label


def local_call(kernel, name, *operands, out_shape):
    return pl.pallas_call(
        kernel,
        out_shape=out_shape,
        compiler_params=pltpu.CompilerParams(vmem_limit_bytes=VMEM_LIMIT),
        name=name,
    )(*operands)


def swap(array, even, odd=None):
    tok_count, feat_count = lax.axis_size("tok"), lax.axis_size("feat")
    bits = (even, odd or even)
    pairs = [
        (f * tok_count + t, (f ^ bits[f & 1][1]) * tok_count + (t ^ bits[f & 1][0]))
        for f in range(feat_count)
        for t in range(tok_count)
    ]
    return lax.ppermute(array, ("feat", "tok"), pairs)


def body(features, signs, columns, labels):
    rows, width = features.shape
    feat_count = lax.axis_size("feat")
    tok_count = lax.axis_size("tok")
    kept = columns.shape[0]
    shard = kept // feat_count
    size = rows // 4
    total_type = jax.ShapeDtypeStruct((size, kept), jnp.float32)
    word_type = jax.ShapeDtypeStruct((kept // LANES * (size // 2) + 8, LANES), jnp.int32)
    row_type = jax.ShapeDtypeStruct((kept // LANES * size + TILE, LANES), jnp.bfloat16)

    keep, got = partial_halves(features, signs, columns, feat_count)
    total, there, here, again = local_call(
        functools.partial(first_kernel, 2),
        "first_split",
        keep,
        got,
        out_shape=[total_type, word_type, word_type, word_type],
    )
    both = swap(again, (0, 10), (0, 6))
    z_word = swap(here, (0, 8), (0, 4))
    x_word = swap(there, (0, 2))
    total, word = local_call(
        square_kernel, "add_square", total, both, z_word, x_word, out_shape=[total_type, word_type]
    )
    word = swap(word, (0, 4), (0, 8))
    stride = 16
    while stride < feat_count:
        total, word = local_call(middle_kernel, "add_encode", total, word, out_shape=[total_type, word_type])
        word = swap(word, (0, stride))
        stride *= 2

    scale = 1.0 / math.sqrt(width * feat_count)
    own, *copies = local_call(
        functools.partial(last_kernel, scale),
        "sketch_rows",
        total,
        word,
        labels.reshape(1, rows),
        out_shape=[row_type] * 5,
    )
    stride = 2
    while stride < tok_count:
        copies = [jnp.concatenate([copies[0], swap(copies[0], (stride, 0))], axis=0)] * 4
        own = copies[0]
        stride *= 2
    far = swap(copies[0], (1, 3))
    second = swap(copies[1], (1, 0), (0, 2))
    third = swap(copies[2], (0, 2), (1, 0))
    crossed = swap(copies[3], (0, 3), (1, 1))
    pieces = [own, far, second, third] + [swap(block, (0, 1)) for block in (own, far, second)] + [crossed]
    concepts = C // tok_count
    gram = gram_blocks(pieces, size, kept, concepts, shard, C / (rows * tok_count))
    return gram.reshape(concepts, shard, kept)


def solution(mesh):
    in_specs = (P("tok", "feat"), P("feat"), P(), P("tok", None))
    out_specs = P("tok", "feat", None)
    return jax.shard_map(body, mesh=mesh, in_specs=in_specs, out_specs=out_specs, check_vma=False)
```
